32 devices in a mesh: rep: 4 (over x, core), shard: 8 (over z, y).
Axes of the slice: x: 2, y: 2, z: 4, core: 2. Of those that a mesh axis runs over, the one named last changes fastest.
Arguments:
- tokens: bfloat16 [256, 128, 768], P(('rep', 'shard')), may hold values from -6 to 6
- word_counts: int32 [256], P(('rep', 'shard')), may hold values from 1 to 28
- region_counts: int32 [256], P(('rep', 'shard')), may hold values from 10 to 100
- qkv_weight: float32 [2304, 768], P('shard'), may hold values from -0.21875 to 0.21875
- qkv_bias: float32 [1536], P('shard'), may hold values from -3 to 3
- out_weight: float32 [768, 768], P('shard'), may hold values from -0.875 to 0.875
- out_bias: float32 [768], P('shard'), may hold values from -3 to 3
- attn_gain: float32 [768], P('shard'), may hold values from 0.5 to 1.5
- attn_shift: float32 [768], P('shard'), may hold values from -2 to 2
- up_weight: float32 [3072, 768], P('shard'), may hold values from -0.21875 to 0.21875
- up_bias: float32 [3072], P('shard'), may hold values from -3 to 3
- down_weight: float32 [768, 3072], P('shard'), may hold values from -0.109375 to 0.109375
- down_bias: float32 [768], P('shard'), may hold values from -2 to 2
- ffn_gain: float32 [768], P('shard'), may hold values from 0.5 to 1.5
- ffn_shift: float32 [768], P('shard'), may hold values from -2 to 2
- cotangent: bfloat16 [256, 128, 768], P(('rep', 'shard')), may hold values from -6 to 6
Outputs:
- layer_out: bfloat16 [256, 128, 768], P(('rep', 'shard'))
- tokens_grad: float32 [256, 128, 768], P(('rep', 'shard'))
- qkv_weight_grad: float32 [2304, 768], P('shard')
- qkv_bias_grad: float32 [1536], P('shard')
- out_weight_grad: float32 [768, 768], P('shard')
- out_bias_grad: float32 [768], P('shard')
- attn_gain_grad: float32 [768], P('shard')
- attn_shift_grad: float32 [768], P('shard')
- up_weight_grad: float32 [3072, 768], P('shard')
- up_bias_grad: float32 [3072], P('shard')
- down_weight_grad: float32 [768, 3072], P('shard')
- down_bias_grad: float32 [768], P('shard')
- ffn_gain_grad: float32 [768], P('shard')
- ffn_shift_grad: float32 [768], P('shard')
The draws below stay inside these ranges and needn't reach their ends.
All inputs are finite; a program needn't handle non-finite values.
Results may differ from the reference program's by a relative error of at most 0.015.
The reference program's roundings to bfloat16 on the way count: a program that leaves them out, or rounds other values in their place, can miss the bound.
Values may be sent and summed in bfloat16 or wider, within the bound.
No kernel may reach another device: no remote copies, remote signals or barrier semaphores. Data moves between devices by JAX's collectives and lax.ppermute only.
A program may use at most 256 MiB of HBM per device.

```python
import math
import jax
import jax.numpy as jnp
from jax import lax

D = 768
FF = 3072
HEADS = 12
HEAD_DIM = 64
WORDS_MAX = 28
REGIONS_MAX = 100
SEQ = 128
PAIRS = 256


def with_ends(drawn, key, smallest, top_value):
    place = [jax.random.randint(jax.random.fold_in(key, axis), (), 0, length) for axis, length in enumerate(drawn.shape)]
    main_axis = drawn.shape.index(max(drawn.shape))
    beside = place[:main_axis] + [(place[main_axis] + 1) % drawn.shape[main_axis]] + place[main_axis + 1:]
    return drawn.at[tuple(place)].set(smallest).at[tuple(beside)].set(top_value)


def with_spikes(drawn, stream_key, source, target, parts, factor):
    def block_of(dim):
        return (jnp.arange(drawn.shape[dim]) // (drawn.shape[dim] // parts)).reshape((-1,) + (1,) * (drawn.ndim - 1 - dim))

    first = jax.random.permutation(stream_key, parts)[block_of(target)]
    other_side = (block_of(target) + parts // 2) % parts
    return jnp.where((block_of(source) == first) | (block_of(source) == other_side), factor * drawn, drawn)


def levels(key, extent, split, smallest, top_value):
    def one(dim, blocks):
        heights = jax.random.uniform(jax.random.fold_in(jax.random.fold_in(key, 6), dim), (blocks,), jnp.float32, smallest / len(split), top_value / len(split))
        return jnp.repeat(jnp.exp(heights), extent[dim] // blocks).reshape((-1,) + (1,) * (len(extent) - dim - 1))

    loudness = one(*split[0])
    for cut in split[1:]:
        loudness = loudness * one(*cut)
    return loudness


def scatter_about(own_key, dims, scale, limit, cuts=(), kind=jnp.bfloat16):
    factor_of = levels(own_key, dims, cuts, -0.22, 0.18) if cuts else 1.0
    array = jax.random.normal(own_key, dims, jnp.float32) * scale * factor_of
    return jnp.minimum(jnp.maximum(array, -limit), limit).astype(kind)


def noise_with(rng, extent, scale, limit, split, heavy, kind=jnp.bfloat16):
    values = scale * jax.random.normal(rng, extent, jnp.float32)
    if split:
        values = values * levels(rng, extent, split, -0.22, 0.18)
    return jnp.clip(with_spikes(values, jax.random.fold_in(rng, 3), *heavy), -limit, limit).astype(kind)


def setup_inputs(seed: int = 0) -> dict:
    seeds = jax.random.split(jax.random.key(seed), 17)
    tokens = scatter_about(seeds[0], (PAIRS, SEQ, D), 1.0, 6.0, ((0, 32),))
    word_counts = with_ends(jax.random.randint(seeds[1], (PAIRS,), 1, WORDS_MAX + 1), jax.random.fold_in(seeds[1], 1), 1, WORDS_MAX).astype(jnp.int32)
    region_counts = with_ends(jax.random.randint(seeds[2], (PAIRS,), min(10, REGIONS_MAX), REGIONS_MAX + 1), jax.random.fold_in(seeds[2], 1), min(10, REGIONS_MAX), REGIONS_MAX).astype(jnp.int32)
    qkv_weight = scatter_about(seeds[3], (3 * D, D), D ** -0.5, 0.21875, ((0, 8),), jnp.float32)
    qkv_bias = scatter_about(seeds[4], (2 * D,), 0.5, 3.0, ((0, 8),), jnp.float32)
    out_weight = scatter_about(seeds[5], (D, D), (D // 16) ** -0.5, 0.875, ((0, 8),), jnp.float32)
    out_bias = scatter_about(seeds[6], (D,), 0.5, 3.0, ((0, 8),), jnp.float32)
    attn_gain = jnp.clip(1.0 + 0.1 * jax.random.normal(seeds[7], (D,), jnp.float32), 0.5, 1.5)
    attn_shift = scatter_about(seeds[8], (D,), 0.3, 2.0, ((0, 8),), jnp.float32)
    up_weight = scatter_about(seeds[9], (FF, D), D ** -0.5, 0.21875, ((0, 8),), jnp.float32)
    up_bias = scatter_about(seeds[10], (FF,), 0.5, 3.0, ((0, 8),), jnp.float32)
    down_weight = scatter_about(seeds[11], (D, FF), FF ** -0.5, 0.109375, ((0, 8),), jnp.float32)
    down_bias = scatter_about(seeds[12], (D,), 0.3, 2.0, ((0, 8),), jnp.float32)
    ffn_gain = jnp.clip(1.0 + 0.1 * jax.random.normal(seeds[13], (D,), jnp.float32), 0.5, 1.5)
    ffn_shift = scatter_about(seeds[14], (D,), 0.3, 2.0, ((0, 8),), jnp.float32)
    cotangent = noise_with(seeds[15], (PAIRS, SEQ, D), 1.0, 6.0, ((0, 32),), (0, 2, 32, 2.75))
    return {"tokens": tokens, "word_counts": word_counts, "region_counts": region_counts, "qkv_weight": qkv_weight, "qkv_bias": qkv_bias, "out_weight": out_weight, "out_bias": out_bias, "attn_gain": attn_gain, "attn_shift": attn_shift, "up_weight": up_weight, "up_bias": up_bias, "down_weight": down_weight, "down_bias": down_bias, "ffn_gain": ffn_gain, "ffn_shift": ffn_shift, "cotangent": cotangent}


PRECISE = lax.Precision.HIGHEST

@jax.custom_vjp
def low(v):
    return lax.optimization_barrier(v.astype(jnp.bfloat16)).astype(jnp.float32)

@jax.custom_vjp
def low_back(v):
    return v

def low_keep(v):
    return (low(v), None)

def low_pass(kept, grad):
    return (grad,)

def back_keep(v):
    return (v, None)

def back_low(kept, grad):
    return (low(grad),)
low.defvjp(low_keep, low_pass)
low_back.defvjp(back_keep, back_low)

def layer_norm(hidden, gain_vec, shift_vec):
    center = hidden - lax.optimization_barrier(jnp.mean(hidden, axis=-1, keepdims=True))
    spread = lax.optimization_barrier(jnp.mean(center * center, axis=-1, keepdims=True))
    return center * lax.rsqrt(spread + 1e-05) * gain_vec + shift_vec

def valid_rows(word_counts, region_counts):
    places = jnp.arange(WORDS_MAX + REGIONS_MAX, dtype=jnp.int32)
    text_rows = places[None, :] < word_counts[:, None]
    image_rows = (places[None, :] >= WORDS_MAX) & (places[None, :] < WORDS_MAX + region_counts[:, None])
    return text_rows | image_rows

def block_forward(inputs, row_mask, params):
    mat_qkv, vec_qv, mat_out, vec_out, gain_attn, shift_attn, mat_up, vec_up, mat_down, vec_down, gain_ffn, shift_ffn = params
    pair_count = inputs.shape[0]
    seq_len = inputs.shape[1]

    def to_heads(tensor):
        return tensor.reshape(pair_count, seq_len, HEADS, HEAD_DIM)
    joined = jnp.einsum('bsd,ed->bse', inputs, mat_qkv, precision=PRECISE)
    queries = low(low_back(joined[..., :D] + vec_qv[:D]))
    key_part = low(low_back(joined[..., D:2 * D]))
    values = low(low_back(joined[..., 2 * D:] + vec_qv[D:]))
    scores = low_back(jnp.einsum('bqhe,bkhe->bhqk', to_heads(queries), to_heads(key_part), precision=PRECISE) * HEAD_DIM ** (-0.5))
    masked = jnp.where(row_mask[:, None, None, :], scores, -1000000000.0)
    highest = lax.optimization_barrier(jnp.max(masked, axis=-1, keepdims=True))
    exponent = jnp.exp(masked - highest)
    soft_probs = exponent / lax.optimization_barrier(jnp.sum(exponent, axis=-1, keepdims=True))
    mixture = jnp.einsum('bhqk,bkhe->bqhe', low(soft_probs), to_heads(values), precision=PRECISE)
    mixture = low(low_back(mixture.reshape(pair_count, seq_len, D)))
    attended = low_back(jnp.einsum('bse,de->bsd', mixture, mat_out, precision=PRECISE) + vec_out)
    first_norm = layer_norm(inputs + attended, gain_attn, shift_attn)
    hidden = low_back(jnp.einsum('bsd,fd->bsf', low(first_norm), mat_up, precision=PRECISE) + vec_up)
    active = low(jax.nn.gelu(hidden, approximate=False))
    feed_out = low_back(jnp.einsum('bsf,df->bsd', active, mat_down, precision=PRECISE) + vec_down)
    second_norm = layer_norm(first_norm + feed_out, gain_ffn, shift_ffn)
    return second_norm * row_mask[:, :, None].astype(jnp.float32)

def reference(tokens, word_counts, region_counts, qkv_weight, qkv_bias, out_weight, out_bias, attn_gain, attn_shift, up_weight, up_bias, down_weight, down_bias, ffn_gain, ffn_shift, cotangent):
    params = tuple((weight.astype(jnp.float32) for weight in (qkv_weight, qkv_bias, out_weight, out_bias, attn_gain, attn_shift, up_weight, up_bias, down_weight, down_bias, ffn_gain, ffn_shift)))
    row_mask = valid_rows(word_counts, region_counts)
    group_size = math.gcd(PAIRS, 32)
    block_count = PAIRS // group_size

    def forward(inputs, weights):
        lowered = tuple((low(weight) for weight in weights))

        def one_block(packed):
            return block_forward(packed[0], packed[1], lowered)
        outputs = lax.map(jax.checkpoint(one_block), (inputs.reshape(block_count, group_size, SEQ, D), row_mask.reshape(block_count, group_size, SEQ)))
        return outputs.reshape(PAIRS, SEQ, D)
    result, pullback = jax.vjp(forward, tokens.astype(jnp.float32), params)
    input_grad, gradients = pullback(cotangent.astype(jnp.float32))
    return (result.astype(jnp.bfloat16), input_grad, gradients[0], gradients[1], gradients[2], gradients[3], gradients[4], gradients[5], gradients[6], gradients[7], gradients[8], gradients[9], gradients[10], gradients[11])
```

```python
import functools

import jax
import jax.numpy as jnp
import numpy as np
from jax import lax
from jax.experimental import pallas as pl
from jax.experimental.pallas import tpu as pltpu
from jax.sharding import PartitionSpec as P

HEADS = 12
WORDS_MAX = 28
EPS = 1e-05
BF = jnp.bfloat16
F32 = jnp.float32
ANY = pl.BlockSpec(memory_space=pl.ANY)
SMEM = pl.BlockSpec(memory_space=pltpu.SMEM)
HBM, VMEM = pltpu.HBM, pltpu.VMEM
TOKEN = jax.ShapeDtypeStruct((8, 128), F32)
WHOLE = pl.BlockSpec(memory_space=pltpu.VMEM)
SQRT_HALF = 0.7071067811865476
INV_SQRT_2PI = 0.3989422804014327


def nt(a, b):
    return lax.dot_general(a, b, (((1,), (1,)), ((), ())), preferred_element_type=F32)


def nn(a, b):
    return jnp.dot(a, b, preferred_element_type=F32)


def tn(a, b):
    return lax.dot_general(a, b, (((0,), (0,)), ((), ())), preferred_element_type=F32)


def fixed(shape):
    return pl.BlockSpec(shape, lambda i: (0,) * len(shape))


def rows(shape):
    return pl.BlockSpec(shape, lambda i: (i,) + (0,) * (len(shape) - 1))


def far(value):
    return pltpu.with_memory_space_constraint(value, HBM)


def near(value):
    return pltpu.with_memory_space_constraint(value, VMEM)


def kernel_call(body, deps, in_specs, args, mebibytes=8, **options):
    count, extra = len(args), len(deps)

    def inner(*refs):
        body(*refs[:count], *refs[count + extra :])

    call = pl.pallas_call(
        inner, in_specs=list(in_specs) + [ANY] * extra, compiler_params=params(mebibytes), **options
    )
    return call(*args, *deps)


def params(mebibytes):
    return pltpu.CompilerParams(vmem_limit_bytes=mebibytes * 1024 * 1024)


def piece_place(meta, cc, a, b, rz, local_rows, start, height, width):
    x0, z0, y0 = meta[0], meta[2], meta[3]
    y_rel = jnp.where(cc == 0, a, b)
    x_rel = jnp.where(cc == 0, b, a)
    shard = (z0 ^ rz) * 2 + (y0 ^ y_rel)
    row = shard * local_rows + cc * height + start
    col = (x0 ^ x_rel) * width
    return pl.multiple_of(row, 16), pl.multiple_of(col, 128)


def piece_copies(meta, pieces, whole, sems, local_rows, first, height, width):
    copies = []
    for number, ref in enumerate(pieces):
        cc = meta[1] if number < 2 else 1 - meta[1]
        a = number % 2
        for b in range(2):
            for rz in range(4):
                row, col = piece_place(meta, cc, a, b, rz, local_rows, 0, height, width)
                copies.append(
                    pltpu.make_async_copy(
                        ref.at[b * 4 + rz, pl.ds(first, height), :],
                        whole.at[pl.ds(row, height), pl.ds(col, width)],
                        sems.at[len(copies)],
                    )
                )
    return copies


def tile_waits(whole, outs, sems, count, first, height, span):
    return [
        pltpu.make_async_copy(
            whole.at[pl.ds(0, height), pl.ds(0, span)],
            ref.at[0, pl.ds(first, height), pl.ds(0, span)],
            sems.at[number * count + i],
        )
        for number, ref in enumerate(outs)
        for i in range(count)
    ]


def load_copies(fast, meta, refs, whole, sems, first):
    if not fast:
        return [pltpu.make_async_copy(refs[0], whole, sems.at[0])]
    local_rows, cols = whole.shape[0] // 8, whole.shape[1]
    if len(refs) == 1:
        height, width = local_rows // 2, cols // 2
        return [
            pltpu.make_async_copy(
                refs[0].at[(x * 2 + c) * 8 + shard],
                whole.at[
                    pl.ds(shard * local_rows + c * height, height), pl.ds(x * width, width)
                ],
                sems.at[(x * 2 + c) * 8 + shard],
            )
            for x in range(2)
            for c in range(2)
            for shard in range(8)
        ]
    return piece_copies(meta, refs, whole, sems, local_rows, first, local_rows // 2, cols // 2)


def go(copies):
    for copy in copies:
        copy.start()


def done(copies):
    for copy in copies:
        copy.wait()


def key_mask(words, regions, shape, axis):
    place = lax.broadcasted_iota(jnp.int32, shape, axis)
    return (place < words) | ((place >= WORDS_MAX) & (place < WORDS_MAX + regions))


def split_heads(block):
    low = lax.broadcasted_iota(jnp.int32, block.shape, 1) < 64
    zero = jnp.zeros_like(block)
    return jnp.concatenate([jnp.where(low, block, zero), jnp.where(low, zero, block)], axis=0)


def turn_heads(block):
    n = block.shape[0]
    return jnp.concatenate([block[:, :n].T, block[:, n:].T], axis=1)


def norm_parts(value):
    center = value - jnp.mean(value, axis=-1, keepdims=True)
    rstd = lax.rsqrt(jnp.mean(center * center, axis=-1, keepdims=True) + EPS)
    return center * rstd, rstd


def norm_back(grad, xhat, rstd, gain):
    scaled = grad * gain
    mean_one = jnp.mean(scaled, axis=-1, keepdims=True)
    mean_two = jnp.mean(scaled * xhat, axis=-1, keepdims=True)
    return rstd * (scaled - mean_one - xhat * mean_two)


def attention_kernel(fast, n_in, *refs):
    meta, words, regions = refs[:3]
    x_ref, vec_ref = refs[3:5]
    pieces = refs[5 : 5 + n_in]
    (joined_ref, probs_ref, mix_ref, low_ref, xhat_ref, rstd_ref, wqkv_out, wo_out) = refs[
        5 + n_in : 13 + n_in
    ]
    wqkv, wo, sem_a, sem_b, sem_c = refs[13 + n_in :]
    step = pl.program_id(0)
    d = x_ref.shape[1]
    seq = probs_ref.shape[2]

    @pl.when(step == 0)
    def _():
        if fast:
            first = load_copies(fast, meta, pieces, wqkv, sem_a, 0)
            second = load_copies(fast, meta, pieces, wo, sem_b, wqkv.shape[0] // 16)
        else:
            first = load_copies(fast, meta, pieces[:1], wqkv, sem_a, 0)
            second = load_copies(fast, meta, pieces[1:], wo, sem_b, 0)
        go(first)
        go(second)
        done(first)
        done(second)

    saves = [
        pltpu.make_async_copy(wqkv, wqkv_out, sem_c.at[0]),
        pltpu.make_async_copy(wo, wo_out, sem_c.at[1]),
    ]

    @pl.when(step == 0)
    def _():
        go(saves)

    x = x_ref[...]
    bq = vec_ref[:, :d]
    bv = vec_ref[:, d : 2 * d]
    joined_ref[:, :d] = (nt(x, wqkv[:d, :]) + bq).astype(BF) * BF(0.125)
    joined_ref[:, d : 2 * d] = nt(x, wqkv[d : 2 * d, :]).astype(BF)
    joined_ref[:, 2 * d :] = (nt(x, wqkv[2 * d :, :]) + bv).astype(BF)
    per_step = x_ref.shape[0] // seq
    for p in range(per_step):
        pair = step * per_step + p
        valid = key_mask(words[pair], regions[pair], (seq, 2 * seq), 0)
        here = pl.ds(p * seq, seq)
        for h in range(d // 128):
            cols = pl.ds(h * 128, 128)
            queries = split_heads(joined_ref[here, pl.ds(h * 128, 128)])
            keys = joined_ref[here, pl.ds(d + h * 128, 128)]
            values = split_heads(joined_ref[here, pl.ds(2 * d + h * 128, 128)])
            scores = jnp.where(valid, nt(keys, queries), -1000000000.0)
            exponent = jnp.exp(scores - jnp.max(scores, axis=0, keepdims=True))
            probs = exponent * (1.0 / jnp.sum(exponent, axis=0, keepdims=True))
            probs = probs.astype(BF)
            probs_ref[p, h] = probs
            mix_ref[here, cols] = nn(turn_heads(probs), values).astype(BF)
    first_sum = x.astype(F32) + nt(mix_ref[...], wo[...]) + vec_ref[:, 2 * d : 3 * d]
    xhat, rstd = norm_parts(first_sum)
    xhat_ref[...] = xhat
    rstd_ref[...] = jnp.broadcast_to(rstd, rstd_ref.shape)
    low_ref[...] = (xhat * vec_ref[:, 3 * d : 4 * d] + vec_ref[:, 4 * d : 5 * d]).astype(BF)

    @pl.when(step == pl.num_programs(0) - 1)
    def _():
        done(saves)


def attention_forward(fast, meta, words, regions, x, vec, pieces, seq, deps=()):
    n, d = x.shape
    tile = 2 * seq
    shapes = [
        HBM((n, 3 * d), BF),
        HBM((n // seq, d // 128, seq, 2 * seq), BF),
        HBM((n, d), BF),
        HBM((n, d), BF),
        HBM((n, d), F32),
        HBM((n, 128), F32),
        HBM((3 * d, d), BF),
        HBM((d, d), BF),
    ]
    return kernel_call(
        functools.partial(attention_kernel, fast, len(pieces)),
        deps,
        [SMEM] * 3 + [rows((tile, d)), fixed(vec.shape)] + [ANY] * len(pieces),
        [meta, words, regions, far(x), vec, *pieces],
        grid=(n // tile,),
        out_specs=[
            rows((tile, 3 * d)),
            rows((2, d // 128, seq, 2 * seq)),
            rows((tile, d)),
            rows((tile, d)),
            rows((tile, d)),
            rows((tile, 128)),
            ANY,
            ANY,
        ],
        out_shape=shapes,
        scratch_shapes=[
            pltpu.VMEM((3 * d, d), BF),
            pltpu.VMEM((d, d), BF),
            pltpu.SemaphoreType.DMA((32,)),
            pltpu.SemaphoreType.DMA((32,)),
            pltpu.SemaphoreType.DMA((2,)),
        ],
        cost_estimate=pl.CostEstimate(
            flops=2 * n * d * 4 * d, bytes_accessed=16 * n * d, transcendentals=0
        ),
        mebibytes=17,
        name="attention_forward",
    )


def up_kernel(fast, n_in, *refs):
    meta, low_ref, bias_ref = refs[:3]
    pieces = refs[3 : 3 + n_in]
    act_ref, slope_ref, token_ref, w, sem_a = refs[3 + n_in :]
    token_ref[...] = jnp.zeros_like(token_ref)
    step = pl.program_id(0)

    @pl.when(step == 0)
    def _():
        loads = load_copies(fast, meta, pieces, w, sem_a, 0)
        go(loads)
        done(loads)

    x = low_ref[...]
    chunk = 512
    for f in range(w.shape[0] // chunk):
        part = pl.ds(f * chunk, chunk)
        hidden = nt(x, w[f * chunk : (f + 1) * chunk, :]) + bias_ref[:, part]
        phi = 0.5 + 0.5 * lax.erf(hidden * SQRT_HALF)
        act_ref[:, part] = (hidden * phi).astype(BF)
        bell = jnp.exp(hidden * hidden * -0.5) * INV_SQRT_2PI
        slope_ref[:, part] = (phi + hidden * bell).astype(BF)


def up_forward(fast, meta, low, bias, pieces, deps=()):
    n, d = low.shape
    ff = bias.shape[1]
    tile = 256
    return kernel_call(
        functools.partial(up_kernel, fast, len(pieces)),
        deps,
        [SMEM, rows((tile, d)), fixed(bias.shape)] + [ANY] * len(pieces),
        [meta, far(low), bias, *pieces],
        grid=(n // tile,),
        out_specs=[rows((tile, ff)), rows((tile, ff)), fixed((8, 128))],
        out_shape=[VMEM((n, ff), BF), VMEM((n, ff), BF), TOKEN],
        scratch_shapes=[pltpu.VMEM((ff, d), BF), pltpu.SemaphoreType.DMA((32,))],
        cost_estimate=pl.CostEstimate(
            flops=4 * n * d * ff, bytes_accessed=4 * n * ff, transcendentals=0
        ),
        mebibytes=14,
        name="up_forward",
    )


def down_kernel(fast, n_in, seq, *refs):
    meta, words, regions = refs[:3]
    act_ref, slope_ref, xhat_far, vec_ref, cot_far = refs[3:8]
    pieces = refs[8 : 8 + n_in]
    outs_end = 13 + n_in + (2 if fast else 1)
    out_far, second_ref, hidden_ref, sums_ref, bias_ref = refs[8 + n_in : 13 + n_in]
    grads = refs[13 + n_in : outs_end]
    xhat_ref, cot_ref, out_ref, feed_ref, w, whole, sem_a, sem_b, sem_c = refs[outs_end:]
    n, d = second_ref.shape
    ff = act_ref.shape[1]
    tile = 256
    loads = load_copies(fast, meta, pieces, w, sem_a, 0)
    go(loads)
    reads, writes = [], []
    for i in range(n // tile):
        part = pl.ds(i * tile, tile)
        reads.append(
            [
                pltpu.make_async_copy(xhat_far.at[part], xhat_ref.at[part], sem_b.at[0, i]),
                pltpu.make_async_copy(cot_far.at[part], cot_ref.at[part], sem_b.at[1, i]),
            ]
        )
        writes.append(pltpu.make_async_copy(out_ref.at[part], out_far.at[part], sem_b.at[2, i]))
        go(reads[i])
    gain_one, shift_one = vec_ref[:, :d], vec_ref[:, d : 2 * d]
    bias, gain, shift = vec_ref[:, 2 * d : 3 * d], vec_ref[:, 3 * d : 4 * d], vec_ref[:, 4 * d :]
    done(loads)
    sums = [jnp.zeros((1, d), F32)] * 3
    for i in range(n // tile):
        part = slice(i * tile, (i + 1) * tile)
        product = nt(act_ref[part, :], w[...])
        done(reads[i])
        second_sum = xhat_ref[part, :] * gain_one + shift_one + product + bias
        xhat, rstd = norm_parts(second_sum)
        first = i * (tile // seq)
        keep = jnp.concatenate(
            [
                key_mask(words[first + p], regions[first + p], (seq, 128), 0)
                for p in range(tile // seq)
            ],
            axis=0,
        )[:, :1]
        out_ref[part, :] = jnp.where(keep, xhat * gain + shift, 0.0).astype(BF)
        go([writes[i]])
        grad = jnp.where(keep, cot_ref[part, :].astype(F32), 0.0)
        second = norm_back(grad, xhat, rstd, gain)
        second_ref[part, :] = second
        feed = second.astype(BF)
        feed_ref[part, :] = feed
        for k, value in enumerate((grad * xhat, grad, feed.astype(F32))):
            sums[k] = sums[k] + jnp.sum(value, axis=0, keepdims=True)
    for k in range(3):
        sums_ref[k : k + 1, :] = sums[k]
    width = 512
    for i in range(ff // width):
        here = slice(i * width, (i + 1) * width)
        hidden = nn(feed_ref[...], w[:, here]) * slope_ref[:, here].astype(F32)
        hidden = hidden.astype(BF)
        hidden_ref[:, here] = hidden
        bias_ref[:, here] = jnp.sum(hidden.astype(F32), axis=0, keepdims=True)
    waits = []
    width, span = ff // 4, ff // 8
    for i in range(4):
        here = slice(i * width, (i + 1) * width)
        whole[:, here] = tn(feed_ref[...], act_ref[:, here]).astype(BF)
        if fast:
            for k in range(2):
                chunk = (i % 2) * 2 + k
                copies = tile_copies(
                    meta, whole, grads, sem_c.at[2 * i + k], range(8), [i // 2], d // 8,
                    chunk * (d // 16), d // 16, ff // 2, (chunk * span, span),
                )
                go(copies)
                waits += tile_waits(
                    whole, grads, sem_c.at[2 * i + k], 8, chunk * (d // 16), d // 16, span
                )
    if not fast:
        waits = [pltpu.make_async_copy(whole, grads[0], sem_c.at[0, 0])]
        go(waits)
    done(waits)
    done(writes)


def down_forward(
    fast, meta, words, regions, act, slope, xhat, vec, cot, pieces, seq, deps=()
):
    n, ff = act.shape
    d = xhat.shape[1]
    shapes = grad_shapes(fast, d, ff)
    return kernel_call(
        functools.partial(down_kernel, fast, len(pieces), seq),
        deps,
        [SMEM] * 3 + [WHOLE, WHOLE, ANY, WHOLE, ANY] + [ANY] * len(pieces),
        [meta, words, regions, near(act), near(slope), far(xhat), vec, far(cot), *pieces],
        out_specs=[ANY, WHOLE, WHOLE, WHOLE, WHOLE] + [ANY] * len(shapes),
        out_shape=[
            HBM((n, d), BF),
            VMEM((n, d), F32),
            VMEM((n, ff), BF),
            jax.ShapeDtypeStruct((8, d), F32),
            jax.ShapeDtypeStruct((1, ff), F32),
        ]
        + shapes,
        scratch_shapes=[
            pltpu.VMEM((n, d), F32),
            pltpu.VMEM((n, d), BF),
            pltpu.VMEM((n, d), BF),
            pltpu.VMEM((n, d), BF),
            pltpu.VMEM((d, ff), BF),
            pltpu.VMEM((d, ff), BF),
            pltpu.SemaphoreType.DMA((32,)),
            pltpu.SemaphoreType.DMA((3, n // 256)),
            pltpu.SemaphoreType.DMA((8, 16)),
        ],
        cost_estimate=pl.CostEstimate(
            flops=12 * n * d * ff, bytes_accessed=2 * n * ff, transcendentals=0
        ),
        mebibytes=25,
        name="down_forward",
    )


def grad_shapes(fast, total_rows, cols):
    if fast:
        width = min(total_rows, cols) // 2
        return [HBM((16, total_rows * cols // (32 * width), width), BF)] * 2
    return [HBM((total_rows, cols), BF)]


def tile_copies(meta, whole, outs, sems, shards, sides, local_rows, first, height, width, cols=None):
    x0, c0, z0, y0 = meta[0], meta[1], meta[2], meta[3]
    offset, span = (0, width) if cols is None else cols
    there = pl.ds(0, span)
    copies = []
    for number, ref in enumerate(outs):
        cc = c0 ^ number
        for shard in shards:
            for side in sides:
                y_rel, x_rel = y0 ^ (shard % 2), x0 ^ side
                a = jnp.where(cc == 0, y_rel, x_rel)
                b = jnp.where(cc == 0, x_rel, y_rel)
                row = pl.multiple_of(shard * local_rows + cc * height, 16)
                col = pl.multiple_of(side * width + offset, 128)
                copies.append(
                    pltpu.make_async_copy(
                        whole.at[pl.ds(row, height), pl.ds(col, span)],
                        ref.at[a * 8 + b * 4 + (z0 ^ (shard // 2)), pl.ds(first, height), there],
                        sems.at[len(copies)],
                    )
                )
    return copies


def up_grad_kernel(fast, *refs):
    meta, hidden_ref, low_far = refs[:3]
    outs = refs[3 : (5 if fast else 4)]
    token_ref, _, low_ref, whole, sems, sem_b = refs[5 if fast else 4 :]
    reads = [pltpu.make_async_copy(low_far, low_ref, sem_b.at[0])]
    go(reads)
    token_ref[...] = jnp.zeros_like(token_ref)
    done(reads)
    ff, d = whole.shape
    height = ff // 4
    waits = []
    for i in range(4):
        here = slice(i * height, (i + 1) * height)
        whole[here, :] = tn(hidden_ref[:, here], low_ref[...]).astype(BF)
        if fast:
            copies = tile_copies(
                meta, whole, outs, sems.at[i], [2 * i, 2 * i + 1], [0, 1], ff // 8, 0, ff // 16,
                d // 2,
            )
            go(copies)
            waits += tile_waits(whole, outs, sems.at[i], 4, 0, ff // 16, d // 2)
    if not fast:
        waits = [pltpu.make_async_copy(whole, outs[0], sems.at[0, 0])]
        go(waits)
    done(waits)


def up_grad(fast, meta, hidden, low, deps=()):
    n, d = low.shape
    ff = hidden.shape[1]
    shapes = grad_shapes(fast, ff, d)
    return kernel_call(
        functools.partial(up_grad_kernel, fast),
        deps,
        [SMEM, WHOLE, ANY],
        [meta, near(hidden), far(low)],
        out_specs=[ANY] * len(shapes) + [WHOLE, WHOLE],
        out_shape=shapes + [TOKEN, VMEM((n, ff), BF)],
        scratch_shapes=[
            pltpu.VMEM((n, d), BF),
            pltpu.VMEM((ff, d), BF),
            pltpu.SemaphoreType.DMA((4, 8)),
            pltpu.SemaphoreType.DMA((1,)),
        ],
        input_output_aliases={1: len(shapes) + 1},
        cost_estimate=pl.CostEstimate(
            flops=4 * n * d * ff, bytes_accessed=2 * n * ff, transcendentals=0
        ),
        mebibytes=12,
        name="up_grad",
    )


def first_back_kernel(fast, *refs):
    meta, second_ref, hidden_ref, wu_far, xhat_far, rstd_far, gain_ref, wo_far = refs[:8]
    sum_far, low_far, mix_ref, sums_ref = refs[8:12]
    wu_ref, xhat_ref, rstd_ref, wo_ref, sum_ref, low_ref, sem, sem_b = refs[12:]
    weights = load_copies(fast, meta, [wu_far], wu_ref, sem_b, 0)
    go(weights)
    n, d = low_ref.shape
    tile = 256
    count = n // tile
    reads = [
        pltpu.make_async_copy(rstd_far, rstd_ref, sem.at[0]),
        pltpu.make_async_copy(wo_far, wo_ref, sem.at[1]),
    ]
    lines, writes = [], []
    for i in range(count):
        part = pl.ds(i * tile, tile)
        lines.append(pltpu.make_async_copy(xhat_far.at[part], xhat_ref.at[part], sem.at[2 + i]))
        writes.append(
            [
                pltpu.make_async_copy(sum_ref.at[part], sum_far.at[part], sem.at[2 + count + i]),
                pltpu.make_async_copy(
                    low_ref.at[part], low_far.at[part], sem.at[2 + 2 * count + i]
                ),
            ]
        )
    go(lines[:1] + reads + lines[1:])
    done(weights)
    product = nn(hidden_ref[:tile, :], wu_ref[...])
    done(reads)
    sums = [jnp.zeros((1, d), F32)] * 3
    for i in range(count):
        part = slice(i * tile, (i + 1) * tile)
        grad = second_ref[part, :] + product
        if i + 1 < count:
            product = nn(hidden_ref[(i + 1) * tile : (i + 2) * tile, :], wu_ref[...])
        done([lines[i]])
        xhat = xhat_ref[part, :]
        attn_sum = norm_back(grad, xhat, rstd_ref[part, :1], gain_ref[...])
        sum_ref[part, :] = attn_sum
        low = attn_sum.astype(BF)
        low_ref[part, :] = low
        go(writes[i])
        mix_ref[part, :] = nn(low, wo_ref[...]).astype(BF)
        for k, value in enumerate((grad * xhat, grad, low.astype(F32))):
            sums[k] = sums[k] + jnp.sum(value, axis=0, keepdims=True)
    for k in range(3):
        sums_ref[k : k + 1, :] = sums[k]
    for pair in writes:
        done(pair)


def first_back(fast, meta, second, hidden, wu, xhat, rstd, gain, wo, deps=()):
    n, d = xhat.shape
    ff = hidden.shape[1]
    return kernel_call(
        functools.partial(first_back_kernel, fast),
        deps,
        [SMEM, WHOLE, WHOLE, ANY, ANY, ANY, WHOLE, ANY],
        [meta, near(second), near(hidden), far(wu), far(xhat), far(rstd), gain, far(wo)],
        out_specs=[ANY, ANY, WHOLE, WHOLE],
        out_shape=[
            HBM((n, d), F32),
            HBM((n, d), BF),
            VMEM((n, d), BF),
            jax.ShapeDtypeStruct((8, d), F32),
        ],
        scratch_shapes=[
            pltpu.VMEM((ff, d), BF),
            pltpu.VMEM((n, d), F32),
            pltpu.VMEM((n, 128), F32),
            pltpu.VMEM((d, d), BF),
            pltpu.VMEM((n, d), F32),
            pltpu.VMEM((n, d), BF),
            pltpu.SemaphoreType.DMA((2 + 3 * (n // 256),)),
            pltpu.SemaphoreType.DMA((32,)),
        ],
        cost_estimate=pl.CostEstimate(
            flops=4 * n * d * ff, bytes_accessed=2 * n * ff, transcendentals=0
        ),
        mebibytes=18,
        name="first_back",
    )


def attention_back_kernel(seq, *refs):
    mix_ref, joined_ref, probs_ref, grad_ref, copy_ref, sums_ref = refs
    d = mix_ref.shape[1]

    @pl.when(pl.program_id(0) == 0)
    def _():
        sums_ref[...] = jnp.zeros_like(sums_ref)

    for p in range(mix_ref.shape[0] // seq):
        here = pl.ds(p * seq, seq)
        for h in range(d // 128):
            one = pl.ds(h * 128, 128)
            two = pl.ds(d + h * 128, 128)
            three = pl.ds(2 * d + h * 128, 128)
            outer = split_heads(mix_ref[here, one])
            probs = probs_ref[p, h]
            grad_probs = nt(joined_ref[here, three], outer)
            wide = probs.astype(F32)
            product = wide * grad_probs
            scores = product - wide * jnp.sum(product, axis=0, keepdims=True)
            scores = scores.astype(BF)
            grad_ref[here, three] = nn(probs, outer).astype(BF)
            grad_ref[here, two] = nn(scores, split_heads(joined_ref[here, one])).astype(BF)
            keys = split_heads(joined_ref[here, two])
            grad_ref[here, one] = (nn(turn_heads(scores), keys) * 0.125).astype(BF)
    copy_ref[...] = grad_ref[...]
    sums_ref[0:1, :] += jnp.sum(grad_ref[:, :d].astype(F32), axis=0, keepdims=True)
    sums_ref[1:2, :] += jnp.sum(grad_ref[:, 2 * d :].astype(F32), axis=0, keepdims=True)


def attention_back(mix, joined, probs, seq, deps=()):
    n, d = mix.shape
    tile = 2 * seq
    return kernel_call(
        functools.partial(attention_back_kernel, seq),
        deps,
        [
            rows((tile, d)),
            rows((tile, 3 * d)),
            rows((2, d // 128, seq, 2 * seq)),
        ],
        [near(mix), far(joined), far(probs)],
        grid=(n // tile,),
        out_specs=[rows((tile, 3 * d))] * 2 + [fixed((8, d))],
        out_shape=[
            VMEM((n, 3 * d), BF),
            HBM((n, 3 * d), BF),
            jax.ShapeDtypeStruct((8, d), F32),
        ],
        cost_estimate=pl.CostEstimate(
            flops=16 * n * d * d, bytes_accessed=30 * n * d, transcendentals=0
        ),
        mebibytes=14,
        name="attention_back",
    )


def qkv_grad_kernel(fast, *refs):
    meta, grad_ref, x_far, low_far, mix_far = refs[:5]
    outs = refs[5:7]
    token_ref, whole, whole_out, x_ref, low_ref, mix_ref, sem_a, sem_b, sem_c = refs[7:]
    reads = [
        pltpu.make_async_copy(x_far, x_ref, sem_c.at[0]),
        pltpu.make_async_copy(low_far, low_ref, sem_c.at[1]),
        pltpu.make_async_copy(mix_far, mix_ref, sem_c.at[2]),
    ]
    go(reads)
    token_ref[...] = jnp.zeros_like(token_ref)
    total, d = whole.shape
    waits = []
    done(reads[:1])
    for i in range(2):
        here = slice(i * total // 2, (i + 1) * total // 2)
        whole[here, :] = tn(grad_ref[:, here], x_ref[...]).astype(BF)
        if fast:
            go(
                tile_copies(
                    meta, whole, outs, sem_a.at[i], range(4 * i, 4 * i + 4), [0, 1], total // 8,
                    0, total // 16, d // 2,
                )
            )
            waits += tile_waits(whole, outs, sem_a.at[i], 8, 0, total // 16, d // 2)
    done(reads[1:])
    whole_out[...] = tn(low_ref[...], mix_ref[...]).astype(BF)
    if fast:
        go(
            tile_copies(
                meta, whole_out, outs, sem_b, range(8), [0, 1], d // 8, total // 16, d // 16,
                d // 2,
            )
        )
        waits += tile_waits(whole_out, outs, sem_b, 16, total // 16, d // 16, d // 2)
    else:
        waits = [
            pltpu.make_async_copy(whole, outs[0], sem_b.at[0]),
            pltpu.make_async_copy(whole_out, outs[1], sem_b.at[1]),
        ]
        go(waits)
    done(waits)


def qkv_grad(fast, meta, grad, x, low, mix, deps=()):
    n, d = x.shape
    if fast:
        shapes = [HBM((16, 4 * d // 16, d // 2), BF)] * 2
    else:
        shapes = [jax.ShapeDtypeStruct((3 * d, d), BF), jax.ShapeDtypeStruct((d, d), BF)]
    return kernel_call(
        functools.partial(qkv_grad_kernel, fast),
        deps,
        [SMEM, WHOLE, ANY, ANY, ANY],
        [meta, near(grad), far(x), far(low), far(mix)],
        out_specs=[ANY] * 2 + [WHOLE],
        out_shape=shapes + [TOKEN],
        scratch_shapes=[
            pltpu.VMEM((3 * d, d), BF),
            pltpu.VMEM((d, d), BF),
            pltpu.VMEM((n, d), BF),
            pltpu.VMEM((n, d), BF),
            pltpu.VMEM((n, d), BF),
            pltpu.SemaphoreType.DMA((2, 16)),
            pltpu.SemaphoreType.DMA((32,)),
            pltpu.SemaphoreType.DMA((3,)),
        ],
        cost_estimate=pl.CostEstimate(
            flops=16 * n * d * d, bytes_accessed=16 * n * d, transcendentals=0
        ),
        mebibytes=14,
        name="qkv_grad",
    )


def tokens_grad_kernel(sum_ref, grad_ref, w_ref, out_ref):
    out_ref[...] = sum_ref[...] + nn(grad_ref[...], w_ref[...])


def tokens_back(attn_sum, grad, w, deps=()):
    n, d = attn_sum.shape
    tile = 256
    return kernel_call(
        tokens_grad_kernel,
        deps,
        [rows((tile, d)), rows((tile, 3 * d)), fixed((3 * d, d))],
        [far(attn_sum), far(grad), far(w)],
        grid=(n // tile,),
        out_specs=rows((tile, d)),
        out_shape=HBM((n, d), F32),
        cost_estimate=pl.CostEstimate(
            flops=12 * n * d * d, bytes_accessed=14 * n * d, transcendentals=0
        ),
        mebibytes=14,
        name="tokens_back",
    )


AXES = ("rep", "shard")


def route(fn):
    pairs = []
    for x in range(2):
        for c in range(2):
            for z in range(4):
                for y in range(2):
                    to = fn(x, c, z, y)
                    pairs.append(
                        ((x * 2 + c) * 8 + z * 2 + y, (to[0] * 2 + to[1]) * 8 + to[2] * 2 + to[3])
                    )
    return pairs


def to_core(v):
    return lax.ppermute(v, AXES, route(lambda x, c, z, y: (x, 1 - c, z, y)))


def to_x(v):
    return lax.ppermute(v, AXES, route(lambda x, c, z, y: (1 - x, c, z, y)))


def to_z(v, k):
    return lax.ppermute(v, AXES, route(lambda x, c, z, y: (x, c, z ^ k, y)))


def to_cross(v, first_core):
    return lax.ppermute(
        v,
        AXES,
        route(lambda x, c, z, y: (1 - x, c, z, y) if c == first_core else (x, c, z, 1 - y)),
    )


def after(value, *others):
    return lax.optimization_barrier((value, others))[0]


def start_gather(own):
    return jnp.stack([own] + [to_z(own, k) for k in (1, 2, 3)])


def first_cross(along):
    return jnp.concatenate([along, to_cross(along, 0)])


def add_core_kernel(kept_ref, got_ref, *refs):
    keep_ref, send_ref = refs[-2:]
    count, height, width = keep_ref.shape
    for k in range(count):
        here = slice(k * height, (k + 1) * height)
        keep_ref[k] = (kept_ref[k].astype(F32) + got_ref[k].astype(F32)).astype(BF)
        other = kept_ref[count + k].astype(F32) + got_ref[count + k].astype(F32)
        send_ref[here, :] = other.astype(BF)
    if len(refs) == 3:
        send_ref[count * height :, :] = refs[0][...].astype(BF)


def add_cross_kernel(keep_ref, got_ref, *refs):
    small = len(refs) == 4
    new_ref, send_ref = refs[1:3] if small else refs
    count, height, width = new_ref.shape
    for k in range(2 * count):
        here = slice(k * height, (k + 1) * height)
        total = (keep_ref[k].astype(F32) + got_ref[here, :].astype(F32)).astype(BF)
        if k < count:
            new_ref[k] = total
        else:
            send_ref[(k - count) * height : (k - count + 1) * height, :] = total
    if small:
        rows_in = refs[0][...] + got_ref[2 * count * height :, :].astype(F32)
        refs[3][...] = rows_in
        tail = jnp.concatenate([rows_in[count : 2 * count], rows_in[2 * count :]], axis=0)
        tail = jnp.concatenate([tail, jnp.zeros((count, width), F32)], axis=0)
        send_ref[count * height :, :] = tail.astype(BF)


def add_last_kernel(keep_ref, got_ref, *refs):
    small = len(refs) == 5
    outs = refs[1:] if small else refs
    count, height, width = keep_ref.shape
    if small:
        rows_in = refs[0][...] + got_ref[count * height :, :].astype(F32)
        place = lax.broadcasted_iota(jnp.int32, rows_in.shape, 0)
    for k in range(count):
        here = slice(k * height, (k + 1) * height)
        total = keep_ref[k].astype(F32) + got_ref[here, :].astype(F32)
        outs[k][:height, :] = total.astype(outs[k].dtype)
        if small:
            row = jnp.sum(jnp.where(place == k, rows_in, 0.0), axis=0, keepdims=True)
            outs[k][height:, :] = jnp.broadcast_to(row, (16, width)).astype(outs[k].dtype)


def add_cross_pair_kernel(*refs):
    new_ref, send_ref, token_ref = refs[4:]
    token_ref[...] = jnp.zeros_like(token_ref)
    count, height, _ = new_ref.shape
    half = count // 2
    for group in range(2):
        keep_ref, got_ref = refs[2 * group : 2 * group + 2]
        for k in range(count):
            got = got_ref[k * height : (k + 1) * height, :]
            total = (keep_ref[k].astype(F32) + got.astype(F32)).astype(BF)
            place = group * half + k % half
            if k < half:
                new_ref[place] = total
            else:
                send_ref[place * height : (place + 1) * height, :] = total


def add_last_pair_kernel(keep_ref, got_ref, *refs):
    refs[4][...] = jnp.zeros_like(refs[4])
    count, height, _ = keep_ref.shape
    for k in range(count):
        group, along = divmod(k, count // 2)
        got = got_ref[k * height : (k + 1) * height, :]
        total = keep_ref[k].astype(F32) + got.astype(F32)
        refs[along][group * height : (group + 1) * height, :] = total.astype(refs[along].dtype)


def total_kernel(own_ref, one_ref, two_ref, three_ref, out_ref):
    total = own_ref[...] + one_ref[...].astype(F32)
    total = total + two_ref[...].astype(F32) + three_ref[...].astype(F32)
    out_ref[...] = total.astype(BF)


class Scatter:
    def __init__(self, kept, sent):
        self.kept, self.small = kept, None
        self.got = to_core(sent)

    def call(self, body, out_shape, extra, deps, name):
        args = [near(self.keep), near(self.got)] + list(extra)

        def marked(*refs):
            refs[-1][...] = jnp.zeros_like(refs[-1])
            body(*refs[:-1])

        *out, self.token = kernel_call(
            marked,
            deps,
            [WHOLE] * len(args),
            args,
            out_specs=[WHOLE] * (len(out_shape) + 1),
            out_shape=out_shape + [TOKEN],
            name=name,
        )
        return out

    def add_core(self, deps=(), small=None):
        self.keep = self.kept
        count, height, width = self.kept.shape[0] // 2, *self.kept.shape[1:]
        tail, extra = 0, []
        if small is not None:
            tail, extra = 16, [jnp.concatenate([small[8:], jnp.zeros_like(small[8:])])]
            self.small = jnp.concatenate([small[:8], jnp.zeros_like(small[8:])])
        self.keep, self.send = self.call(
            add_core_kernel,
            [VMEM((count, height, width), BF), VMEM((count * height + tail, width), BF)],
            extra,
            deps,
            "add_core",
        )
        return self.token

    def cross(self, core):
        self.got = to_cross(self.send, core)

    def add_cross(self, deps=()):
        count, height, width = self.keep.shape[0] // 2, *self.keep.shape[1:]
        small = self.small is not None
        outs = [
            VMEM((count, height, width), BF),
            VMEM((count * height + 16 * small, width), BF),
        ]
        if small:
            outs.append(VMEM((16, width), F32))
        out = self.call(
            add_cross_kernel, outs, [self.small] if small else [], deps, "add_cross"
        )
        self.keep, self.send = out[:2]
        if small:
            self.small = out[2]
        return self.token

    def add_last(self, deps=()):
        height, width = self.keep.shape[1:]
        small = self.small is not None
        shape = (height + 16 * small, width)
        self.parts = self.call(
            add_last_kernel,
            [VMEM(shape, F32)] + [VMEM(shape, BF)] * 3,
            [self.small] if small else [],
            deps,
            "add_last",
        )
        return self.token

    def along(self):
        self.got = [to_z(self.parts[k], k) for k in (1, 2, 3)]

    def total(self, deps=()):
        args = [near(v) for v in [self.parts[0]] + self.got]
        return kernel_call(
            total_kernel,
            deps,
            [WHOLE] * 4,
            args,
            out_specs=WHOLE,
            out_shape=jax.ShapeDtypeStruct(self.parts[0].shape, BF),
            name="total",
        )


class Pair:
    def __init__(self, one, two, deps):
        _, height, width = one.keep.shape
        args = [near(v) for v in (one.keep, one.got, two.keep, two.got)]
        self.keep, self.send, self.token = kernel_call(
            add_cross_pair_kernel,
            deps,
            [WHOLE] * 4,
            args,
            out_specs=[WHOLE] * 3,
            out_shape=[VMEM((8, height, width), BF), VMEM((8 * height, width), BF), TOKEN],
            mebibytes=10,
            name="add_cross_pair",
        )
        self.got = to_cross(self.send, 0)

    def along(self, deps=()):
        _, height, width = self.keep.shape
        shape = (2 * height, width)
        *self.parts, self.token = kernel_call(
            add_last_pair_kernel,
            deps,
            [WHOLE] * 2,
            [near(self.keep), near(self.got)],
            out_specs=[WHOLE] * 5,
            out_shape=[VMEM(shape, F32)] + [VMEM(shape, BF)] * 3 + [TOKEN],
            name="add_last_pair",
        )
        self.got = [to_z(self.parts[k], k) for k in (1, 2, 3)]

    total = Scatter.total


def in_columns(piece):
    return jnp.concatenate(jnp.split(piece, 4, axis=0), axis=1)


def side_by_side(low, across, x):
    return jnp.concatenate(
        [jnp.where(x == 0, low, across), jnp.where(x == 0, across, low)], axis=1
    )


def owner_block(mine, other, c, first, height):
    mine, other = mine[first : first + height], other[first : first + height]
    return jnp.concatenate(
        [jnp.where(c == 0, mine, other), jnp.where(c == 0, other, mine)], axis=0
    ).astype(F32)


def quarter_of(w, x, c):
    half_rows, half_cols = w.shape[0] // 2, w.shape[1] // 2
    side = jnp.where(x == 0, w[:, :half_cols], w[:, half_cols:])
    return jnp.where(c == 0, side[:half_rows], side[half_rows:]).astype(BF)


def order_matrix(x, c, z, y):
    rel = jnp.arange(32, dtype=jnp.int32)
    other, a, b, rz = rel // 16, rel // 8 % 2, rel // 4 % 2, rel % 4
    cc = c ^ other
    y_rel = jnp.where(cc == 0, a, b)
    x_rel = jnp.where(cc == 0, b, a)
    place = (((z ^ rz) * 2 + (y ^ y_rel)) * 2 + cc) * 2 + (x ^ x_rel)
    return (place[:, None] == rel[None, :]).astype(F32)


def line_matrices(order, heights):
    place = []
    for shard in range(8):
        at = 0
        for height in heights:
            place += [at + shard * height + k for k in range(height)]
            at += 8 * height
    lines = len(place) // 32
    count = len(place)
    return [
        order @ jnp.asarray(np.eye(count, dtype=np.float32)[np.array(place[k::lines])])
        for k in range(lines)
    ]


def per_device(
    tokens,
    word_counts,
    region_counts,
    qkv_weight,
    qkv_bias,
    out_weight,
    out_bias,
    attn_gain,
    attn_shift,
    up_weight,
    up_bias,
    down_weight,
    down_bias,
    ffn_gain,
    ffn_shift,
    cotangent,
):
    pairs, seq, d = tokens.shape
    n = pairs * seq
    shard_count, rep_count = lax.axis_size("shard"), lax.axis_size("rep")
    fast = shard_count == 8 and rep_count == 4
    rep, shard = lax.axis_index("rep"), lax.axis_index("shard")
    x, c, z, y = rep // 2, rep % 2, shard // 2, shard % 2
    meta = jnp.stack([x, c, z, y]).astype(jnp.int32)
    vectors = (qkv_bias, out_bias, attn_gain, attn_shift, up_bias, down_bias, ffn_gain, ffn_shift)
    small_own = jnp.concatenate(vectors)
    sizes = [v.shape[0] for v in vectors]

    flat = tokens.reshape(n, d)
    if fast:
        quarter = small_own.shape[0] // 4
        own_small = jnp.where(
            x == 0,
            jnp.where(c == 0, small_own[:quarter], small_own[2 * quarter : 3 * quarter]),
            jnp.where(c == 0, small_own[quarter : 2 * quarter], small_own[3 * quarter :]),
        )
        own_small = jnp.pad(own_small.astype(BF)[None, :], ((0, 15), (0, d // 2 - quarter)))
        own_one = jnp.concatenate(
            [quarter_of(qkv_weight, x, c), quarter_of(out_weight, x, c), own_small], axis=0
        )
        up_pieces = [lax.all_gather(quarter_of(up_weight, x, c), AXES, axis=0)]
        along_one = start_gather(own_one)
        eight_one = first_cross(along_one)
        more_one = to_cross(eight_one, 1)
        along_two = start_gather(after(quarter_of(down_weight, x, c), eight_one))
        other_one = to_core(eight_one)
        along_two, more_one, other_one = after((along_two, more_one, other_one))
        last_one = to_core(more_one)
        qkv_pieces = [eight_one, more_one, other_one, last_one]
        order = order_matrix(x, c, z, y)
        row = d // 4
        rel_small = jnp.concatenate([p[:, row, :quarter] for p in qkv_pieces]).astype(F32)
        whole_small = lax.dot_general(
            order, rel_small, (((0,), (0,)), ((), ())), precision=lax.Precision.HIGHEST
        ).reshape(8, -1)
        cross_two = to_cross(along_two, 0)
        first_deps = [along_two]
    else:
        qkv_pieces = [
            lax.all_gather(w.astype(BF), "shard", axis=0, tiled=True)
            for w in (qkv_weight, out_weight)
        ]
        whole_small = lax.all_gather(small_own.astype(BF), "shard", axis=0).astype(F32)
        first_deps = []
    parts, at = [], 0
    for size in sizes:
        parts.append(whole_small[:, at : at + size].reshape(1, -1))
        at += size
    bqv, bo, g1, c1, bu, bd, g2, c2 = parts

    vec_one = jnp.concatenate([bqv, bo, g1, c1], axis=1)
    joined, probs, mix, low, xhat, rstd, wqkv, wo = attention_forward(
        fast, meta, word_counts, region_counts, flat, vec_one, qkv_pieces, seq, first_deps
    )
    if fast:
        cross_two = after(cross_two, rstd)
        eight_two = jnp.concatenate([along_two, cross_two])
        more_two = to_cross(eight_two, 1)
        up_deps = [eight_two]
    else:
        up_pieces = [lax.all_gather(up_weight.astype(BF), "shard", axis=0, tiled=True)]
        up_deps = []
    act, slope, token = up_forward(fast, meta, low, bu, up_pieces, up_deps)
    if fast:
        more_two = after(more_two, token)
        down_pieces = [eight_two, more_two, to_core(after(eight_two, token)), to_core(more_two)]
    else:
        down_pieces = [lax.all_gather(down_weight.astype(BF), "shard", axis=0, tiled=True)]
    vec_two = jnp.concatenate([g1, c1, bd, g2, c2], axis=1)
    layer_out, second, hidden, sums_two, grad_bu, *down_grads = down_forward(
        fast, meta, word_counts, region_counts, act, slope, xhat, vec_two,
        cotangent.reshape(n, d), down_pieces, seq,
    )
    deps = []
    if fast:
        down_sum = Scatter(*down_grads)
    *up_grads, token, hidden = up_grad(fast, meta, hidden, low)
    deps = [token]
    if fast:
        up_sum = Scatter(*up_grads)
        deps += [down_sum.add_core([token])]
        down_sum.cross(1)
    attn_sum, attn_low, grad_mix, sums_first = first_back(
        fast, meta, second, hidden, up_pieces[0], xhat, rstd, g1, wo, deps
    )
    if fast:
        deps = [down_sum.got, up_sum.add_core([sums_first])]
        up_sum.cross(1)
    grad_joined, joined_far, sums_attn = attention_back(grad_mix, joined, probs, seq, deps)
    grad_vectors = [
        jnp.concatenate([sums_attn[0:1], sums_attn[1:2]], axis=1),
        sums_first[2:3],
        sums_first[0:1],
        sums_first[1:2],
        grad_bu,
        sums_two[2:3],
        sums_two[0:1],
        sums_two[1:2],
    ]
    small_grad = jnp.concatenate(grad_vectors, axis=1)
    if fast:
        lines = small_grad.reshape(-1, d // 8)
        small_rel = jnp.concatenate(
            [
                lax.dot_general(
                    m, lines, (((1,), (0,)), ((), ())), precision=lax.Precision.HIGHEST
                )
                for m in line_matrices(order, [v // (d // 8) for v in sizes])
            ],
            axis=1,
        )
        small_rel = jnp.pad(small_rel, ((0, 0), (0, d // 2 - quarter)))
        small_low = small_rel[16:].astype(BF)
        pair = Pair(down_sum, up_sum, [sums_attn])
        deps = [small_low, pair.token]
        small_got = to_core(small_low)
    else:
        deps = []
    qkv_out = qkv_grad(fast, meta, grad_joined, flat, attn_low, mix, deps)
    qkv_grads, token = qkv_out[:2], qkv_out[2]
    if fast:
        small_got, pair.got = after((small_got, pair.got), token)
        sent = after(qkv_grads[1], small_got, pair.got)
        qkv_sum = Scatter(qkv_grads[0], sent)
        pair.along()
        small = small_rel[:16] + small_got.astype(F32)
        token = qkv_sum.add_core([pair.token], small=small)
        qkv_sum.cross(1)
        tokens_grad = tokens_back(attn_sum, joined_far, wqkv, [token])
        token = qkv_sum.add_cross([tokens_grad])
        qkv_sum.cross(0)
        two = pair.total([token])
        across = to_x(two)
        token = qkv_sum.add_last()
        qkv_sum.along()
        across = after(across, token)
        height = two.shape[0] // 2
        down_mine = side_by_side(in_columns(two[:height]), in_columns(across[:height]), x)
        up_mine = side_by_side(two[height:], across[height:], x)
        down_other, up_other = to_core(down_mine), to_core(up_mine)
        grad_down = owner_block(down_mine, down_other, c, 0, down_mine.shape[0])
        grad_up = owner_block(up_mine, up_other, c, 0, up_mine.shape[0])
        qkv_total = qkv_sum.total()
        qkv_mine = side_by_side(qkv_total, to_x(qkv_total), x)
        qkv_other = to_core(qkv_mine)
        q_rows, o_rows = qkv_weight.shape[0] // 2, out_weight.shape[0] // 2
        grad_qkv = owner_block(qkv_mine, qkv_other, c, 0, q_rows)
        grad_out = owner_block(qkv_mine, qkv_other, c, q_rows, o_rows)
        small_all = owner_block(qkv_mine, qkv_other, c, q_rows + o_rows, 1)
        small_total = small_all.reshape(4, d // 2)[:, :quarter].reshape(-1)
    else:
        tokens_grad = tokens_back(attn_sum, joined_far, wqkv)

        def total(v):
            part = lax.psum_scatter(v.astype(F32), "shard", scatter_dimension=0, tiled=True)
            return lax.psum(part, "rep")

        grad_down, grad_up = total(down_grads[0]), total(up_grads[0])
        grad_qkv, grad_out = total(qkv_grads[0]), total(qkv_grads[1])
        small_total = lax.dynamic_index_in_dim(
            jnp.concatenate(
                [lax.psum(g, AXES).reshape(shard_count, -1) for g in grad_vectors], axis=1
            ),
            shard,
            axis=0,
            keepdims=False,
        )
    vector_grads, at = [], 0
    for size in sizes:
        vector_grads.append(small_total[at : at + size])
        at += size
    g_qv, g_bo, g_g1, g_c1, g_bu, g_bd, g_g2, g_c2 = vector_grads
    return (
        layer_out.reshape(tokens.shape),
        tokens_grad.reshape(tokens.shape),
        grad_qkv,
        g_qv,
        grad_out,
        g_bo,
        g_g1,
        g_c1,
        grad_up,
        g_bu,
        grad_down,
        g_bd,
        g_g2,
        g_c2,
    )


def solution(mesh):
    matrix, vector = P("shard", None), P("shard")
    batch, counts = P(AXES, None, None), P(AXES)
    weights = (
        matrix, vector, matrix, vector, vector, vector,
        matrix, vector, matrix, vector, vector, vector,
    )
    return jax.shard_map(
        per_device,
        mesh=mesh,
        in_specs=(batch, counts, counts) + weights + (batch,),
        out_specs=(batch, batch) + weights,
        check_vma=False,
    )
```

```python
import functools

import jax
import jax.numpy as jnp
import numpy as np
from jax import lax
from jax.experimental import pallas as pl
from jax.experimental.pallas import tpu as pltpu
from jax.sharding import PartitionSpec as P

HEADS = 12
WORDS_MAX = 28
EPS = 1e-05
BF = jnp.bfloat16
F32 = jnp.float32
ANY = pl.BlockSpec(memory_space=pl.ANY)
SMEM = pl.BlockSpec(memory_space=pltpu.SMEM)
HBM, VMEM = pltpu.HBM, pltpu.VMEM
TOKEN = jax.ShapeDtypeStruct((8, 128), F32)
WHOLE = pl.BlockSpec(memory_space=pltpu.VMEM)
SQRT_HALF = 0.7071067811865476
INV_SQRT_2PI = 0.3989422804014327


def nt(a, b):
    return lax.dot_general(a, b, (((1,), (1,)), ((), ())), preferred_element_type=F32)


def nn(a, b):
    return jnp.dot(a, b, preferred_element_type=F32)


def tn(a, b):
    return lax.dot_general(a, b, (((0,), (0,)), ((), ())), preferred_element_type=F32)


def fixed(shape):
    return pl.BlockSpec(shape, lambda i: (0,) * len(shape))


def rows(shape):
    return pl.BlockSpec(shape, lambda i: (i,) + (0,) * (len(shape) - 1))


def far(value):
    return pltpu.with_memory_space_constraint(value, HBM)


def near(value):
    return pltpu.with_memory_space_constraint(value, VMEM)


def kernel_call(body, deps, in_specs, args, mebibytes=8, **options):
    count, extra = len(args), len(deps)

    def inner(*refs):
        body(*refs[:count], *refs[count + extra :])

    call = pl.pallas_call(
        inner, in_specs=list(in_specs) + [ANY] * extra, compiler_params=params(mebibytes), **options
    )
    return call(*args, *deps)


def params(mebibytes):
    return pltpu.CompilerParams(vmem_limit_bytes=mebibytes * 1024 * 1024)


def piece_place(meta, cc, a, b, rz, local_rows, start, height, width):
    x0, z0, y0 = meta[0], meta[2], meta[3]
    y_rel = jnp.where(cc == 0, a, b)
    x_rel = jnp.where(cc == 0, b, a)
    shard = (z0 ^ rz) * 2 + (y0 ^ y_rel)
    row = shard * local_rows + cc * height + start
    col = (x0 ^ x_rel) * width
    return pl.multiple_of(row, 16), pl.multiple_of(col, 128)


def piece_copies(meta, pieces, whole, sems, local_rows, first, height, width):
    copies = []
    for number, ref in enumerate(pieces):
        cc = meta[1] if number < 2 else 1 - meta[1]
        a = number % 2
        for b in range(2):
            for rz in range(4):
                row, col = piece_place(meta, cc, a, b, rz, local_rows, 0, height, width)
                copies.append(
                    pltpu.make_async_copy(
                        ref.at[b * 4 + rz, pl.ds(first, height), :],
                        whole.at[pl.ds(row, height), pl.ds(col, width)],
                        sems.at[len(copies)],
                    )
                )
    return copies


def tile_waits(whole, outs, sems, count, first, height, span):
    return [
        pltpu.make_async_copy(
            whole.at[pl.ds(0, height), pl.ds(0, span)],
            ref.at[0, pl.ds(first, height), pl.ds(0, span)],
            sems.at[number * count + i],
        )
        for number, ref in enumerate(outs[1:])
        for i in range(count)
    ]


def load_copies(fast, meta, refs, whole, sems, first):
    if not fast:
        return [pltpu.make_async_copy(refs[0], whole, sems.at[0])]
    local_rows, cols = whole.shape[0] // 8, whole.shape[1]
    if len(refs) == 1:
        height, width = local_rows // 2, cols // 2
        return [
            pltpu.make_async_copy(
                refs[0].at[(x * 2 + c) * 8 + shard],
                whole.at[
                    pl.ds(shard * local_rows + c * height, height), pl.ds(x * width, width)
                ],
                sems.at[(x * 2 + c) * 8 + shard],
            )
            for x in range(2)
            for c in range(2)
            for shard in range(8)
        ]
    return piece_copies(meta, refs, whole, sems, local_rows, first, local_rows // 2, cols // 2)


def go(copies):
    for copy in copies:
        copy.start()


def done(copies):
    for copy in copies:
        copy.wait()


def key_mask(words, regions, shape, axis):
    place = lax.broadcasted_iota(jnp.int32, shape, axis)
    return (place < words) | ((place >= WORDS_MAX) & (place < WORDS_MAX + regions))


def split_heads(block):
    low = lax.broadcasted_iota(jnp.int32, block.shape, 1) < 64
    zero = jnp.zeros_like(block)
    return jnp.concatenate([jnp.where(low, block, zero), jnp.where(low, zero, block)], axis=0)


def turn_heads(block):
    n = block.shape[0]
    return jnp.concatenate([block[:, :n].T, block[:, n:].T], axis=1)


def norm_parts(value):
    center = value - jnp.mean(value, axis=-1, keepdims=True)
    rstd = lax.rsqrt(jnp.mean(center * center, axis=-1, keepdims=True) + EPS)
    return center * rstd, rstd


def norm_back(grad, xhat, rstd, gain):
    scaled = grad * gain
    mean_one = jnp.mean(scaled, axis=-1, keepdims=True)
    mean_two = jnp.mean(scaled * xhat, axis=-1, keepdims=True)
    return rstd * (scaled - mean_one - xhat * mean_two)


def attention_kernel(fast, n_in, *refs):
    meta, words, regions = refs[:3]
    x_ref, vec_ref = refs[3:5]
    pieces = refs[5 : 5 + n_in]
    (joined_ref, probs_ref, mix_ref, low_ref, xhat_ref, rstd_ref, wqkv_out, wo_out) = refs[
        5 + n_in : 13 + n_in
    ]
    wqkv, wo, sem_a, sem_b, sem_c = refs[13 + n_in :]
    step = pl.program_id(0)
    d = x_ref.shape[1]
    seq = probs_ref.shape[2]

    @pl.when(step == 0)
    def _():
        if fast:
            first = load_copies(fast, meta, pieces, wqkv, sem_a, 0)
            second = load_copies(fast, meta, pieces, wo, sem_b, wqkv.shape[0] // 16)
        else:
            first = load_copies(fast, meta, pieces[:1], wqkv, sem_a, 0)
            second = load_copies(fast, meta, pieces[1:], wo, sem_b, 0)
        go(first)
        go(second)
        done(first)
        done(second)

    saves = [
        pltpu.make_async_copy(wqkv, wqkv_out, sem_c.at[0]),
        pltpu.make_async_copy(wo, wo_out, sem_c.at[1]),
    ]

    @pl.when(step == 0)
    def _():
        go(saves)

    x = x_ref[...]
    bq = vec_ref[:, :d]
    bv = vec_ref[:, d : 2 * d]
    joined_ref[:, :d] = (nt(x, wqkv[:d, :]) + bq).astype(BF) * BF(0.125)
    joined_ref[:, d : 2 * d] = nt(x, wqkv[d : 2 * d, :]).astype(BF)
    joined_ref[:, 2 * d :] = (nt(x, wqkv[2 * d :, :]) + bv).astype(BF)
    per_step = x_ref.shape[0] // seq
    for p in range(per_step):
        pair = step * per_step + p
        valid = key_mask(words[pair], regions[pair], (seq, 2 * seq), 0)
        here = pl.ds(p * seq, seq)
        for h in range(d // 128):
            cols = pl.ds(h * 128, 128)
            queries = split_heads(joined_ref[here, pl.ds(h * 128, 128)])
            keys = joined_ref[here, pl.ds(d + h * 128, 128)]
            values = split_heads(joined_ref[here, pl.ds(2 * d + h * 128, 128)])
            scores = jnp.where(valid, nt(keys, queries), -1000000000.0)
            exponent = jnp.exp(scores - jnp.max(scores, axis=0, keepdims=True))
            probs = exponent * (1.0 / jnp.sum(exponent, axis=0, keepdims=True))
            probs = probs.astype(BF)
            probs_ref[p, h] = probs
            mix_ref[here, cols] = nn(turn_heads(probs), values).astype(BF)
    first_sum = x.astype(F32) + nt(mix_ref[...], wo[...]) + vec_ref[:, 2 * d : 3 * d]
    xhat, rstd = norm_parts(first_sum)
    xhat_ref[...] = xhat
    rstd_ref[...] = jnp.broadcast_to(rstd, rstd_ref.shape)
    low_ref[...] = (xhat * vec_ref[:, 3 * d : 4 * d] + vec_ref[:, 4 * d : 5 * d]).astype(BF)

    @pl.when(step == pl.num_programs(0) - 1)
    def _():
        done(saves)


def attention_forward(fast, meta, words, regions, x, vec, pieces, seq, deps=()):
    n, d = x.shape
    tile = 2 * seq
    shapes = [
        HBM((n, 3 * d), BF),
        HBM((n // seq, d // 128, seq, 2 * seq), BF),
        HBM((n, d), BF),
        HBM((n, d), BF),
        HBM((n, d), F32),
        HBM((n, 128), F32),
        HBM((3 * d, d), BF),
        HBM((d, d), BF),
    ]
    return kernel_call(
        functools.partial(attention_kernel, fast, len(pieces)),
        deps,
        [SMEM] * 3 + [rows((tile, d)), fixed(vec.shape)] + [ANY] * len(pieces),
        [meta, words, regions, far(x), vec, *map(far, pieces)],
        grid=(n // tile,),
        out_specs=[
            rows((tile, 3 * d)),
            rows((2, d // 128, seq, 2 * seq)),
            rows((tile, d)),
            rows((tile, d)),
            rows((tile, d)),
            rows((tile, 128)),
            ANY,
            ANY,
        ],
        out_shape=shapes,
        scratch_shapes=[
            pltpu.VMEM((3 * d, d), BF),
            pltpu.VMEM((d, d), BF),
            pltpu.SemaphoreType.DMA((32,)),
            pltpu.SemaphoreType.DMA((32,)),
            pltpu.SemaphoreType.DMA((2,)),
        ],
        cost_estimate=pl.CostEstimate(
            flops=2 * n * d * 4 * d, bytes_accessed=16 * n * d, transcendentals=0
        ),
        mebibytes=17,
        name="attention_forward",
    )


def up_kernel(fast, n_in, *refs):
    meta, low_far, bias_ref = refs[:3]
    pieces = refs[3 : 3 + n_in]
    act_ref, slope_ref, token_ref, low_ref, w, sem_a, sem_b = refs[3 + n_in :]
    token_ref[...] = jnp.zeros_like(token_ref)
    n = low_ref.shape[0]
    tile, width = 256, w.shape[0] // 4
    reads = [pltpu.make_async_copy(low_far, low_ref, sem_b.at[0])]
    go(reads)
    loads = load_copies(fast, meta, pieces, w, sem_a, 0)
    parts = [loads] + [[]] * 3
    if len(loads) == 32:
        parts = [[v for k, v in enumerate(loads) if k % 8 // 2 == j] for j in range(4)]
    for part in parts:
        go(part)
    done(reads)
    for j in range(4):
        done(parts[j])
        here = slice(j * width, (j + 1) * width)
        for i in range(n // tile):
            part = slice(i * tile, (i + 1) * tile)
            hidden = nt(low_ref[part, :], w[here, :]) + bias_ref[:, here]
            phi = 0.5 + 0.5 * lax.erf(hidden * SQRT_HALF)
            act_ref[part, here] = (hidden * phi).astype(BF)
            bell = jnp.exp(hidden * hidden * -0.5) * INV_SQRT_2PI
            slope_ref[part, here] = (phi + hidden * bell).astype(BF)


def up_forward(fast, meta, low, bias, pieces, deps=()):
    n, d = low.shape
    ff = bias.shape[1]
    return kernel_call(
        functools.partial(up_kernel, fast, len(pieces)),
        deps,
        [SMEM, ANY, WHOLE] + [ANY] * len(pieces),
        [meta, far(low), bias, *map(far, pieces)],
        out_specs=[WHOLE] * 3,
        out_shape=[VMEM((n, ff), BF), VMEM((n, ff), BF), TOKEN],
        scratch_shapes=[
            pltpu.VMEM((n, d), BF),
            pltpu.VMEM((ff, d), BF),
            pltpu.SemaphoreType.DMA((32,)),
            pltpu.SemaphoreType.DMA((1,)),
        ],
        cost_estimate=pl.CostEstimate(
            flops=4 * n * d * ff, bytes_accessed=4 * n * ff, transcendentals=0
        ),
        mebibytes=14,
        name="up_forward",
    )


def down_kernel(fast, n_in, seq, *refs):
    meta, words, regions = refs[:3]
    act_ref, slope_ref, xhat_far, vec_ref, cot_far = refs[3:8]
    pieces = refs[8 : 8 + n_in]
    outs_end = 13 + n_in + (2 if fast else 1)
    out_far, second_far, hidden_ref, sums_ref, bias_ref = refs[8 + n_in : 13 + n_in]
    grads = refs[13 + n_in : outs_end]
    xhat_ref, cot_ref, out_ref, second_ref, feed_ref, w, whole = refs[outs_end:-3]
    sem_a, sem_b, sem_c = refs[-3:]
    n, d = feed_ref.shape
    ff = act_ref.shape[1]
    tile = 256
    count = n // tile
    loads = load_copies(fast, meta, pieces, w, sem_a, 0)
    go(loads)
    reads, writes = [], []
    for i in range(count):
        part = pl.ds(i * tile, tile)
        reads.append(
            [
                pltpu.make_async_copy(xhat_far.at[part], xhat_ref.at[part], sem_b.at[0, i]),
                pltpu.make_async_copy(cot_far.at[part], cot_ref.at[part], sem_b.at[1, i]),
            ]
        )
        writes += [
            pltpu.make_async_copy(out_ref.at[part], out_far.at[part], sem_b.at[2, i]),
            pltpu.make_async_copy(second_ref.at[part], second_far.at[part], sem_b.at[3, i]),
        ]
    for pair in reads:
        go(pair)
    gain_one, shift_one = vec_ref[:, :d], vec_ref[:, d : 2 * d]
    bias, gain, shift = vec_ref[:, 2 * d : 3 * d], vec_ref[:, 3 * d : 4 * d], vec_ref[:, 4 * d :]
    done(loads)
    sums = [jnp.zeros((1, d), F32)] * 3
    product = nt(act_ref[:tile, :], w[...])
    for i in range(count):
        part = slice(i * tile, (i + 1) * tile)
        done(reads[i])
        if i:
            go(writes[2 * i - 2 : 2 * i])
        this = product
        if i + 1 < count:
            product = nt(act_ref[(i + 1) * tile : (i + 2) * tile, :], w[...])
        second_sum = xhat_ref[part, :] * gain_one + shift_one + this + bias
        xhat, rstd = norm_parts(second_sum)
        first = i * (tile // seq)
        keep = jnp.concatenate(
            [
                key_mask(words[first + p], regions[first + p], (seq, 128), 0)
                for p in range(tile // seq)
            ],
            axis=0,
        )[:, :1]
        out_ref[part, :] = jnp.where(keep, xhat * gain + shift, 0.0).astype(BF)
        grad = jnp.where(keep, cot_ref[part, :].astype(F32), 0.0)
        second = norm_back(grad, xhat, rstd, gain)
        second_ref[part, :] = second
        feed = second.astype(BF)
        feed_ref[part, :] = feed
        for k, value in enumerate((grad * xhat, grad, feed.astype(F32))):
            sums[k] = sums[k] + jnp.sum(value, axis=0, keepdims=True)
    go(writes[-2:])
    for k in range(3):
        sums_ref[k : k + 1, :] = sums[k]
    width = 512
    for i in range(ff // width):
        here = slice(i * width, (i + 1) * width)
        hidden = nn(feed_ref[...], w[:, here]) * slope_ref[:, here].astype(F32)
        hidden = hidden.astype(BF)
        hidden_ref[:, here] = hidden
        bias_ref[:, here] = jnp.sum(hidden.astype(F32), axis=0, keepdims=True)
    waits = []
    width, span = ff // 4, ff // 8
    for i in range(4):
        here = slice(i * width, (i + 1) * width)
        whole[:, here] = tn(feed_ref[...], act_ref[:, here]).astype(BF)
        if fast:
            for k in range(2):
                chunk = (i % 2) * 2 + k
                copies = tile_copies(
                    meta, whole, grads, sem_c.at[2 * i + k], range(8), [i // 2], d // 8,
                    chunk * (d // 16), d // 16, ff // 2, (chunk * span, span),
                )
                go(copies)
                waits += tile_waits(
                    whole, grads, sem_c.at[2 * i + k], 8, chunk * (d // 16), d // 16, span
                )
    if not fast:
        waits = [pltpu.make_async_copy(whole, grads[0], sem_c.at[0, 0])]
        go(waits)
    done(waits)
    done(writes)


def down_forward(
    fast, meta, words, regions, act, slope, xhat, vec, cot, pieces, seq, deps=()
):
    n, ff = act.shape
    d = xhat.shape[1]
    shapes = grad_shapes(fast, d, ff)
    return kernel_call(
        functools.partial(down_kernel, fast, len(pieces), seq),
        deps,
        [SMEM] * 3 + [WHOLE, WHOLE, ANY, WHOLE, ANY] + [ANY] * len(pieces),
        [meta, words, regions, near(act), near(slope), far(xhat), vec, far(cot), *map(far, pieces)],
        out_specs=[ANY, ANY, WHOLE, WHOLE, WHOLE] + [WHOLE, ANY][-len(shapes) :],
        out_shape=[
            HBM((n, d), BF),
            HBM((n, d), F32),
            VMEM((n, ff), BF),
            jax.ShapeDtypeStruct((8, d), F32),
            jax.ShapeDtypeStruct((1, ff), F32),
        ]
        + shapes,
        scratch_shapes=[
            pltpu.VMEM((n, d), F32),
            pltpu.VMEM((n, d), BF),
            pltpu.VMEM((n, d), BF),
            pltpu.VMEM((n, d), F32),
            pltpu.VMEM((n, d), BF),
            pltpu.VMEM((d, ff), BF),
            pltpu.VMEM((d, ff), BF),
            pltpu.SemaphoreType.DMA((32,)),
            pltpu.SemaphoreType.DMA((4, n // 256)),
            pltpu.SemaphoreType.DMA((8, 16)),
        ],
        cost_estimate=pl.CostEstimate(
            flops=12 * n * d * ff, bytes_accessed=2 * n * ff, transcendentals=0
        ),
        mebibytes=28,
        name="down_forward",
    )


def grad_shapes(fast, total_rows, cols):
    if fast:
        width = min(total_rows, cols) // 2
        shape = (16, total_rows * cols // (32 * width), width)
        return [VMEM(shape, BF), HBM(shape, BF)]
    return [HBM((total_rows, cols), BF)]


def tile_copies(meta, whole, outs, sems, shards, sides, local_rows, first, height, width, cols=None):
    x0, c0, z0, y0 = meta[0], meta[1], meta[2], meta[3]
    offset, span = (0, width) if cols is None else cols
    there = pl.ds(0, span)
    copies = []
    for number, ref in enumerate(outs):
        cc = c0 ^ number
        for shard in shards:
            for side in sides:
                y_rel, x_rel = y0 ^ (shard % 2), x0 ^ side
                a = jnp.where(cc == 0, y_rel, x_rel)
                b = jnp.where(cc == 0, x_rel, y_rel)
                row = pl.multiple_of(shard * local_rows + cc * height, 16)
                col = pl.multiple_of(side * width + offset, 128)
                place = a * 8 + b * 4 + (z0 ^ (shard // 2))
                if number == 0:
                    static = pl.ds(side * width + offset, span)
                    ref[place, pl.ds(first, height), there] = whole[pl.ds(row, height), static]
                    continue
                copies.append(
                    pltpu.make_async_copy(
                        whole.at[pl.ds(row, height), pl.ds(col, span)],
                        ref.at[place, pl.ds(first, height), there],
                        sems.at[len(copies)],
                    )
                )
    return copies


def up_grad_kernel(fast, *refs):
    meta, hidden_ref, low_far, wu_far, *others_far = refs[:8]
    outs = refs[8 : (10 if fast else 9)]
    token_ref, _, wu_ref, *others = refs[10 if fast else 9 : -5]
    low_ref, whole, sems, sem_b, sem_c = refs[-5:]
    reads = [pltpu.make_async_copy(low_far, low_ref, sem_b.at[0])]
    go(reads)
    ahead = load_copies(fast, meta, [wu_far], wu_ref, sem_c, 0)
    for i, (source, target) in enumerate(zip(others_far, others)):
        ahead.append(pltpu.make_async_copy(source, target, sem_b.at[1 + i]))
    go(ahead)
    token_ref[...] = jnp.zeros_like(token_ref)
    done(reads)
    ff, d = whole.shape
    height = ff // 4
    waits = []
    for i in range(4):
        here = slice(i * height, (i + 1) * height)
        whole[here, :] = tn(hidden_ref[:, here], low_ref[...]).astype(BF)
        if fast:
            copies = tile_copies(
                meta, whole, outs, sems.at[i], [2 * i, 2 * i + 1], [0, 1], ff // 8, 0, ff // 16,
                d // 2,
            )
            go(copies)
            waits += tile_waits(whole, outs, sems.at[i], 4, 0, ff // 16, d // 2)
    if not fast:
        waits = [pltpu.make_async_copy(whole, outs[0], sems.at[0, 0])]
        go(waits)
    done(waits + ahead)


def up_grad(fast, meta, hidden, low, wu, others, deps=()):
    n, d = low.shape
    ff = hidden.shape[1]
    shapes = grad_shapes(fast, ff, d)
    return kernel_call(
        functools.partial(up_grad_kernel, fast),
        deps,
        [SMEM, WHOLE] + [ANY] * 6,
        [meta, near(hidden), far(low), far(wu), *map(far, others)],
        out_specs=[WHOLE, ANY][-len(shapes) :] + [WHOLE] * 7,
        out_shape=shapes
        + [TOKEN, VMEM((n, ff), BF), VMEM((ff, d), BF)]
        + [VMEM(v.shape, v.dtype) for v in others],
        scratch_shapes=[
            pltpu.VMEM((n, d), BF),
            pltpu.VMEM((ff, d), BF),
            pltpu.SemaphoreType.DMA((4, 8)),
            pltpu.SemaphoreType.DMA((5,)),
            pltpu.SemaphoreType.DMA((32,)),
        ],
        input_output_aliases={1: len(shapes) + 1},
        cost_estimate=pl.CostEstimate(
            flops=4 * n * d * ff, bytes_accessed=2 * n * ff, transcendentals=0
        ),
        mebibytes=12,
        name="up_grad",
    )


def first_back_kernel(*refs):
    second_ref, hidden_ref, wu_ref, xhat_ref, rstd_ref, wo_ref, gain_ref = refs[:7]
    sum_far, low_far, mix_ref, sums_ref, sum_ref, low_ref, sem = refs[7:]
    n, d = low_ref.shape
    tile = 256
    count = n // tile
    writes = []
    for i in range(count):
        part = pl.ds(i * tile, tile)
        writes.append(
            [
                pltpu.make_async_copy(sum_ref.at[part], sum_far.at[part], sem.at[0, i]),
                pltpu.make_async_copy(low_ref.at[part], low_far.at[part], sem.at[1, i]),
            ]
        )
    product = nn(hidden_ref[:tile, :], wu_ref[...])
    sums = [jnp.zeros((1, d), F32)] * 3
    for i in range(count):
        part = slice(i * tile, (i + 1) * tile)
        if i:
            go(writes[i - 1])
        grad = second_ref[part, :] + product
        if i + 1 < count:
            product = nn(hidden_ref[(i + 1) * tile : (i + 2) * tile, :], wu_ref[...])
        xhat = xhat_ref[part, :]
        attn_sum = norm_back(grad, xhat, rstd_ref[part, :1], gain_ref[...])
        sum_ref[part, :] = attn_sum
        low = attn_sum.astype(BF)
        low_ref[part, :] = low
        mix_ref[part, :] = nn(low, wo_ref[...]).astype(BF)
        for k, value in enumerate((grad * xhat, grad, low.astype(F32))):
            sums[k] = sums[k] + jnp.sum(value, axis=0, keepdims=True)
    go(writes[-1])
    for k in range(3):
        sums_ref[k : k + 1, :] = sums[k]
    for group in writes:
        done(group)


def first_back(second, hidden, wu, xhat, rstd, wo, gain, deps=()):
    n, ff = hidden.shape
    d = xhat.shape[1]
    return kernel_call(
        first_back_kernel,
        deps,
        [WHOLE] * 7,
        [near(v) for v in (second, hidden, wu, xhat, rstd, wo)] + [gain],
        out_specs=[ANY, ANY, WHOLE, WHOLE],
        out_shape=[
            HBM((n, d), F32),
            HBM((n, d), BF),
            VMEM((n, d), BF),
            jax.ShapeDtypeStruct((8, d), F32),
        ],
        scratch_shapes=[
            pltpu.VMEM((n, d), F32),
            pltpu.VMEM((n, d), BF),
            pltpu.SemaphoreType.DMA((2, n // 256)),
        ],
        cost_estimate=pl.CostEstimate(
            flops=4 * n * d * ff, bytes_accessed=2 * n * ff, transcendentals=0
        ),
        mebibytes=12,
        name="first_back",
    )


def attention_back_kernel(seq, *refs):
    mix_ref, joined_ref, probs_ref, grad_ref, sums_ref = refs
    d = mix_ref.shape[1]

    @pl.when(pl.program_id(0) == 0)
    def _():
        sums_ref[...] = jnp.zeros_like(sums_ref)

    for p in range(mix_ref.shape[0] // seq):
        here = pl.ds(p * seq, seq)
        for h in range(d // 128):
            one = pl.ds(h * 128, 128)
            two = pl.ds(d + h * 128, 128)
            three = pl.ds(2 * d + h * 128, 128)
            outer = split_heads(mix_ref[here, one])
            probs = probs_ref[p, h]
            grad_probs = nt(joined_ref[here, three], outer)
            wide = probs.astype(F32)
            product = wide * grad_probs
            scores = product - wide * jnp.sum(product, axis=0, keepdims=True)
            scores = scores.astype(BF)
            grad_ref[here, three] = nn(probs, outer).astype(BF)
            grad_ref[here, two] = nn(scores, split_heads(joined_ref[here, one])).astype(BF)
            keys = split_heads(joined_ref[here, two])
            grad_ref[here, one] = (nn(turn_heads(scores), keys) * 0.125).astype(BF)
    sums_ref[0:1, :] += jnp.sum(grad_ref[:, :d].astype(F32), axis=0, keepdims=True)
    sums_ref[1:2, :] += jnp.sum(grad_ref[:, 2 * d :].astype(F32), axis=0, keepdims=True)


def attention_back(mix, joined, probs, seq, deps=()):
    n, d = mix.shape
    tile = 2 * seq
    return kernel_call(
        functools.partial(attention_back_kernel, seq),
        deps,
        [
            rows((tile, d)),
            rows((tile, 3 * d)),
            rows((2, d // 128, seq, 2 * seq)),
        ],
        [near(mix), far(joined), far(probs)],
        grid=(n // tile,),
        out_specs=[rows((tile, 3 * d)), fixed((8, d))],
        out_shape=[
            HBM((n, 3 * d), BF),
            jax.ShapeDtypeStruct((8, d), F32),
        ],
        cost_estimate=pl.CostEstimate(
            flops=16 * n * d * d, bytes_accessed=30 * n * d, transcendentals=0
        ),
        mebibytes=14,
        name="attention_back",
    )


def qkv_grad_kernel(fast, *refs):
    meta, grad_far, x_far, low_far, mix_far = refs[:5]
    outs = refs[5:7]
    token_ref, whole, whole_out, grad_ref, x_ref, low_ref, mix_ref, sem_a, sem_b, sem_c = refs[7:]
    total, d = whole.shape
    width = total // 6
    columns = [pl.ds(i * width, width) for i in range(6)]
    reads = [
        pltpu.make_async_copy(x_far, x_ref, sem_c.at[0]),
        pltpu.make_async_copy(low_far, low_ref, sem_c.at[1]),
        pltpu.make_async_copy(mix_far, mix_ref, sem_c.at[2]),
    ]
    grads = [
        pltpu.make_async_copy(grad_far.at[:, here], grad_ref.at[:, here], sem_c.at[3 + i])
        for i, here in enumerate(columns)
    ]
    go(reads[:1] + grads + reads[1:])
    token_ref[...] = jnp.zeros_like(token_ref)
    waits = []
    done(reads[:1])
    for i in range(2):
        for k in range(3 * i, 3 * i + 3):
            done([grads[k]])
            here = slice(k * width, (k + 1) * width)
            whole[here, :] = tn(grad_ref[:, here], x_ref[...]).astype(BF)
        if fast:
            go(
                tile_copies(
                    meta, whole, outs, sem_a.at[i], range(4 * i, 4 * i + 4), [0, 1], total // 8,
                    0, total // 16, d // 2,
                )
            )
            waits += tile_waits(whole, outs, sem_a.at[i], 8, 0, total // 16, d // 2)
    done(reads[1:])
    whole_out[...] = tn(low_ref[...], mix_ref[...]).astype(BF)
    if fast:
        go(
            tile_copies(
                meta, whole_out, outs, sem_b, range(8), [0, 1], d // 8, total // 16, d // 16,
                d // 2,
            )
        )
        waits += tile_waits(whole_out, outs, sem_b, 16, total // 16, d // 16, d // 2)
    else:
        waits = [
            pltpu.make_async_copy(whole, outs[0], sem_b.at[0]),
            pltpu.make_async_copy(whole_out, outs[1], sem_b.at[1]),
        ]
        go(waits)
    done(waits)


def qkv_grad(fast, meta, grad, x, low, mix, deps=()):
    n, d = x.shape
    if fast:
        shapes = [f((16, 4 * d // 16, d // 2), BF) for f in (VMEM, HBM)]
    else:
        shapes = [jax.ShapeDtypeStruct((3 * d, d), BF), jax.ShapeDtypeStruct((d, d), BF)]
    return kernel_call(
        functools.partial(qkv_grad_kernel, fast),
        deps,
        [SMEM, ANY, ANY, ANY, ANY],
        [meta, far(grad), far(x), far(low), far(mix)],
        out_specs=([WHOLE, ANY] if fast else [ANY] * 2) + [WHOLE],
        out_shape=shapes + [TOKEN],
        scratch_shapes=[
            pltpu.VMEM((3 * d, d), BF),
            pltpu.VMEM((d, d), BF),
            pltpu.VMEM((n, 3 * d), BF),
            pltpu.VMEM((n, d), BF),
            pltpu.VMEM((n, d), BF),
            pltpu.VMEM((n, d), BF),
            pltpu.SemaphoreType.DMA((2, 16)),
            pltpu.SemaphoreType.DMA((32,)),
            pltpu.SemaphoreType.DMA((9,)),
        ],
        cost_estimate=pl.CostEstimate(
            flops=16 * n * d * d, bytes_accessed=16 * n * d, transcendentals=0
        ),
        mebibytes=20,
        name="qkv_grad",
    )


def tokens_grad_kernel(sum_ref, grad_ref, w_ref, out_ref, token_ref):
    token_ref[...] = jnp.zeros_like(token_ref)
    out_ref[...] = sum_ref[...] + nn(grad_ref[...], w_ref[...])


def tokens_back(attn_sum, grad, w, deps=()):
    n, d = attn_sum.shape
    tile = 256
    return kernel_call(
        tokens_grad_kernel,
        deps,
        [rows((tile, d)), rows((tile, 3 * d)), fixed((3 * d, d))],
        [far(attn_sum), far(grad), far(w)],
        grid=(n // tile,),
        out_specs=[rows((tile, d)), fixed((8, 128))],
        out_shape=[HBM((n, d), F32), TOKEN],
        cost_estimate=pl.CostEstimate(
            flops=12 * n * d * d, bytes_accessed=14 * n * d, transcendentals=0
        ),
        mebibytes=14,
        name="tokens_back",
    )


AXES = ("rep", "shard")


def route(fn):
    pairs = []
    for x in range(2):
        for c in range(2):
            for z in range(4):
                for y in range(2):
                    to = fn(x, c, z, y)
                    pairs.append(
                        ((x * 2 + c) * 8 + z * 2 + y, (to[0] * 2 + to[1]) * 8 + to[2] * 2 + to[3])
                    )
    return pairs


def to_core(v):
    return lax.ppermute(v, AXES, route(lambda x, c, z, y: (x, 1 - c, z, y)))


def to_x(v):
    return lax.ppermute(v, AXES, route(lambda x, c, z, y: (1 - x, c, z, y)))


def to_z(v, k):
    return lax.ppermute(v, AXES, route(lambda x, c, z, y: (x, c, z ^ k, y)))


def to_cross(v, first_core):
    return lax.ppermute(
        v,
        AXES,
        route(lambda x, c, z, y: (1 - x, c, z, y) if c == first_core else (x, c, z, 1 - y)),
    )


def after(value, *others):
    return lax.optimization_barrier((value, others))[0]


def start_gather(own):
    return jnp.stack([own] + [to_z(own, k) for k in (1, 2, 3)])


def first_cross(along):
    return jnp.concatenate([along, to_cross(along, 0)])


def add_core_kernel(kept_ref, got_ref, *refs):
    keep_ref, send_ref = refs[-2:]
    count, height, width = keep_ref.shape
    for k in range(count):
        here = slice(k * height, (k + 1) * height)
        keep_ref[k] = (kept_ref[k].astype(F32) + got_ref[k].astype(F32)).astype(BF)
        other = kept_ref[count + k].astype(F32) + got_ref[count + k].astype(F32)
        send_ref[here, :] = other.astype(BF)
    if len(refs) == 3:
        send_ref[count * height :, :] = refs[0][...].astype(BF)


def add_cross_kernel(keep_ref, got_ref, *refs):
    small = len(refs) == 4
    new_ref, send_ref = refs[1:3] if small else refs
    count, height, width = new_ref.shape
    for k in range(2 * count):
        here = slice(k * height, (k + 1) * height)
        total = (keep_ref[k].astype(F32) + got_ref[here, :].astype(F32)).astype(BF)
        if k < count:
            new_ref[k] = total
        else:
            send_ref[(k - count) * height : (k - count + 1) * height, :] = total
    if small:
        rows_in = refs[0][...] + got_ref[2 * count * height :, :].astype(F32)
        refs[3][...] = rows_in
        tail = jnp.concatenate([rows_in[count : 2 * count], rows_in[2 * count :]], axis=0)
        tail = jnp.concatenate([tail, jnp.zeros((count, width), F32)], axis=0)
        send_ref[count * height :, :] = tail.astype(BF)


def add_last_kernel(keep_ref, got_ref, *refs):
    small = len(refs) == 5
    outs = refs[1:] if small else refs
    count, height, width = keep_ref.shape
    if small:
        rows_in = refs[0][...] + got_ref[count * height :, :].astype(F32)
        place = lax.broadcasted_iota(jnp.int32, rows_in.shape, 0)
    for k in range(count):
        here = slice(k * height, (k + 1) * height)
        total = keep_ref[k].astype(F32) + got_ref[here, :].astype(F32)
        outs[k][:height, :] = total.astype(outs[k].dtype)
        if small:
            row = jnp.sum(jnp.where(place == k, rows_in, 0.0), axis=0, keepdims=True)
            outs[k][height:, :] = jnp.broadcast_to(row, (16, width)).astype(outs[k].dtype)


def total_kernel(own_ref, one_ref, two_ref, three_ref, out_ref):
    total = own_ref[...] + one_ref[...].astype(F32)
    total = total + two_ref[...].astype(F32) + three_ref[...].astype(F32)
    out_ref[...] = total.astype(BF)


class Scatter:
    def __init__(self, kept, sent):
        self.kept, self.small = kept, None
        self.got = to_core(sent)

    def call(self, body, out_shape, extra, deps, name):
        args = [near(self.keep), near(self.got)] + list(extra)

        def marked(*refs):
            refs[-1][...] = jnp.zeros_like(refs[-1])
            body(*refs[:-1])

        *out, self.token = kernel_call(
            marked,
            deps,
            [WHOLE] * len(args),
            args,
            out_specs=[WHOLE] * (len(out_shape) + 1),
            out_shape=out_shape + [TOKEN],
            name=name,
        )
        return out

    def add_core(self, deps=(), small=None):
        self.keep = self.kept
        count, height, width = self.kept.shape[0] // 2, *self.kept.shape[1:]
        tail, extra = 0, []
        if small is not None:
            tail, extra = 16, [jnp.concatenate([small[8:], jnp.zeros_like(small[8:])])]
            self.small = jnp.concatenate([small[:8], jnp.zeros_like(small[8:])])
        self.keep, self.send = self.call(
            add_core_kernel,
            [VMEM((count, height, width), BF), VMEM((count * height + tail, width), BF)],
            extra,
            deps,
            "add_core",
        )
        return self.token

    def cross(self, core):
        self.got = to_cross(self.send, core)

    def add_cross(self, deps=()):
        count, height, width = self.keep.shape[0] // 2, *self.keep.shape[1:]
        small = self.small is not None
        outs = [
            VMEM((count, height, width), BF),
            VMEM((count * height + 16 * small, width), BF),
        ]
        if small:
            outs.append(VMEM((16, width), F32))
        out = self.call(
            add_cross_kernel, outs, [self.small] if small else [], deps, "add_cross"
        )
        self.keep, self.send = out[:2]
        if small:
            self.small = out[2]
        return self.token

    def add_last(self, deps=()):
        height, width = self.keep.shape[1:]
        small = self.small is not None
        shape = (height + 16 * small, width)
        self.parts = self.call(
            add_last_kernel,
            [VMEM(shape, F32)] + [VMEM(shape, BF)] * 3,
            [self.small] if small else [],
            deps,
            "add_last",
        )
        return self.token

    def along(self):
        self.got = [to_z(self.parts[k], k) for k in (1, 2, 3)]

    def total(self, deps=()):
        args = [near(v) for v in [self.parts[0]] + self.got]
        return kernel_call(
            total_kernel,
            deps,
            [WHOLE] * 4,
            args,
            out_specs=WHOLE,
            out_shape=jax.ShapeDtypeStruct(self.parts[0].shape, BF),
            name="total",
        )


def finish_kernel(meta, mine_ref, other_ref, qkv_ref, out_ref, small_ref):
    c = meta[1]
    first = 0
    for target in (qkv_ref, out_ref):
        half = target.shape[0] // 2
        part = slice(first, first + half)
        target[pl.ds(pl.multiple_of(c * half, 8), half), :] = mine_ref[part, :].astype(F32)
        target[pl.ds(pl.multiple_of((1 - c) * half, 8), half), :] = other_ref[part, :].astype(F32)
        first += half
    mine = mine_ref[first : first + 16, :].astype(F32)[:1]
    other = other_ref[first : first + 16, :].astype(F32)[:1]
    width = small_ref.shape[1]
    for k, line in enumerate((jnp.where(c == 0, mine, other), jnp.where(c == 0, other, mine))):
        small_ref[2 * k : 2 * k + 1, :] = line[:, :width]
        small_ref[2 * k + 1 : 2 * k + 2, :] = line[:, width:]


def finish(meta, mine, other, d):
    return kernel_call(
        finish_kernel,
        [],
        [SMEM, WHOLE, WHOLE],
        [meta, near(mine), near(other)],
        out_specs=[WHOLE] * 3,
        out_shape=[HBM((3 * d // 8, d), F32), HBM((d // 8, d), F32), VMEM((4, d // 2), F32)],
        name="finish",
    )


def in_columns(piece):
    return jnp.concatenate(jnp.split(piece, 4, axis=0), axis=1)


def side_by_side(low, across, x):
    return jnp.concatenate(
        [jnp.where(x == 0, low, across), jnp.where(x == 0, across, low)], axis=1
    )


def owner_block(mine, other, c, first, height):
    mine, other = mine[first : first + height], other[first : first + height]
    return jnp.concatenate(
        [jnp.where(c == 0, mine, other), jnp.where(c == 0, other, mine)], axis=0
    ).astype(F32)


def quarter_of(w, x, c):
    half_rows, half_cols = w.shape[0] // 2, w.shape[1] // 2
    side = jnp.where(x == 0, w[:, :half_cols], w[:, half_cols:])
    return jnp.where(c == 0, side[:half_rows], side[half_rows:]).astype(BF)


def order_matrix(x, c, z, y):
    rel = jnp.arange(32, dtype=jnp.int32)
    other, a, b, rz = rel // 16, rel // 8 % 2, rel // 4 % 2, rel % 4
    cc = c ^ other
    y_rel = jnp.where(cc == 0, a, b)
    x_rel = jnp.where(cc == 0, b, a)
    place = (((z ^ rz) * 2 + (y ^ y_rel)) * 2 + cc) * 2 + (x ^ x_rel)
    return (place[:, None] == rel[None, :]).astype(F32)


def line_tables(heights):
    place = []
    for shard in range(8):
        at = 0
        for height in heights:
            place += [at + shard * height + k for k in range(height)]
            at += 8 * height
    place = np.array(place).reshape(32, -1)
    count = place.size // 8
    row = np.zeros((place.shape[1], 32, 16), np.float32)
    lane = np.zeros((place.shape[1], 32, 8), np.float32)
    for piece in range(32):
        for k in range(place.shape[1]):
            row[k, piece, place[piece, k] // 8] = 1.0
            lane[k, piece, place[piece, k] % 8] = 1.0
    assert count <= 16
    return jnp.asarray(row), jnp.asarray(lane)


def pack_kernel(order, rows_of, lanes_of, attn_ref, first_ref, bias_ref, two_ref, keep_ref, send_ref, vecs):
    d = vecs.shape[1]
    width = d // 8
    vecs[...] = jnp.zeros_like(vecs)
    vecs[0:2, :] = attn_ref[0:2, :]
    vecs[2:3, :] = first_ref[2:3, :]
    vecs[3:5, :] = first_ref[0:2, :]
    for k in range(4):
        vecs[5 + k : 6 + k, :] = bias_ref[:, k * d : (k + 1) * d]
    vecs[9:10, :] = two_ref[2:3, :]
    vecs[10:12, :] = two_ref[0:2, :]
    parts = []
    for k in range(rows_of.shape[0]):
        chosen = jnp.dot(
            rows_of[k], vecs[...], preferred_element_type=F32, precision=lax.Precision.HIGHEST
        )
        part = jnp.zeros((32, width), F32)
        for m in range(8):
            part = part + chosen[:, m * width : (m + 1) * width] * lanes_of[k, :, m : m + 1]
        parts.append(part)
    parts.append(jnp.zeros((32, keep_ref.shape[1] - len(parts) * width), F32))
    packed = jnp.concatenate(parts, axis=1)
    packed = jnp.dot(
        order[...], packed, preferred_element_type=F32, precision=lax.Precision.HIGHEST
    )
    keep_ref[...] = packed[:16]
    send_ref[...] = packed[16:].astype(BF)


def pack_small(order, tables, attn, first, bias, two):
    d = attn.shape[1]
    return kernel_call(
        pack_kernel,
        [],
        [WHOLE] * 7,
        [order, *tables, attn, first, bias, two],
        out_specs=[WHOLE] * 2,
        out_shape=[
            jax.ShapeDtypeStruct((16, d // 2), F32),
            jax.ShapeDtypeStruct((16, d // 2), BF),
        ],
        scratch_shapes=[pltpu.VMEM((16, d), F32)],
        name="pack_small",
    )


def per_device(
    tokens,
    word_counts,
    region_counts,
    qkv_weight,
    qkv_bias,
    out_weight,
    out_bias,
    attn_gain,
    attn_shift,
    up_weight,
    up_bias,
    down_weight,
    down_bias,
    ffn_gain,
    ffn_shift,
    cotangent,
):
    pairs, seq, d = tokens.shape
    n = pairs * seq
    shard_count, rep_count = lax.axis_size("shard"), lax.axis_size("rep")
    fast = shard_count == 8 and rep_count == 4
    rep, shard = lax.axis_index("rep"), lax.axis_index("shard")
    x, c, z, y = rep // 2, rep % 2, shard // 2, shard % 2
    meta = jnp.stack([x, c, z, y]).astype(jnp.int32)
    vectors = (qkv_bias, out_bias, attn_gain, attn_shift, up_bias, down_bias, ffn_gain, ffn_shift)
    small_own = jnp.concatenate(vectors)
    sizes = [v.shape[0] for v in vectors]

    flat = tokens.reshape(n, d)
    if fast:
        quarter = small_own.shape[0] // 4
        own_small = jnp.where(
            x == 0,
            jnp.where(c == 0, small_own[:quarter], small_own[2 * quarter : 3 * quarter]),
            jnp.where(c == 0, small_own[quarter : 2 * quarter], small_own[3 * quarter :]),
        )
        own_small = jnp.pad(own_small.astype(BF)[None, :], ((0, 15), (0, d // 2 - quarter)))
        own_one = jnp.concatenate(
            [quarter_of(qkv_weight, x, c), quarter_of(out_weight, x, c), own_small], axis=0
        )
        up_pieces = [lax.all_gather(quarter_of(up_weight, x, c), AXES, axis=0)]
        along_one = start_gather(own_one)
        eight_one = first_cross(along_one)
        more_one = to_cross(eight_one, 1)
        along_two = start_gather(after(quarter_of(down_weight, x, c), eight_one))
        other_one = to_core(eight_one)
        along_two, more_one, other_one = after((along_two, more_one, other_one))
        last_one = to_core(more_one)
        qkv_pieces = [eight_one, more_one, other_one, last_one]
        order = order_matrix(x, c, z, y)
        row = d // 4
        tables = line_tables([v // (d // 8) for v in sizes])
        rel_small = jnp.concatenate([p[:, row, :quarter] for p in qkv_pieces]).astype(F32)
        whole_small = lax.dot_general(
            order, rel_small, (((0,), (0,)), ((), ())), precision=lax.Precision.HIGHEST
        ).reshape(8, -1)
        cross_two = to_cross(along_two, 0)
        first_deps = [along_two]
    else:
        qkv_pieces = [
            lax.all_gather(w.astype(BF), "shard", axis=0, tiled=True)
            for w in (qkv_weight, out_weight)
        ]
        whole_small = lax.all_gather(small_own.astype(BF), "shard", axis=0).astype(F32)
        first_deps = []
    parts, at = [], 0
    for size in sizes:
        parts.append(whole_small[:, at : at + size].reshape(1, -1))
        at += size
    bqv, bo, g1, c1, bu, bd, g2, c2 = parts

    vec_one = jnp.concatenate([bqv, bo, g1, c1], axis=1)
    vec_two = jnp.concatenate([g1, c1, bd, g2, c2], axis=1)
    joined, probs, mix, low, xhat, rstd, wqkv, wo = attention_forward(
        fast, meta, word_counts, region_counts, flat, vec_one, qkv_pieces, seq, first_deps
    )
    if fast:
        cross_two = after(cross_two, rstd)
        eight_two = jnp.concatenate([along_two, cross_two])
        more_two = to_cross(eight_two, 1)
        up_deps = [eight_two, vec_two]
    else:
        up_pieces = [lax.all_gather(up_weight.astype(BF), "shard", axis=0, tiled=True)]
        up_deps = []
    act, slope, token = up_forward(fast, meta, low, bu, up_pieces, up_deps)
    if fast:
        more_two = after(more_two, token)
        down_pieces = [eight_two, more_two, to_core(after(eight_two, token)), to_core(more_two)]
    else:
        down_pieces = [lax.all_gather(down_weight.astype(BF), "shard", axis=0, tiled=True)]
    layer_out, second, hidden, sums_two, grad_bu, *down_grads = down_forward(
        fast, meta, word_counts, region_counts, act, slope, xhat, vec_two,
        cotangent.reshape(n, d), down_pieces, seq,
    )
    deps = []
    if fast:
        down_sum = Scatter(*down_grads)
        deps = [down_sum.add_core()]
        down_sum.cross(1)
    up_out = up_grad(fast, meta, hidden, low, up_pieces[0], [second, xhat, rstd, wo], deps)
    up_grads, (token, hidden, wu, second, xhat, rstd, wo) = up_out[:-7], up_out[-7:]
    deps = [token]
    if fast:
        deps = [down_sum.add_cross([token])]
        up_sum = Scatter(up_grads[0], after(up_grads[1], deps[0]))
        down_sum.cross(0)
    attn_sum, attn_low, grad_mix, sums_first = first_back(
        second, hidden, wu, xhat, rstd, wo, g1, deps
    )
    if fast:
        deps = [down_sum.add_last([sums_first]), up_sum.add_core([sums_first])]
        down_sum.along()
        up_sum.cross(1)
    grad_joined, sums_attn = attention_back(grad_mix, joined, probs, seq, deps)
    grad_vectors = [
        jnp.concatenate([sums_attn[0:1], sums_attn[1:2]], axis=1),
        sums_first[2:3],
        sums_first[0:1],
        sums_first[1:2],
        grad_bu,
        sums_two[2:3],
        sums_two[0:1],
        sums_two[1:2],
    ]
    deps = []
    if fast:
        small, small_low = pack_small(order, tables, sums_attn, sums_first, grad_bu, sums_two)
        deps = [up_sum.add_cross([sums_attn]), small_low] + down_sum.got
        up_sum.cross(0)
        small_got = to_core(small_low)
    qkv_out = qkv_grad(fast, meta, grad_joined, flat, attn_low, mix, deps)
    qkv_grads, token = qkv_out[:2], qkv_out[2]
    if fast:
        small_got, up_sum.got = after((small_got, up_sum.got), token)
        qkv_sum = Scatter(qkv_grads[0], after(qkv_grads[1], small_got, up_sum.got))
        up_sum.add_last()
        up_sum.along()
        small = small + small_got.astype(F32)
        token = qkv_sum.add_core([up_sum.token], small=small)
        qkv_sum.cross(1)
        down_total = down_sum.total([token])
        down_across = to_x(down_total)
        tokens_grad, token = tokens_back(attn_sum, grad_joined, wqkv, [token, down_total])
        token = qkv_sum.add_cross([token, down_across] + up_sum.got)
        qkv_sum.cross(0)
        up_total = up_sum.total([token])
        up_across = to_x(up_total)
        token = qkv_sum.add_last([up_across])
        qkv_sum.along()
        down_mine = side_by_side(in_columns(down_total), in_columns(down_across), x)
        up_mine = side_by_side(up_total, up_across, x)
        down_other, up_other = to_core(down_mine), to_core(up_mine)
        grad_down = owner_block(down_mine, down_other, c, 0, down_mine.shape[0])
        grad_up = owner_block(up_mine, up_other, c, 0, up_mine.shape[0])
        grad_up, grad_down, qkv_sum.got = after((grad_up, grad_down, qkv_sum.got))
        qkv_total = qkv_sum.total()
        qkv_mine = side_by_side(qkv_total, to_x(qkv_total), x)
        qkv_other = to_core(qkv_mine)
        grad_qkv, grad_out, small_all = finish(meta, qkv_mine, qkv_other, d)
        small_total = small_all[:, :quarter].reshape(-1)
    else:
        tokens_grad, _ = tokens_back(attn_sum, grad_joined, wqkv)

        def total(v):
            part = lax.psum_scatter(v.astype(F32), "shard", scatter_dimension=0, tiled=True)
            return lax.psum(part, "rep")

        grad_down, grad_up = total(down_grads[0]), total(up_grads[0])
        grad_qkv, grad_out = total(qkv_grads[0]), total(qkv_grads[1])
        small_total = lax.dynamic_index_in_dim(
            jnp.concatenate(
                [lax.psum(g, AXES).reshape(shard_count, -1) for g in grad_vectors], axis=1
            ),
            shard,
            axis=0,
            keepdims=False,
        )
    vector_grads, at = [], 0
    for size in sizes:
        vector_grads.append(small_total[at : at + size])
        at += size
    g_qv, g_bo, g_g1, g_c1, g_bu, g_bd, g_g2, g_c2 = vector_grads
    return (
        layer_out.reshape(tokens.shape),
        tokens_grad.reshape(tokens.shape),
        grad_qkv,
        g_qv,
        grad_out,
        g_bo,
        g_g1,
        g_c1,
        grad_up,
        g_bu,
        grad_down,
        g_bd,
        g_g2,
        g_c2,
    )


def solution(mesh):
    matrix, vector = P("shard", None), P("shard")
    batch, counts = P(AXES, None, None), P(AXES)
    weights = (
        matrix, vector, matrix, vector, vector, vector,
        matrix, vector, matrix, vector, vector, vector,
    )
    return jax.shard_map(
        per_device,
        mesh=mesh,
        in_specs=(batch, counts, counts) + weights + (batch,),
        out_specs=(batch, batch) + weights,
        check_vma=False,
    )
```

```python
import functools

import jax
import jax.numpy as jnp
import numpy as np
from jax import lax
from jax.experimental import pallas as pl
from jax.experimental.pallas import tpu as pltpu
from jax.sharding import PartitionSpec as P

HEADS = 12
WORDS_MAX = 28
EPS = 1e-05
BF = jnp.bfloat16
F32 = jnp.float32
ANY = pl.BlockSpec(memory_space=pl.ANY)
SMEM = pl.BlockSpec(memory_space=pltpu.SMEM)
HBM, VMEM = pltpu.HBM, pltpu.VMEM
TOKEN = jax.ShapeDtypeStruct((8, 128), F32)
WHOLE = pl.BlockSpec(memory_space=pltpu.VMEM)
SQRT_HALF = 0.7071067811865476
INV_SQRT_2PI = 0.3989422804014327


def nt(a, b):
    return lax.dot_general(a, b, (((1,), (1,)), ((), ())), preferred_element_type=F32)


def nn(a, b):
    return jnp.dot(a, b, preferred_element_type=F32)


def tn(a, b):
    return lax.dot_general(a, b, (((0,), (0,)), ((), ())), preferred_element_type=F32)


def fixed(shape):
    return pl.BlockSpec(shape, lambda i: (0,) * len(shape))


def rows(shape):
    return pl.BlockSpec(shape, lambda i: (i,) + (0,) * (len(shape) - 1))


def far(value):
    return pltpu.with_memory_space_constraint(value, HBM)


def near(value):
    return pltpu.with_memory_space_constraint(value, VMEM)


def kernel_call(body, deps, in_specs, args, mebibytes=8, **options):
    count, extra = len(args), len(deps)

    def inner(*refs):
        body(*refs[:count], *refs[count + extra :])

    call = pl.pallas_call(
        inner, in_specs=list(in_specs) + [ANY] * extra, compiler_params=params(mebibytes), **options
    )
    return call(*args, *deps)


def params(mebibytes):
    return pltpu.CompilerParams(vmem_limit_bytes=mebibytes * 1024 * 1024)


def piece_place(meta, cc, a, b, rz, local_rows, start, height, width):
    x0, z0, y0 = meta[0], meta[2], meta[3]
    y_rel = jnp.where(cc == 0, a, b)
    x_rel = jnp.where(cc == 0, b, a)
    shard = (z0 ^ rz) * 2 + (y0 ^ y_rel)
    row = shard * local_rows + cc * height + start
    col = (x0 ^ x_rel) * width
    return pl.multiple_of(row, 16), pl.multiple_of(col, 128)


def piece_copies(meta, pieces, whole, sems, local_rows, first, height, width):
    copies = []
    for number, ref in enumerate(pieces):
        cc = meta[1] if number < 2 else 1 - meta[1]
        a = number % 2
        for b in range(2):
            for rz in range(4):
                row, col = piece_place(meta, cc, a, b, rz, local_rows, 0, height, width)
                copies.append(
                    pltpu.make_async_copy(
                        ref.at[b * 4 + rz, pl.ds(first, height), :],
                        whole.at[pl.ds(row, height), pl.ds(col, width)],
                        sems.at[len(copies)],
                    )
                )
    return copies


def tile_waits(whole, outs, sems, count, first, height, span):
    return [
        pltpu.make_async_copy(
            whole.at[pl.ds(0, height), pl.ds(0, span)],
            ref.at[0, pl.ds(first, height), pl.ds(0, span)],
            sems.at[number * count + i],
        )
        for number, ref in enumerate(outs[1:])
        for i in range(count)
    ]


def load_copies(fast, meta, refs, whole, sems, first):
    if not fast:
        return [pltpu.make_async_copy(refs[0], whole, sems.at[0])]
    local_rows, cols = whole.shape[0] // 8, whole.shape[1]
    if len(refs) == 1:
        height, width = local_rows // 2, cols // 2
        return [
            pltpu.make_async_copy(
                refs[0].at[(x * 2 + c) * 8 + shard],
                whole.at[
                    pl.ds(shard * local_rows + c * height, height), pl.ds(x * width, width)
                ],
                sems.at[(x * 2 + c) * 8 + shard],
            )
            for x in range(2)
            for c in range(2)
            for shard in range(8)
        ]
    return piece_copies(meta, refs, whole, sems, local_rows, first, local_rows // 2, cols // 2)


def go(copies):
    for copy in copies:
        copy.start()


def done(copies):
    for copy in copies:
        copy.wait()


def key_mask(words, regions, shape, axis):
    place = lax.broadcasted_iota(jnp.int32, shape, axis)
    return (place < words) | ((place >= WORDS_MAX) & (place < WORDS_MAX + regions))


def split_heads(block):
    low = lax.broadcasted_iota(jnp.int32, block.shape, 1) < 64
    zero = jnp.zeros_like(block)
    return jnp.concatenate([jnp.where(low, block, zero), jnp.where(low, zero, block)], axis=0)


def turn_heads(block):
    n = block.shape[0]
    return jnp.concatenate([block[:, :n].T, block[:, n:].T], axis=1)


def norm_parts(value):
    center = value - jnp.mean(value, axis=-1, keepdims=True)
    rstd = lax.rsqrt(jnp.mean(center * center, axis=-1, keepdims=True) + EPS)
    return center * rstd, rstd


def norm_back(grad, xhat, rstd, gain):
    scaled = grad * gain
    mean_one = jnp.mean(scaled, axis=-1, keepdims=True)
    mean_two = jnp.mean(scaled * xhat, axis=-1, keepdims=True)
    return rstd * (scaled - mean_one - xhat * mean_two)


def attention_kernel(fast, n_in, *refs):
    meta, words, regions = refs[:3]
    x_ref, vec_ref = refs[3:5]
    pieces = refs[5 : 5 + n_in]
    (joined_ref, probs_ref, mix_ref, low_ref, xhat_ref, rstd_ref, wqkv_out, wo_out) = refs[
        5 + n_in : 13 + n_in
    ]
    wqkv, wo, sem_a, sem_b, sem_c = refs[13 + n_in :]
    step = pl.program_id(0)
    d = x_ref.shape[1]
    seq = probs_ref.shape[2]

    @pl.when(step == 0)
    def _():
        if fast:
            first = load_copies(fast, meta, pieces, wqkv, sem_a, 0)
            second = load_copies(fast, meta, pieces, wo, sem_b, wqkv.shape[0] // 16)
        else:
            first = load_copies(fast, meta, pieces[:1], wqkv, sem_a, 0)
            second = load_copies(fast, meta, pieces[1:], wo, sem_b, 0)
        go(first)
        go(second)
        done(first)
        done(second)

    saves = [
        pltpu.make_async_copy(wqkv, wqkv_out, sem_c.at[0]),
        pltpu.make_async_copy(wo, wo_out, sem_c.at[1]),
    ]

    @pl.when(step == 0)
    def _():
        go(saves)

    x = x_ref[...]
    bq = vec_ref[:, :d]
    bv = vec_ref[:, d : 2 * d]
    joined_ref[:, :d] = (nt(x, wqkv[:d, :]) + bq).astype(BF) * BF(0.125)
    joined_ref[:, d : 2 * d] = nt(x, wqkv[d : 2 * d, :]).astype(BF)
    joined_ref[:, 2 * d :] = (nt(x, wqkv[2 * d :, :]) + bv).astype(BF)
    per_step = x_ref.shape[0] // seq
    for p in range(per_step):
        pair = step * per_step + p
        valid = key_mask(words[pair], regions[pair], (seq, 2 * seq), 0)
        here = pl.ds(p * seq, seq)
        for h in range(d // 128):
            cols = pl.ds(h * 128, 128)
            queries = split_heads(joined_ref[here, pl.ds(h * 128, 128)])
            keys = joined_ref[here, pl.ds(d + h * 128, 128)]
            values = split_heads(joined_ref[here, pl.ds(2 * d + h * 128, 128)])
            scores = jnp.where(valid, nt(keys, queries), -1000000000.0)
            exponent = jnp.exp(scores - jnp.max(scores, axis=0, keepdims=True))
            probs = exponent * (1.0 / jnp.sum(exponent, axis=0, keepdims=True))
            probs = probs.astype(BF)
            probs_ref[p, h] = probs
            mix_ref[here, cols] = nn(turn_heads(probs), values).astype(BF)
    first_sum = x.astype(F32) + nt(mix_ref[...], wo[...]) + vec_ref[:, 2 * d : 3 * d]
    xhat, rstd = norm_parts(first_sum)
    xhat_ref[...] = xhat
    rstd_ref[...] = jnp.broadcast_to(rstd, rstd_ref.shape)
    low_ref[...] = (xhat * vec_ref[:, 3 * d : 4 * d] + vec_ref[:, 4 * d : 5 * d]).astype(BF)

    @pl.when(step == pl.num_programs(0) - 1)
    def _():
        done(saves)


def attention_forward(fast, meta, words, regions, x, vec, pieces, seq, deps=()):
    n, d = x.shape
    tile = 2 * seq
    shapes = [
        HBM((n, 3 * d), BF),
        HBM((n // seq, d // 128, seq, 2 * seq), BF),
        HBM((n, d), BF),
        HBM((n, d), BF),
        HBM((n, d), F32),
        HBM((n, 128), F32),
        HBM((3 * d, d), BF),
        HBM((d, d), BF),
    ]
    return kernel_call(
        functools.partial(attention_kernel, fast, len(pieces)),
        deps,
        [SMEM] * 3 + [rows((tile, d)), fixed(vec.shape)] + [ANY] * len(pieces),
        [meta, words, regions, far(x), vec, *map(far, pieces)],
        grid=(n // tile,),
        out_specs=[
            rows((tile, 3 * d)),
            rows((2, d // 128, seq, 2 * seq)),
            rows((tile, d)),
            rows((tile, d)),
            rows((tile, d)),
            rows((tile, 128)),
            ANY,
            ANY,
        ],
        out_shape=shapes,
        scratch_shapes=[
            pltpu.VMEM((3 * d, d), BF),
            pltpu.VMEM((d, d), BF),
            pltpu.SemaphoreType.DMA((32,)),
            pltpu.SemaphoreType.DMA((32,)),
            pltpu.SemaphoreType.DMA((2,)),
        ],
        cost_estimate=pl.CostEstimate(
            flops=2 * n * d * 4 * d, bytes_accessed=16 * n * d, transcendentals=0
        ),
        mebibytes=17,
        name="attention_forward",
    )


def up_kernel(fast, n_in, *refs):
    meta, low_far, bias_ref = refs[:3]
    pieces = refs[3 : 3 + n_in]
    act_ref, slope_ref, token_ref, low_ref, w, sem_a, sem_b = refs[3 + n_in :]
    token_ref[...] = jnp.zeros_like(token_ref)
    n = low_ref.shape[0]
    tile, width = 256, w.shape[0] // 4
    reads = [pltpu.make_async_copy(low_far, low_ref, sem_b.at[0])]
    go(reads)
    loads = load_copies(fast, meta, pieces, w, sem_a, 0)
    parts = [loads] + [[]] * 3
    if len(loads) == 32:
        parts = [[v for k, v in enumerate(loads) if k % 8 // 2 == j] for j in range(4)]
    for part in parts:
        go(part)
    done(reads)
    for j in range(4):
        done(parts[j])
        here = slice(j * width, (j + 1) * width)
        for i in range(n // tile):
            part = slice(i * tile, (i + 1) * tile)
            hidden = nt(low_ref[part, :], w[here, :]) + bias_ref[:, here]
            phi = 0.5 + 0.5 * lax.erf(hidden * SQRT_HALF)
            act_ref[part, here] = (hidden * phi).astype(BF)
            bell = jnp.exp(hidden * hidden * -0.5) * INV_SQRT_2PI
            slope_ref[part, here] = (phi + hidden * bell).astype(BF)


def up_forward(fast, meta, low, bias, pieces, deps=()):
    n, d = low.shape
    ff = bias.shape[1]
    return kernel_call(
        functools.partial(up_kernel, fast, len(pieces)),
        deps,
        [SMEM, ANY, WHOLE] + [ANY] * len(pieces),
        [meta, far(low), bias, *map(far, pieces)],
        out_specs=[WHOLE] * 3,
        out_shape=[VMEM((n, ff), BF), VMEM((n, ff), BF), TOKEN],
        scratch_shapes=[
            pltpu.VMEM((n, d), BF),
            pltpu.VMEM((ff, d), BF),
            pltpu.SemaphoreType.DMA((32,)),
            pltpu.SemaphoreType.DMA((1,)),
        ],
        cost_estimate=pl.CostEstimate(
            flops=4 * n * d * ff, bytes_accessed=4 * n * ff, transcendentals=0
        ),
        mebibytes=14,
        name="up_forward",
    )


def down_kernel(fast, n_in, seq, *refs):
    meta, words, regions = refs[:3]
    act_ref, slope_ref, xhat_far, vec_ref, cot_far = refs[3:8]
    pieces = refs[8 : 8 + n_in]
    outs_end = 14 + n_in + (2 if fast else 1)
    out_far, second_far, feed_ref, sums_ref, w, _ = refs[8 + n_in : 14 + n_in]
    grads = refs[14 + n_in : outs_end]
    xhat_ref, cot_ref, out_ref, second_ref, whole = refs[outs_end:-3]
    sem_a, sem_b, sem_c = refs[-3:]
    n, d = feed_ref.shape
    ff = act_ref.shape[1]
    tile = 256
    count = n // tile
    loads = load_copies(fast, meta, pieces, w, sem_a, 0)
    go(loads)
    reads, writes = [], []
    for i in range(count):
        part = pl.ds(i * tile, tile)
        reads.append(
            [
                pltpu.make_async_copy(xhat_far.at[part], xhat_ref.at[part], sem_b.at[0, i]),
                pltpu.make_async_copy(cot_far.at[part], cot_ref.at[part], sem_b.at[1, i]),
            ]
        )
        writes += [
            pltpu.make_async_copy(out_ref.at[part], out_far.at[part], sem_b.at[2, i]),
            pltpu.make_async_copy(second_ref.at[part], second_far.at[part], sem_b.at[3, i]),
        ]
    for pair in reads:
        go(pair)
    gain_one, shift_one = vec_ref[:, :d], vec_ref[:, d : 2 * d]
    bias, gain, shift = vec_ref[:, 2 * d : 3 * d], vec_ref[:, 3 * d : 4 * d], vec_ref[:, 4 * d :]
    done(loads)
    sums = [jnp.zeros((1, d), F32)] * 3
    product = nt(act_ref[:tile, :], w[...])
    for i in range(count):
        part = slice(i * tile, (i + 1) * tile)
        done(reads[i])
        if i:
            go(writes[2 * i - 2 : 2 * i])
        this = product
        if i + 1 < count:
            product = nt(act_ref[(i + 1) * tile : (i + 2) * tile, :], w[...])
        second_sum = xhat_ref[part, :] * gain_one + shift_one + this + bias
        xhat, rstd = norm_parts(second_sum)
        first = i * (tile // seq)
        keep = jnp.concatenate(
            [
                key_mask(words[first + p], regions[first + p], (seq, 128), 0)
                for p in range(tile // seq)
            ],
            axis=0,
        )[:, :1]
        out_ref[part, :] = jnp.where(keep, xhat * gain + shift, 0.0).astype(BF)
        grad = jnp.where(keep, cot_ref[part, :].astype(F32), 0.0)
        second = norm_back(grad, xhat, rstd, gain)
        second_ref[part, :] = second
        feed = second.astype(BF)
        feed_ref[part, :] = feed
        for k, value in enumerate((grad * xhat, grad, feed.astype(F32))):
            sums[k] = sums[k] + jnp.sum(value, axis=0, keepdims=True)
    go(writes[-2:])
    for k in range(3):
        sums_ref[k : k + 1, :] = sums[k]
    waits = []
    width, span = ff // 4, ff // 8
    for i in range(4):
        here = slice(i * width, (i + 1) * width)
        whole[:, here] = tn(feed_ref[...], act_ref[:, here]).astype(BF)
        if fast:
            for k in range(2):
                chunk = (i % 2) * 2 + k
                copies = tile_copies(
                    meta, whole, grads, sem_c.at[2 * i + k], range(8), [i // 2], d // 8,
                    chunk * (d // 16), d // 16, ff // 2, (chunk * span, span),
                )
                go(copies)
                waits += tile_waits(
                    whole, grads, sem_c.at[2 * i + k], 8, chunk * (d // 16), d // 16, span
                )
    if not fast:
        waits = [pltpu.make_async_copy(whole, grads[0], sem_c.at[0, 0])]
        go(waits)
    done(waits)
    done(writes)


def down_forward(
    fast, meta, words, regions, act, slope, xhat, vec, cot, pieces, seq, deps=()
):
    n, ff = act.shape
    d = xhat.shape[1]
    shapes = grad_shapes(fast, d, ff)
    return kernel_call(
        functools.partial(down_kernel, fast, len(pieces), seq),
        deps,
        [SMEM] * 3 + [WHOLE, WHOLE, ANY, WHOLE, ANY] + [ANY] * len(pieces),
        [meta, words, regions, near(act), near(slope), far(xhat), vec, far(cot), *map(far, pieces[:-1]), *pieces[-1:]],
        out_specs=[ANY, ANY, WHOLE, WHOLE, WHOLE, WHOLE] + [WHOLE, ANY][-len(shapes) :],
        out_shape=[
            HBM((n, d), BF),
            HBM((n, d), F32),
            VMEM((n, d), BF),
            jax.ShapeDtypeStruct((8, d), F32),
            VMEM((d, ff), BF),
            VMEM((n, ff), BF),
        ]
        + shapes,
        scratch_shapes=[
            pltpu.VMEM((n, d), F32),
            pltpu.VMEM((n, d), BF),
            pltpu.VMEM((n, d), BF),
            pltpu.VMEM((n, d), F32),
            pltpu.VMEM((d, ff), BF),
            pltpu.SemaphoreType.DMA((32,)),
            pltpu.SemaphoreType.DMA((4, n // 256)),
            pltpu.SemaphoreType.DMA((8, 16)),
        ],
        cost_estimate=pl.CostEstimate(
            flops=12 * n * d * ff, bytes_accessed=2 * n * ff, transcendentals=0
        ),
        input_output_aliases={4: 5},
        mebibytes=24,
        name="down_forward",
    )


def hidden_grad_kernel(feed_ref, slope_ref, w, hidden_ref, bias_ref):
    width = 512
    for i in range(slope_ref.shape[1] // width):
        here = slice(i * width, (i + 1) * width)
        hidden = nn(feed_ref[...], w[:, here]) * slope_ref[:, here].astype(F32)
        hidden = hidden.astype(BF)
        hidden_ref[:, here] = hidden
        bias_ref[:, here] = jnp.sum(hidden.astype(F32), axis=0, keepdims=True)


def hidden_grad(feed, slope, w, deps=()):
    n, ff = slope.shape
    d = feed.shape[1]
    return kernel_call(
        hidden_grad_kernel,
        deps,
        [WHOLE] * 3,
        [near(feed), near(slope), near(w)],
        out_specs=[WHOLE] * 2,
        out_shape=[VMEM((n, ff), BF), jax.ShapeDtypeStruct((1, ff), F32)],
        cost_estimate=pl.CostEstimate(
            flops=4 * n * d * ff, bytes_accessed=4 * n * ff, transcendentals=0
        ),
        mebibytes=10,
        name="hidden_grad",
    )


def grad_shapes(fast, total_rows, cols):
    if fast:
        width = min(total_rows, cols) // 2
        shape = (16, total_rows * cols // (32 * width), width)
        return [VMEM(shape, BF), HBM(shape, BF)]
    return [HBM((total_rows, cols), BF)]


def tile_copies(meta, whole, outs, sems, shards, sides, local_rows, first, height, width, cols=None):
    x0, c0, z0, y0 = meta[0], meta[1], meta[2], meta[3]
    offset, span = (0, width) if cols is None else cols
    there = pl.ds(0, span)
    copies = []
    for number, ref in enumerate(outs):
        cc = c0 ^ number
        for shard in shards:
            for side in sides:
                y_rel, x_rel = y0 ^ (shard % 2), x0 ^ side
                a = jnp.where(cc == 0, y_rel, x_rel)
                b = jnp.where(cc == 0, x_rel, y_rel)
                row = pl.multiple_of(shard * local_rows + cc * height, 16)
                col = pl.multiple_of(side * width + offset, 128)
                place = a * 8 + b * 4 + (z0 ^ (shard // 2))
                if number == 0:
                    static = pl.ds(side * width + offset, span)
                    ref[place, pl.ds(first, height), there] = whole[pl.ds(row, height), static]
                    continue
                copies.append(
                    pltpu.make_async_copy(
                        whole.at[pl.ds(row, height), pl.ds(col, span)],
                        ref.at[place, pl.ds(first, height), there],
                        sems.at[len(copies)],
                    )
                )
    return copies


def up_grad_kernel(fast, *refs):
    meta, hidden_ref, low_far, wu_far, *others_far = refs[:8]
    outs = refs[8 : (10 if fast else 9)]
    token_ref, _, wu_ref, *others = refs[10 if fast else 9 : -5]
    low_ref, whole, sems, sem_b, sem_c = refs[-5:]
    reads = [pltpu.make_async_copy(low_far, low_ref, sem_b.at[0])]
    go(reads)
    ahead = load_copies(fast, meta, [wu_far], wu_ref, sem_c, 0)
    for i, (source, target) in enumerate(zip(others_far, others)):
        ahead.append(pltpu.make_async_copy(source, target, sem_b.at[1 + i]))
    go(ahead)
    token_ref[...] = jnp.zeros_like(token_ref)
    done(reads)
    ff, d = whole.shape
    height = ff // 4
    waits = []
    for i in range(4):
        here = slice(i * height, (i + 1) * height)
        whole[here, :] = tn(hidden_ref[:, here], low_ref[...]).astype(BF)
        if fast:
            copies = tile_copies(
                meta, whole, outs, sems.at[i], [2 * i, 2 * i + 1], [0, 1], ff // 8, 0, ff // 16,
                d // 2,
            )
            go(copies)
            waits += tile_waits(whole, outs, sems.at[i], 4, 0, ff // 16, d // 2)
    if not fast:
        waits = [pltpu.make_async_copy(whole, outs[0], sems.at[0, 0])]
        go(waits)
    done(waits + ahead)


def up_grad(fast, meta, hidden, low, wu, others, deps=()):
    n, d = low.shape
    ff = hidden.shape[1]
    shapes = grad_shapes(fast, ff, d)
    return kernel_call(
        functools.partial(up_grad_kernel, fast),
        deps,
        [SMEM, WHOLE] + [ANY] * 6,
        [meta, near(hidden), far(low), far(wu), *map(far, others)],
        out_specs=[WHOLE, ANY][-len(shapes) :] + [WHOLE] * 7,
        out_shape=shapes
        + [TOKEN, VMEM((n, ff), BF), VMEM((ff, d), BF)]
        + [VMEM(v.shape, v.dtype) for v in others],
        scratch_shapes=[
            pltpu.VMEM((n, d), BF),
            pltpu.VMEM((ff, d), BF),
            pltpu.SemaphoreType.DMA((4, 8)),
            pltpu.SemaphoreType.DMA((5,)),
            pltpu.SemaphoreType.DMA((32,)),
        ],
        input_output_aliases={1: len(shapes) + 1},
        cost_estimate=pl.CostEstimate(
            flops=4 * n * d * ff, bytes_accessed=2 * n * ff, transcendentals=0
        ),
        mebibytes=12,
        name="up_grad",
    )


def first_back_kernel(*refs):
    second_ref, hidden_ref, wu_ref, xhat_ref, rstd_ref, wo_ref, gain_ref = refs[:7]
    sum_far, low_far, mix_ref, sums_ref, sum_ref, low_ref, sem = refs[7:]
    n, d = low_ref.shape
    tile = 256
    count = n // tile
    writes = []
    for i in range(count):
        part = pl.ds(i * tile, tile)
        writes.append(
            [
                pltpu.make_async_copy(sum_ref.at[part], sum_far.at[part], sem.at[0, i]),
                pltpu.make_async_copy(low_ref.at[part], low_far.at[part], sem.at[1, i]),
            ]
        )
    product = nn(hidden_ref[:tile, :], wu_ref[...])
    sums = [jnp.zeros((1, d), F32)] * 3
    for i in range(count):
        part = slice(i * tile, (i + 1) * tile)
        if i:
            go(writes[i - 1])
        grad = second_ref[part, :] + product
        if i + 1 < count:
            product = nn(hidden_ref[(i + 1) * tile : (i + 2) * tile, :], wu_ref[...])
        xhat = xhat_ref[part, :]
        attn_sum = norm_back(grad, xhat, rstd_ref[part, :1], gain_ref[...])
        sum_ref[part, :] = attn_sum
        low = attn_sum.astype(BF)
        low_ref[part, :] = low
        mix_ref[part, :] = nn(low, wo_ref[...]).astype(BF)
        for k, value in enumerate((grad * xhat, grad, low.astype(F32))):
            sums[k] = sums[k] + jnp.sum(value, axis=0, keepdims=True)
    go(writes[-1])
    for k in range(3):
        sums_ref[k : k + 1, :] = sums[k]
    for group in writes:
        done(group)


def first_back(second, hidden, wu, xhat, rstd, wo, gain, deps=()):
    n, ff = hidden.shape
    d = xhat.shape[1]
    return kernel_call(
        first_back_kernel,
        deps,
        [WHOLE] * 7,
        [near(v) for v in (second, hidden, wu, xhat, rstd, wo)] + [gain],
        out_specs=[ANY, ANY, WHOLE, WHOLE],
        out_shape=[
            HBM((n, d), F32),
            HBM((n, d), BF),
            VMEM((n, d), BF),
            jax.ShapeDtypeStruct((8, d), F32),
        ],
        scratch_shapes=[
            pltpu.VMEM((n, d), F32),
            pltpu.VMEM((n, d), BF),
            pltpu.SemaphoreType.DMA((2, n // 256)),
        ],
        cost_estimate=pl.CostEstimate(
            flops=4 * n * d * ff, bytes_accessed=2 * n * ff, transcendentals=0
        ),
        mebibytes=12,
        name="first_back",
    )


def attention_back_kernel(seq, *refs):
    mix_ref, joined_ref, probs_ref, grad_ref, sums_ref = refs
    d = mix_ref.shape[1]

    @pl.when(pl.program_id(0) == 0)
    def _():
        sums_ref[...] = jnp.zeros_like(sums_ref)

    for p in range(mix_ref.shape[0] // seq):
        here = pl.ds(p * seq, seq)
        for h in range(d // 128):
            one = pl.ds(h * 128, 128)
            two = pl.ds(d + h * 128, 128)
            three = pl.ds(2 * d + h * 128, 128)
            outer = split_heads(mix_ref[here, one])
            probs = probs_ref[p, h]
            grad_probs = nt(joined_ref[here, three], outer)
            wide = probs.astype(F32)
            product = wide * grad_probs
            scores = product - wide * jnp.sum(product, axis=0, keepdims=True)
            scores = scores.astype(BF)
            grad_ref[here, three] = nn(probs, outer).astype(BF)
            grad_ref[here, two] = nn(scores, split_heads(joined_ref[here, one])).astype(BF)
            keys = split_heads(joined_ref[here, two])
            grad_ref[here, one] = (nn(turn_heads(scores), keys) * 0.125).astype(BF)
    sums_ref[0:1, :] += jnp.sum(grad_ref[:, :d].astype(F32), axis=0, keepdims=True)
    sums_ref[1:2, :] += jnp.sum(grad_ref[:, 2 * d :].astype(F32), axis=0, keepdims=True)


def attention_back(mix, joined, probs, seq, deps=()):
    n, d = mix.shape
    tile = 2 * seq
    return kernel_call(
        functools.partial(attention_back_kernel, seq),
        deps,
        [
            rows((tile, d)),
            rows((tile, 3 * d)),
            rows((2, d // 128, seq, 2 * seq)),
        ],
        [near(mix), far(joined), far(probs)],
        grid=(n // tile,),
        out_specs=[rows((tile, 3 * d)), fixed((8, d))],
        out_shape=[
            HBM((n, 3 * d), BF),
            jax.ShapeDtypeStruct((8, d), F32),
        ],
        cost_estimate=pl.CostEstimate(
            flops=16 * n * d * d, bytes_accessed=30 * n * d, transcendentals=0
        ),
        mebibytes=14,
        name="attention_back",
    )


def qkv_grad_kernel(fast, *refs):
    meta, grad_far, x_far, low_far, mix_far = refs[:5]
    outs = refs[5:7]
    token_ref, whole, whole_out, grad_ref, x_ref, low_ref, mix_ref, sem_a, sem_b, sem_c = refs[7:]
    total, d = whole.shape
    width = total // 6
    columns = [pl.ds(i * width, width) for i in range(6)]
    reads = [
        pltpu.make_async_copy(x_far, x_ref, sem_c.at[0]),
        pltpu.make_async_copy(low_far, low_ref, sem_c.at[1]),
        pltpu.make_async_copy(mix_far, mix_ref, sem_c.at[2]),
    ]
    grads = [
        pltpu.make_async_copy(grad_far.at[:, here], grad_ref.at[:, here], sem_c.at[3 + i])
        for i, here in enumerate(columns)
    ]
    go(reads[:1] + grads + reads[1:])
    token_ref[...] = jnp.zeros_like(token_ref)
    waits = []
    done(reads[:1])
    for i in range(2):
        for k in range(3 * i, 3 * i + 3):
            done([grads[k]])
            here = slice(k * width, (k + 1) * width)
            whole[here, :] = tn(grad_ref[:, here], x_ref[...]).astype(BF)
        if fast:
            go(
                tile_copies(
                    meta, whole, outs, sem_a.at[i], range(4 * i, 4 * i + 4), [0, 1], total // 8,
                    0, total // 16, d // 2,
                )
            )
            waits += tile_waits(whole, outs, sem_a.at[i], 8, 0, total // 16, d // 2)
    done(reads[1:])
    whole_out[...] = tn(low_ref[...], mix_ref[...]).astype(BF)
    if fast:
        go(
            tile_copies(
                meta, whole_out, outs, sem_b, range(8), [0, 1], d // 8, total // 16, d // 16,
                d // 2,
            )
        )
        waits += tile_waits(whole_out, outs, sem_b, 16, total // 16, d // 16, d // 2)
    else:
        waits = [
            pltpu.make_async_copy(whole, outs[0], sem_b.at[0]),
            pltpu.make_async_copy(whole_out, outs[1], sem_b.at[1]),
        ]
        go(waits)
    done(waits)


def qkv_grad(fast, meta, grad, x, low, mix, deps=()):
    n, d = x.shape
    if fast:
        shapes = [f((16, 4 * d // 16, d // 2), BF) for f in (VMEM, HBM)]
    else:
        shapes = [jax.ShapeDtypeStruct((3 * d, d), BF), jax.ShapeDtypeStruct((d, d), BF)]
    return kernel_call(
        functools.partial(qkv_grad_kernel, fast),
        deps,
        [SMEM, ANY, ANY, ANY, ANY],
        [meta, far(grad), far(x), far(low), far(mix)],
        out_specs=([WHOLE, ANY] if fast else [ANY] * 2) + [WHOLE],
        out_shape=shapes + [TOKEN],
        scratch_shapes=[
            pltpu.VMEM((3 * d, d), BF),
            pltpu.VMEM((d, d), BF),
            pltpu.VMEM((n, 3 * d), BF),
            pltpu.VMEM((n, d), BF),
            pltpu.VMEM((n, d), BF),
            pltpu.VMEM((n, d), BF),
            pltpu.SemaphoreType.DMA((2, 16)),
            pltpu.SemaphoreType.DMA((32,)),
            pltpu.SemaphoreType.DMA((9,)),
        ],
        cost_estimate=pl.CostEstimate(
            flops=16 * n * d * d, bytes_accessed=16 * n * d, transcendentals=0
        ),
        mebibytes=20,
        name="qkv_grad",
    )


def tokens_grad_kernel(sum_ref, grad_ref, w_ref, out_ref, token_ref):
    token_ref[...] = jnp.zeros_like(token_ref)
    out_ref[...] = sum_ref[...] + nn(grad_ref[...], w_ref[...])


def tokens_back(attn_sum, grad, w, deps=()):
    n, d = attn_sum.shape
    tile = 256
    return kernel_call(
        tokens_grad_kernel,
        deps,
        [rows((tile, d)), rows((tile, 3 * d)), fixed((3 * d, d))],
        [far(attn_sum), far(grad), far(w)],
        grid=(n // tile,),
        out_specs=[rows((tile, d)), fixed((8, 128))],
        out_shape=[HBM((n, d), F32), TOKEN],
        cost_estimate=pl.CostEstimate(
            flops=12 * n * d * d, bytes_accessed=14 * n * d, transcendentals=0
        ),
        mebibytes=14,
        name="tokens_back",
    )


AXES = ("rep", "shard")


def route(fn):
    pairs = []
    for x in range(2):
        for c in range(2):
            for z in range(4):
                for y in range(2):
                    to = fn(x, c, z, y)
                    pairs.append(
                        ((x * 2 + c) * 8 + z * 2 + y, (to[0] * 2 + to[1]) * 8 + to[2] * 2 + to[3])
                    )
    return pairs


def to_core(v):
    return lax.ppermute(v, AXES, route(lambda x, c, z, y: (x, 1 - c, z, y)))


def to_x(v):
    return lax.ppermute(v, AXES, route(lambda x, c, z, y: (1 - x, c, z, y)))


def to_z(v, k):
    return lax.ppermute(v, AXES, route(lambda x, c, z, y: (x, c, z ^ k, y)))


def to_cross(v, first_core):
    return lax.ppermute(
        v,
        AXES,
        route(lambda x, c, z, y: (1 - x, c, z, y) if c == first_core else (x, c, z, 1 - y)),
    )


def after(value, *others):
    return lax.optimization_barrier((value, others))[0]


def start_gather(own):
    return jnp.stack([own] + [to_z(own, k) for k in (1, 2, 3)])


def first_cross(along):
    return jnp.concatenate([along, to_cross(along, 0)])


def add_core_kernel(kept_ref, got_ref, *refs):
    keep_ref, send_ref = refs[-2:]
    count, height, width = keep_ref.shape
    for k in range(count):
        here = slice(k * height, (k + 1) * height)
        keep_ref[k] = (kept_ref[k].astype(F32) + got_ref[k].astype(F32)).astype(BF)
        other = kept_ref[count + k].astype(F32) + got_ref[count + k].astype(F32)
        send_ref[here, :] = other.astype(BF)
    if len(refs) == 3:
        send_ref[count * height :, :] = refs[0][...].astype(BF)


def add_cross_kernel(keep_ref, got_ref, *refs):
    small = len(refs) == 4
    new_ref, send_ref = refs[1:3] if small else refs
    count, height, width = new_ref.shape
    for k in range(2 * count):
        here = slice(k * height, (k + 1) * height)
        total = (keep_ref[k].astype(F32) + got_ref[here, :].astype(F32)).astype(BF)
        if k < count:
            new_ref[k] = total
        else:
            send_ref[(k - count) * height : (k - count + 1) * height, :] = total
    if small:
        rows_in = refs[0][...] + got_ref[2 * count * height :, :].astype(F32)
        refs[3][...] = rows_in
        tail = jnp.concatenate([rows_in[count : 2 * count], rows_in[2 * count :]], axis=0)
        tail = jnp.concatenate([tail, jnp.zeros((count, width), F32)], axis=0)
        send_ref[count * height :, :] = tail.astype(BF)


def add_last_kernel(keep_ref, got_ref, *refs):
    small = len(refs) == 5
    outs = refs[1:] if small else refs
    count, height, width = keep_ref.shape
    if small:
        rows_in = refs[0][...] + got_ref[count * height :, :].astype(F32)
        place = lax.broadcasted_iota(jnp.int32, rows_in.shape, 0)
    for k in range(count):
        here = slice(k * height, (k + 1) * height)
        total = keep_ref[k].astype(F32) + got_ref[here, :].astype(F32)
        outs[k][:height, :] = total.astype(outs[k].dtype)
        if small:
            row = jnp.sum(jnp.where(place == k, rows_in, 0.0), axis=0, keepdims=True)
            outs[k][height:, :] = jnp.broadcast_to(row, (16, width)).astype(outs[k].dtype)


def total_kernel(own_ref, one_ref, two_ref, three_ref, out_ref):
    total = own_ref[...] + one_ref[...].astype(F32)
    total = total + two_ref[...].astype(F32) + three_ref[...].astype(F32)
    out_ref[...] = total.astype(BF)


class Scatter:
    def __init__(self, kept, sent):
        self.kept, self.small = kept, None
        self.got = to_core(sent)

    def call(self, body, out_shape, extra, deps, name):
        args = [near(self.keep), near(self.got)] + list(extra)

        def marked(*refs):
            refs[-1][...] = jnp.zeros_like(refs[-1])
            body(*refs[:-1])

        *out, self.token = kernel_call(
            marked,
            deps,
            [WHOLE] * len(args),
            args,
            out_specs=[WHOLE] * (len(out_shape) + 1),
            out_shape=out_shape + [TOKEN],
            name=name,
        )
        return out

    def add_core(self, deps=(), small=None):
        self.keep = self.kept
        count, height, width = self.kept.shape[0] // 2, *self.kept.shape[1:]
        tail, extra = 0, []
        if small is not None:
            tail, extra = 16, [jnp.concatenate([small[8:], jnp.zeros_like(small[8:])])]
            self.small = jnp.concatenate([small[:8], jnp.zeros_like(small[8:])])
        self.keep, self.send = self.call(
            add_core_kernel,
            [VMEM((count, height, width), BF), VMEM((count * height + tail, width), BF)],
            extra,
            deps,
            "add_core",
        )
        return self.token

    def cross(self, core):
        self.got = to_cross(self.send, core)

    def add_cross(self, deps=()):
        count, height, width = self.keep.shape[0] // 2, *self.keep.shape[1:]
        small = self.small is not None
        outs = [
            VMEM((count, height, width), BF),
            VMEM((count * height + 16 * small, width), BF),
        ]
        if small:
            outs.append(VMEM((16, width), F32))
        out = self.call(
            add_cross_kernel, outs, [self.small] if small else [], deps, "add_cross"
        )
        self.keep, self.send = out[:2]
        if small:
            self.small = out[2]
        return self.token

    def add_last(self, deps=()):
        height, width = self.keep.shape[1:]
        small = self.small is not None
        shape = (height + 16 * small, width)
        self.parts = self.call(
            add_last_kernel,
            [VMEM(shape, F32)] + [VMEM(shape, BF)] * 3,
            [self.small] if small else [],
            deps,
            "add_last",
        )
        return self.token

    def along(self):
        self.got = [to_z(self.parts[k], k) for k in (1, 2, 3)]

    def total(self, deps=()):
        args = [near(v) for v in [self.parts[0]] + self.got]
        return kernel_call(
            total_kernel,
            deps,
            [WHOLE] * 4,
            args,
            out_specs=WHOLE,
            out_shape=jax.ShapeDtypeStruct(self.parts[0].shape, BF),
            name="total",
        )


def finish_kernel(meta, mine_ref, other_ref, qkv_ref, out_ref, small_ref):
    c = meta[1]
    first = 0
    for target in (qkv_ref, out_ref):
        half = target.shape[0] // 2
        part = slice(first, first + half)
        target[pl.ds(pl.multiple_of(c * half, 8), half), :] = mine_ref[part, :].astype(F32)
        target[pl.ds(pl.multiple_of((1 - c) * half, 8), half), :] = other_ref[part, :].astype(F32)
        first += half
    mine = mine_ref[first : first + 16, :].astype(F32)[:1]
    other = other_ref[first : first + 16, :].astype(F32)[:1]
    width = small_ref.shape[1]
    for k, line in enumerate((jnp.where(c == 0, mine, other), jnp.where(c == 0, other, mine))):
        small_ref[2 * k : 2 * k + 1, :] = line[:, :width]
        small_ref[2 * k + 1 : 2 * k + 2, :] = line[:, width:]


def finish(meta, mine, other, d):
    return kernel_call(
        finish_kernel,
        [],
        [SMEM, WHOLE, WHOLE],
        [meta, near(mine), near(other)],
        out_specs=[WHOLE] * 3,
        out_shape=[HBM((3 * d // 8, d), F32), HBM((d // 8, d), F32), VMEM((4, d // 2), F32)],
        name="finish",
    )


def in_columns(piece):
    return jnp.concatenate(jnp.split(piece, 4, axis=0), axis=1)


def side_by_side(low, across, x):
    return jnp.concatenate(
        [jnp.where(x == 0, low, across), jnp.where(x == 0, across, low)], axis=1
    )


def owner_block(mine, other, c, first, height):
    mine, other = mine[first : first + height], other[first : first + height]
    return jnp.concatenate(
        [jnp.where(c == 0, mine, other), jnp.where(c == 0, other, mine)], axis=0
    ).astype(F32)


def quarter_of(w, x, c):
    half_rows, half_cols = w.shape[0] // 2, w.shape[1] // 2
    side = jnp.where(x == 0, w[:, :half_cols], w[:, half_cols:])
    return jnp.where(c == 0, side[:half_rows], side[half_rows:]).astype(BF)


def order_matrix(x, c, z, y):
    rel = jnp.arange(32, dtype=jnp.int32)
    other, a, b, rz = rel // 16, rel // 8 % 2, rel // 4 % 2, rel % 4
    cc = c ^ other
    y_rel = jnp.where(cc == 0, a, b)
    x_rel = jnp.where(cc == 0, b, a)
    place = (((z ^ rz) * 2 + (y ^ y_rel)) * 2 + cc) * 2 + (x ^ x_rel)
    return (place[:, None] == rel[None, :]).astype(F32)


def line_tables(heights):
    place = []
    for shard in range(8):
        at = 0
        for height in heights:
            place += [at + shard * height + k for k in range(height)]
            at += 8 * height
    place = np.array(place).reshape(32, -1)
    count = place.size // 8
    row = np.zeros((place.shape[1], 32, 16), np.float32)
    lane = np.zeros((place.shape[1], 32, 8), np.float32)
    for piece in range(32):
        for k in range(place.shape[1]):
            row[k, piece, place[piece, k] // 8] = 1.0
            lane[k, piece, place[piece, k] % 8] = 1.0
    assert count <= 16
    return jnp.asarray(row), jnp.asarray(lane)


def pack_kernel(order, rows_of, lanes_of, attn_ref, first_ref, bias_ref, two_ref, keep_ref, send_ref, vecs):
    d = vecs.shape[1]
    width = d // 8
    vecs[...] = jnp.zeros_like(vecs)
    vecs[0:2, :] = attn_ref[0:2, :]
    vecs[2:3, :] = first_ref[2:3, :]
    vecs[3:5, :] = first_ref[0:2, :]
    for k in range(4):
        vecs[5 + k : 6 + k, :] = bias_ref[:, k * d : (k + 1) * d]
    vecs[9:10, :] = two_ref[2:3, :]
    vecs[10:12, :] = two_ref[0:2, :]
    parts = []
    for k in range(rows_of.shape[0]):
        chosen = jnp.dot(
            rows_of[k], vecs[...], preferred_element_type=F32, precision=lax.Precision.HIGHEST
        )
        part = jnp.zeros((32, width), F32)
        for m in range(8):
            part = part + chosen[:, m * width : (m + 1) * width] * lanes_of[k, :, m : m + 1]
        parts.append(part)
    parts.append(jnp.zeros((32, keep_ref.shape[1] - len(parts) * width), F32))
    packed = jnp.concatenate(parts, axis=1)
    packed = jnp.dot(
        order[...], packed, preferred_element_type=F32, precision=lax.Precision.HIGHEST
    )
    keep_ref[...] = packed[:16]
    send_ref[...] = packed[16:].astype(BF)


def pack_small(order, tables, attn, first, bias, two):
    d = attn.shape[1]
    return kernel_call(
        pack_kernel,
        [],
        [WHOLE] * 7,
        [order, *tables, attn, first, bias, two],
        out_specs=[WHOLE] * 2,
        out_shape=[
            jax.ShapeDtypeStruct((16, d // 2), F32),
            jax.ShapeDtypeStruct((16, d // 2), BF),
        ],
        scratch_shapes=[pltpu.VMEM((16, d), F32)],
        name="pack_small",
    )


def per_device(
    tokens,
    word_counts,
    region_counts,
    qkv_weight,
    qkv_bias,
    out_weight,
    out_bias,
    attn_gain,
    attn_shift,
    up_weight,
    up_bias,
    down_weight,
    down_bias,
    ffn_gain,
    ffn_shift,
    cotangent,
):
    pairs, seq, d = tokens.shape
    n = pairs * seq
    shard_count, rep_count = lax.axis_size("shard"), lax.axis_size("rep")
    fast = shard_count == 8 and rep_count == 4
    rep, shard = lax.axis_index("rep"), lax.axis_index("shard")
    x, c, z, y = rep // 2, rep % 2, shard // 2, shard % 2
    meta = jnp.stack([x, c, z, y]).astype(jnp.int32)
    vectors = (qkv_bias, out_bias, attn_gain, attn_shift, up_bias, down_bias, ffn_gain, ffn_shift)
    small_own = jnp.concatenate(vectors)
    sizes = [v.shape[0] for v in vectors]

    flat = tokens.reshape(n, d)
    if fast:
        quarter = small_own.shape[0] // 4
        own_small = jnp.where(
            x == 0,
            jnp.where(c == 0, small_own[:quarter], small_own[2 * quarter : 3 * quarter]),
            jnp.where(c == 0, small_own[quarter : 2 * quarter], small_own[3 * quarter :]),
        )
        own_small = jnp.pad(own_small.astype(BF)[None, :], ((0, 15), (0, d // 2 - quarter)))
        own_one = jnp.concatenate(
            [quarter_of(qkv_weight, x, c), quarter_of(out_weight, x, c), own_small], axis=0
        )
        up_pieces = [lax.all_gather(quarter_of(up_weight, x, c), AXES, axis=0)]
        along_one = start_gather(own_one)
        eight_one = first_cross(along_one)
        more_one = to_cross(eight_one, 1)
        along_two = start_gather(after(quarter_of(down_weight, x, c), eight_one))
        other_one = to_core(eight_one)
        along_two, more_one, other_one = after((along_two, more_one, other_one))
        last_one = to_core(more_one)
        qkv_pieces = [eight_one, more_one, other_one, last_one]
        order = order_matrix(x, c, z, y)
        row = d // 4
        tables = line_tables([v // (d // 8) for v in sizes])
        rel_small = jnp.concatenate([p[:, row, :quarter] for p in qkv_pieces]).astype(F32)
        whole_small = lax.dot_general(
            order, rel_small, (((0,), (0,)), ((), ())), precision=lax.Precision.HIGHEST
        ).reshape(8, -1)
        cross_two = to_cross(along_two, 0)
        first_deps = [along_two]
    else:
        qkv_pieces = [
            lax.all_gather(w.astype(BF), "shard", axis=0, tiled=True)
            for w in (qkv_weight, out_weight)
        ]
        whole_small = lax.all_gather(small_own.astype(BF), "shard", axis=0).astype(F32)
        first_deps = []
    parts, at = [], 0
    for size in sizes:
        parts.append(whole_small[:, at : at + size].reshape(1, -1))
        at += size
    bqv, bo, g1, c1, bu, bd, g2, c2 = parts

    vec_one = jnp.concatenate([bqv, bo, g1, c1], axis=1)
    vec_two = jnp.concatenate([g1, c1, bd, g2, c2], axis=1)
    joined, probs, mix, low, xhat, rstd, wqkv, wo = attention_forward(
        fast, meta, word_counts, region_counts, flat, vec_one, qkv_pieces, seq, first_deps
    )
    if fast:
        cross_two = after(cross_two, rstd)
        eight_two = jnp.concatenate([along_two, cross_two])
        more_two = to_cross(eight_two, 1)
        up_deps = [eight_two, vec_two]
    else:
        up_pieces = [lax.all_gather(up_weight.astype(BF), "shard", axis=0, tiled=True)]
        up_deps = []
    act, slope, token = up_forward(fast, meta, low, bu, up_pieces, up_deps)
    if fast:
        more_two = after(more_two, token)
        down_pieces = [eight_two, more_two, to_core(after(eight_two, token)), to_core(more_two)]
    else:
        down_pieces = [lax.all_gather(down_weight.astype(BF), "shard", axis=0, tiled=True)]
    layer_out, second, feed, sums_two, wd, slope, *down_grads = down_forward(
        fast, meta, word_counts, region_counts, act, slope, xhat, vec_two,
        cotangent.reshape(n, d), down_pieces, seq,
    )
    deps = []
    if fast:
        down_sum = Scatter(*down_grads)
    hidden, grad_bu = hidden_grad(feed, slope, wd)
    if fast:
        deps = [down_sum.add_core([grad_bu])]
        down_sum.cross(1)
    up_out = up_grad(fast, meta, hidden, low, up_pieces[0], [second, xhat, rstd, wo], deps)
    up_grads, (token, hidden, wu, second, xhat, rstd, wo) = up_out[:-7], up_out[-7:]
    deps = [token]
    if fast:
        deps = [down_sum.add_cross([token])]
        up_sum = Scatter(up_grads[0], after(up_grads[1], deps[0]))
        down_sum.cross(0)
    attn_sum, attn_low, grad_mix, sums_first = first_back(
        second, hidden, wu, xhat, rstd, wo, g1, deps
    )
    if fast:
        deps = [down_sum.add_last([sums_first]), up_sum.add_core([sums_first])]
        down_sum.along()
        up_sum.cross(1)
    grad_joined, sums_attn = attention_back(grad_mix, joined, probs, seq, deps)
    grad_vectors = [
        jnp.concatenate([sums_attn[0:1], sums_attn[1:2]], axis=1),
        sums_first[2:3],
        sums_first[0:1],
        sums_first[1:2],
        grad_bu,
        sums_two[2:3],
        sums_two[0:1],
        sums_two[1:2],
    ]
    deps = []
    if fast:
        small, small_low = pack_small(order, tables, sums_attn, sums_first, grad_bu, sums_two)
        deps = [up_sum.add_cross([sums_attn]), small_low] + down_sum.got
        up_sum.cross(0)
        small_got = to_core(small_low)
    qkv_out = qkv_grad(fast, meta, grad_joined, flat, attn_low, mix, deps)
    qkv_grads, token = qkv_out[:2], qkv_out[2]
    if fast:
        small_got, up_sum.got = after((small_got, up_sum.got), token)
        qkv_sum = Scatter(qkv_grads[0], after(qkv_grads[1], small_got, up_sum.got))
        up_sum.add_last()
        up_sum.along()
        small = small + small_got.astype(F32)
        token = qkv_sum.add_core([up_sum.token], small=small)
        qkv_sum.cross(1)
        down_total = down_sum.total([token])
        down_across = to_x(down_total)
        tokens_grad, token = tokens_back(attn_sum, grad_joined, wqkv, [token, down_total])
        token = qkv_sum.add_cross([token, down_across] + up_sum.got)
        qkv_sum.cross(0)
        up_total = up_sum.total([token])
        up_across = to_x(up_total)
        token = qkv_sum.add_last([up_across])
        qkv_sum.along()
        down_mine = side_by_side(in_columns(down_total), in_columns(down_across), x)
        up_mine = side_by_side(up_total, up_across, x)
        down_other, up_other = to_core(down_mine), to_core(up_mine)
        grad_down = owner_block(down_mine, down_other, c, 0, down_mine.shape[0])
        grad_up = owner_block(up_mine, up_other, c, 0, up_mine.shape[0])
        grad_up, grad_down, qkv_sum.got = after((grad_up, grad_down, qkv_sum.got))
        qkv_total = qkv_sum.total()
        qkv_mine = side_by_side(qkv_total, to_x(qkv_total), x)
        qkv_other = to_core(qkv_mine)
        grad_qkv, grad_out, small_all = finish(meta, qkv_mine, qkv_other, d)
        small_total = small_all[:, :quarter].reshape(-1)
    else:
        tokens_grad, _ = tokens_back(attn_sum, grad_joined, wqkv)

        def total(v):
            part = lax.psum_scatter(v.astype(F32), "shard", scatter_dimension=0, tiled=True)
            return lax.psum(part, "rep")

        grad_down, grad_up = total(down_grads[0]), total(up_grads[0])
        grad_qkv, grad_out = total(qkv_grads[0]), total(qkv_grads[1])
        small_total = lax.dynamic_index_in_dim(
            jnp.concatenate(
                [lax.psum(g, AXES).reshape(shard_count, -1) for g in grad_vectors], axis=1
            ),
            shard,
            axis=0,
            keepdims=False,
        )
    vector_grads, at = [], 0
    for size in sizes:
        vector_grads.append(small_total[at : at + size])
        at += size
    g_qv, g_bo, g_g1, g_c1, g_bu, g_bd, g_g2, g_c2 = vector_grads
    return (
        layer_out.reshape(tokens.shape),
        tokens_grad.reshape(tokens.shape),
        grad_qkv,
        g_qv,
        grad_out,
        g_bo,
        g_g1,
        g_c1,
        grad_up,
        g_bu,
        grad_down,
        g_bd,
        g_g2,
        g_c2,
    )


def solution(mesh):
    matrix, vector = P("shard", None), P("shard")
    batch, counts = P(AXES, None, None), P(AXES)
    weights = (
        matrix, vector, matrix, vector, vector, vector,
        matrix, vector, matrix, vector, vector, vector,
    )
    return jax.shard_map(
        per_device,
        mesh=mesh,
        in_specs=(batch, counts, counts) + weights + (batch,),
        out_specs=(batch, batch) + weights,
        check_vma=False,
    )
```

```python
import functools

import jax
import jax.numpy as jnp
import numpy as np
from jax import lax
from jax.experimental import pallas as pl
from jax.experimental.pallas import tpu as pltpu
from jax.sharding import PartitionSpec as P

HEADS = 12
WORDS_MAX = 28
EPS = 1e-05
BF = jnp.bfloat16
F32 = jnp.float32
ANY = pl.BlockSpec(memory_space=pl.ANY)
SMEM = pl.BlockSpec(memory_space=pltpu.SMEM)
HBM, VMEM = pltpu.HBM, pltpu.VMEM
TOKEN = jax.ShapeDtypeStruct((8, 128), F32)
WHOLE = pl.BlockSpec(memory_space=pltpu.VMEM)
SQRT_HALF = 0.7071067811865476
INV_SQRT_2PI = 0.3989422804014327


def nt(a, b):
    return lax.dot_general(a, b, (((1,), (1,)), ((), ())), preferred_element_type=F32)


def nn(a, b):
    return jnp.dot(a, b, preferred_element_type=F32)


def tn(a, b):
    return lax.dot_general(a, b, (((0,), (0,)), ((), ())), preferred_element_type=F32)


def fixed(shape):
    return pl.BlockSpec(shape, lambda i: (0,) * len(shape))


def rows(shape):
    return pl.BlockSpec(shape, lambda i: (i,) + (0,) * (len(shape) - 1))


def far(value):
    return pltpu.with_memory_space_constraint(value, HBM)


def near(value):
    return pltpu.with_memory_space_constraint(value, VMEM)


def kernel_call(body, deps, in_specs, args, mebibytes=8, **options):
    count, extra = len(args), len(deps)

    def inner(*refs):
        body(*refs[:count], *refs[count + extra :])

    call = pl.pallas_call(
        inner, in_specs=list(in_specs) + [ANY] * extra, compiler_params=params(mebibytes), **options
    )
    return call(*args, *deps)


def params(mebibytes):
    return pltpu.CompilerParams(vmem_limit_bytes=mebibytes * 1024 * 1024)


def piece_place(meta, cc, a, b, rz, local_rows, start, height, width):
    x0, z0, y0 = meta[0], meta[2], meta[3]
    y_rel = jnp.where(cc == 0, a, b)
    x_rel = jnp.where(cc == 0, b, a)
    shard = (z0 ^ rz) * 2 + (y0 ^ y_rel)
    row = shard * local_rows + cc * height + start
    col = (x0 ^ x_rel) * width
    return pl.multiple_of(row, 16), pl.multiple_of(col, 128)


def piece_copies(meta, pieces, whole, sems, local_rows, first, height, width):
    copies = []
    for number, ref in enumerate(pieces):
        cc = meta[1] if number < 2 else 1 - meta[1]
        a = number % 2
        for b in range(2):
            for rz in range(4):
                row, col = piece_place(meta, cc, a, b, rz, local_rows, 0, height, width)
                copies.append(
                    pltpu.make_async_copy(
                        ref.at[b * 4 + rz, pl.ds(first, height), :],
                        whole.at[pl.ds(row, height), pl.ds(col, width)],
                        sems.at[len(copies)],
                    )
                )
    return copies


def tile_waits(whole, outs, sems, count, first, height, span):
    return [
        pltpu.make_async_copy(
            whole.at[pl.ds(0, height), pl.ds(0, span)],
            ref.at[0, pl.ds(first, height), pl.ds(0, span)],
            sems.at[number * count + i],
        )
        for number, ref in enumerate(outs[1:])
        for i in range(count)
    ]


def load_copies(fast, meta, refs, whole, sems, first):
    if not fast:
        return [pltpu.make_async_copy(refs[0], whole, sems.at[0])]
    local_rows, cols = whole.shape[0] // 8, whole.shape[1]
    if len(refs) == 1:
        height, width = local_rows // 2, cols // 2
        return [
            pltpu.make_async_copy(
                refs[0].at[(x * 2 + c) * 8 + shard],
                whole.at[
                    pl.ds(shard * local_rows + c * height, height), pl.ds(x * width, width)
                ],
                sems.at[(x * 2 + c) * 8 + shard],
            )
            for x in range(2)
            for c in range(2)
            for shard in range(8)
        ]
    return piece_copies(meta, refs, whole, sems, local_rows, first, local_rows // 2, cols // 2)


def go(copies):
    for copy in copies:
        copy.start()


def done(copies):
    for copy in copies:
        copy.wait()


def key_mask(words, regions, shape, axis):
    place = lax.broadcasted_iota(jnp.int32, shape, axis)
    return (place < words) | ((place >= WORDS_MAX) & (place < WORDS_MAX + regions))


def split_heads(block):
    low = lax.broadcasted_iota(jnp.int32, block.shape, 1) < 64
    zero = jnp.zeros_like(block)
    return jnp.concatenate([jnp.where(low, block, zero), jnp.where(low, zero, block)], axis=0)


def turn_heads(block):
    n = block.shape[0]
    return jnp.concatenate([block[:, :n].T, block[:, n:].T], axis=1)


def norm_parts(value):
    center = value - jnp.mean(value, axis=-1, keepdims=True)
    rstd = lax.rsqrt(jnp.mean(center * center, axis=-1, keepdims=True) + EPS)
    return center * rstd, rstd


def norm_back(grad, xhat, rstd, gain):
    scaled = grad * gain
    mean_one = jnp.mean(scaled, axis=-1, keepdims=True)
    mean_two = jnp.mean(scaled * xhat, axis=-1, keepdims=True)
    return rstd * (scaled - mean_one - xhat * mean_two)


def attention_kernel(fast, n_in, *refs):
    meta, words, regions = refs[:3]
    x_ref, vec_ref = refs[3:5]
    pieces = refs[5 : 5 + n_in]
    (joined_ref, probs_ref, mix_ref, low_ref, xhat_ref, rstd_ref, wqkv_out, wo_out) = refs[
        5 + n_in : 13 + n_in
    ]
    wqkv, wo, sem_a, sem_b, sem_c = refs[13 + n_in :]
    step = pl.program_id(0)
    d = x_ref.shape[1]
    seq = probs_ref.shape[2]

    @pl.when(step == 0)
    def _():
        if fast:
            first = load_copies(fast, meta, pieces, wqkv, sem_a, 0)
            second = load_copies(fast, meta, pieces, wo, sem_b, wqkv.shape[0] // 16)
        else:
            first = load_copies(fast, meta, pieces[:1], wqkv, sem_a, 0)
            second = load_copies(fast, meta, pieces[1:], wo, sem_b, 0)
        go(first)
        go(second)
        done(first)
        done(second)

    saves = [
        pltpu.make_async_copy(wqkv, wqkv_out, sem_c.at[0]),
        pltpu.make_async_copy(wo, wo_out, sem_c.at[1]),
    ]

    @pl.when(step == 0)
    def _():
        go(saves)

    x = x_ref[...]
    bq = vec_ref[:, :d]
    bv = vec_ref[:, d : 2 * d]
    joined_ref[:, :d] = (nt(x, wqkv[:d, :]) + bq).astype(BF) * BF(0.125)
    joined_ref[:, d : 2 * d] = nt(x, wqkv[d : 2 * d, :]).astype(BF)
    joined_ref[:, 2 * d :] = (nt(x, wqkv[2 * d :, :]) + bv).astype(BF)
    per_step = x_ref.shape[0] // seq
    for p in range(per_step):
        pair = step * per_step + p
        valid = key_mask(words[pair], regions[pair], (seq, 2 * seq), 0)
        here = pl.ds(p * seq, seq)
        for h in range(d // 128):
            cols = pl.ds(h * 128, 128)
            queries = split_heads(joined_ref[here, pl.ds(h * 128, 128)])
            keys = joined_ref[here, pl.ds(d + h * 128, 128)]
            values = split_heads(joined_ref[here, pl.ds(2 * d + h * 128, 128)])
            scores = jnp.where(valid, nt(keys, queries), -1000000000.0)
            exponent = jnp.exp(scores - jnp.max(scores, axis=0, keepdims=True))
            probs = exponent * (1.0 / jnp.sum(exponent, axis=0, keepdims=True))
            probs = probs.astype(BF)
            probs_ref[p, h] = probs
            mix_ref[here, cols] = nn(turn_heads(probs), values).astype(BF)
    first_sum = x.astype(F32) + nt(mix_ref[...], wo[...]) + vec_ref[:, 2 * d : 3 * d]
    xhat, rstd = norm_parts(first_sum)
    xhat_ref[...] = xhat
    rstd_ref[...] = jnp.broadcast_to(rstd, rstd_ref.shape)
    low_ref[...] = (xhat * vec_ref[:, 3 * d : 4 * d] + vec_ref[:, 4 * d : 5 * d]).astype(BF)

    @pl.when(step == pl.num_programs(0) - 1)
    def _():
        done(saves)


def attention_forward(fast, meta, words, regions, x, vec, pieces, seq, deps=()):
    n, d = x.shape
    tile = 2 * seq
    shapes = [
        HBM((n, 3 * d), BF),
        HBM((n // seq, d // 128, seq, 2 * seq), BF),
        HBM((n, d), BF),
        HBM((n, d), BF),
        HBM((n, d), F32),
        HBM((n, 128), F32),
        HBM((3 * d, d), BF),
        HBM((d, d), BF),
    ]
    return kernel_call(
        functools.partial(attention_kernel, fast, len(pieces)),
        deps,
        [SMEM] * 3 + [rows((tile, d)), fixed(vec.shape)] + [ANY] * len(pieces),
        [meta, words, regions, far(x), vec, *map(far, pieces)],
        grid=(n // tile,),
        out_specs=[
            rows((tile, 3 * d)),
            rows((2, d // 128, seq, 2 * seq)),
            rows((tile, d)),
            rows((tile, d)),
            rows((tile, d)),
            rows((tile, 128)),
            ANY,
            ANY,
        ],
        out_shape=shapes,
        scratch_shapes=[
            pltpu.VMEM((3 * d, d), BF),
            pltpu.VMEM((d, d), BF),
            pltpu.SemaphoreType.DMA((32,)),
            pltpu.SemaphoreType.DMA((32,)),
            pltpu.SemaphoreType.DMA((2,)),
        ],
        cost_estimate=pl.CostEstimate(
            flops=2 * n * d * 4 * d, bytes_accessed=16 * n * d, transcendentals=0
        ),
        mebibytes=17,
        name="attention_forward",
    )


def up_kernel(fast, n_in, *refs):
    meta, low_far, bias_ref = refs[:3]
    pieces = refs[3 : 3 + n_in]
    act_ref, slope_ref, token_ref, low_ref, w, sem_a, sem_b = refs[3 + n_in :]
    token_ref[...] = jnp.zeros_like(token_ref)
    n = low_ref.shape[0]
    tile, width = 256, w.shape[0] // 4
    reads = [pltpu.make_async_copy(low_far, low_ref, sem_b.at[0])]
    go(reads)
    loads = load_copies(fast, meta, pieces, w, sem_a, 0)
    parts = [loads] + [[]] * 3
    if len(loads) == 32:
        parts = [[v for k, v in enumerate(loads) if k % 8 // 2 == j] for j in range(4)]
    for part in parts:
        go(part)
    done(reads)
    for j in range(4):
        done(parts[j])
        here = slice(j * width, (j + 1) * width)
        for i in range(n // tile):
            part = slice(i * tile, (i + 1) * tile)
            hidden = nt(low_ref[part, :], w[here, :]) + bias_ref[:, here]
            phi = 0.5 + 0.5 * lax.erf(hidden * SQRT_HALF)
            act_ref[part, here] = (hidden * phi).astype(BF)
            bell = jnp.exp(hidden * hidden * -0.5) * INV_SQRT_2PI
            slope_ref[part, here] = (phi + hidden * bell).astype(BF)


def up_forward(fast, meta, low, bias, pieces, deps=()):
    n, d = low.shape
    ff = bias.shape[1]
    return kernel_call(
        functools.partial(up_kernel, fast, len(pieces)),
        deps,
        [SMEM, ANY, WHOLE] + [ANY] * len(pieces),
        [meta, far(low), bias, *map(far, pieces)],
        out_specs=[WHOLE] * 3,
        out_shape=[VMEM((n, ff), BF), VMEM((n, ff), BF), TOKEN],
        scratch_shapes=[
            pltpu.VMEM((n, d), BF),
            pltpu.VMEM((ff, d), BF),
            pltpu.SemaphoreType.DMA((32,)),
            pltpu.SemaphoreType.DMA((1,)),
        ],
        cost_estimate=pl.CostEstimate(
            flops=4 * n * d * ff, bytes_accessed=4 * n * ff, transcendentals=0
        ),
        mebibytes=14,
        name="up_forward",
    )


def down_kernel(fast, n_in, seq, *refs):
    meta, words, regions = refs[:3]
    act_ref, slope_ref, xhat_far, vec_ref, cot_far = refs[3:8]
    pieces = refs[8 : 8 + n_in]
    outs_end = 14 + n_in + (2 if fast else 1)
    out_far, second_far, feed_ref, sums_ref, w, _ = refs[8 + n_in : 14 + n_in]
    grads = refs[14 + n_in : outs_end]
    xhat_ref, cot_ref, out_ref, second_ref, whole = refs[outs_end:-3]
    sem_a, sem_b, sem_c = refs[-3:]
    n, d = feed_ref.shape
    ff = act_ref.shape[1]
    tile = 256
    count = n // tile
    loads = load_copies(fast, meta, pieces, w, sem_a, 0)
    go(loads)
    reads, writes = [], []
    for i in range(count):
        part = pl.ds(i * tile, tile)
        reads.append(
            [
                pltpu.make_async_copy(xhat_far.at[part], xhat_ref.at[part], sem_b.at[0, i]),
                pltpu.make_async_copy(cot_far.at[part], cot_ref.at[part], sem_b.at[1, i]),
            ]
        )
        writes += [
            pltpu.make_async_copy(out_ref.at[part], out_far.at[part], sem_b.at[2, i]),
            pltpu.make_async_copy(second_ref.at[part], second_far.at[part], sem_b.at[3, i]),
        ]
    for pair in reads:
        go(pair)
    gain_one, shift_one = vec_ref[:, :d], vec_ref[:, d : 2 * d]
    bias, gain, shift = vec_ref[:, 2 * d : 3 * d], vec_ref[:, 3 * d : 4 * d], vec_ref[:, 4 * d :]
    done(loads)
    sums = [jnp.zeros((1, d), F32)] * 3
    product = nt(act_ref[:tile, :], w[...])
    for i in range(count):
        part = slice(i * tile, (i + 1) * tile)
        done(reads[i])
        if i:
            go(writes[2 * i - 2 : 2 * i])
        this = product
        if i + 1 < count:
            product = nt(act_ref[(i + 1) * tile : (i + 2) * tile, :], w[...])
        second_sum = xhat_ref[part, :] * gain_one + shift_one + this + bias
        xhat, rstd = norm_parts(second_sum)
        first = i * (tile // seq)
        keep = jnp.concatenate(
            [
                key_mask(words[first + p], regions[first + p], (seq, 128), 0)
                for p in range(tile // seq)
            ],
            axis=0,
        )[:, :1]
        out_ref[part, :] = jnp.where(keep, xhat * gain + shift, 0.0).astype(BF)
        grad = jnp.where(keep, cot_ref[part, :].astype(F32), 0.0)
        second = norm_back(grad, xhat, rstd, gain)
        second_ref[part, :] = second
        feed = second.astype(BF)
        feed_ref[part, :] = feed
        for k, value in enumerate((grad * xhat, grad, feed.astype(F32))):
            sums[k] = sums[k] + jnp.sum(value, axis=0, keepdims=True)
    go(writes[-2:])
    for k in range(3):
        sums_ref[k : k + 1, :] = sums[k]
    waits = []
    width, span = ff // 4, ff // 8
    for i in range(4):
        here = slice(i * width, (i + 1) * width)
        whole[:, here] = tn(feed_ref[...], act_ref[:, here]).astype(BF)
        if fast:
            for k in range(2):
                chunk = (i % 2) * 2 + k
                copies = tile_copies(
                    meta, whole, grads, sem_c.at[2 * i + k], range(8), [i // 2], d // 8,
                    chunk * (d // 16), d // 16, ff // 2, (chunk * span, span),
                )
                go(copies)
                waits += tile_waits(
                    whole, grads, sem_c.at[2 * i + k], 8, chunk * (d // 16), d // 16, span
                )
    if not fast:
        waits = [pltpu.make_async_copy(whole, grads[0], sem_c.at[0, 0])]
        go(waits)
    done(waits)
    done(writes)


def down_forward(
    fast, meta, words, regions, act, slope, xhat, vec, cot, pieces, seq, deps=()
):
    n, ff = act.shape
    d = xhat.shape[1]
    shapes = grad_shapes(fast, d, ff)
    return kernel_call(
        functools.partial(down_kernel, fast, len(pieces), seq),
        deps,
        [SMEM] * 3 + [WHOLE, WHOLE, ANY, WHOLE, ANY] + [ANY] * len(pieces),
        [meta, words, regions, near(act), near(slope), far(xhat), vec, far(cot), *map(far, pieces[:-1]), *pieces[-1:]],
        out_specs=[ANY, ANY, WHOLE, WHOLE, WHOLE, WHOLE] + [WHOLE, ANY][-len(shapes) :],
        out_shape=[
            HBM((n, d), BF),
            HBM((n, d), F32),
            VMEM((n, d), BF),
            jax.ShapeDtypeStruct((8, d), F32),
            VMEM((d, ff), BF),
            VMEM((n, ff), BF),
        ]
        + shapes,
        scratch_shapes=[
            pltpu.VMEM((n, d), F32),
            pltpu.VMEM((n, d), BF),
            pltpu.VMEM((n, d), BF),
            pltpu.VMEM((n, d), F32),
            pltpu.VMEM((d, ff), BF),
            pltpu.SemaphoreType.DMA((32,)),
            pltpu.SemaphoreType.DMA((4, n // 256)),
            pltpu.SemaphoreType.DMA((8, 16)),
        ],
        cost_estimate=pl.CostEstimate(
            flops=12 * n * d * ff, bytes_accessed=2 * n * ff, transcendentals=0
        ),
        input_output_aliases={4: 5},
        mebibytes=24,
        name="down_forward",
    )


def hidden_grad_kernel(feed_ref, slope_ref, w, hidden_ref, bias_ref):
    width = 512
    for i in range(slope_ref.shape[1] // width):
        here = slice(i * width, (i + 1) * width)
        hidden = nn(feed_ref[...], w[:, here]) * slope_ref[:, here].astype(F32)
        hidden = hidden.astype(BF)
        hidden_ref[:, here] = hidden
        bias_ref[:, here] = jnp.sum(hidden.astype(F32), axis=0, keepdims=True)


def hidden_grad(feed, slope, w, deps=()):
    n, ff = slope.shape
    d = feed.shape[1]
    return kernel_call(
        hidden_grad_kernel,
        deps,
        [WHOLE] * 3,
        [near(feed), near(slope), near(w)],
        out_specs=[WHOLE] * 2,
        out_shape=[VMEM((n, ff), BF), jax.ShapeDtypeStruct((1, ff), F32)],
        cost_estimate=pl.CostEstimate(
            flops=4 * n * d * ff, bytes_accessed=4 * n * ff, transcendentals=0
        ),
        mebibytes=10,
        name="hidden_grad",
    )


def grad_shapes(fast, total_rows, cols):
    if fast:
        width = min(total_rows, cols) // 2
        shape = (16, total_rows * cols // (32 * width), width)
        return [VMEM(shape, BF), HBM(shape, BF)]
    return [HBM((total_rows, cols), BF)]


def tile_copies(meta, whole, outs, sems, shards, sides, local_rows, first, height, width, cols=None):
    x0, c0, z0, y0 = meta[0], meta[1], meta[2], meta[3]
    offset, span = (0, width) if cols is None else cols
    there = pl.ds(0, span)
    copies = []
    for number, ref in enumerate(outs):
        cc = c0 ^ number
        for shard in shards:
            for side in sides:
                y_rel, x_rel = y0 ^ (shard % 2), x0 ^ side
                a = jnp.where(cc == 0, y_rel, x_rel)
                b = jnp.where(cc == 0, x_rel, y_rel)
                row = pl.multiple_of(shard * local_rows + cc * height, 16)
                col = pl.multiple_of(side * width + offset, 128)
                place = a * 8 + b * 4 + (z0 ^ (shard // 2))
                if number == 0:
                    static = pl.ds(side * width + offset, span)
                    ref[place, pl.ds(first, height), there] = whole[pl.ds(row, height), static]
                    continue
                copies.append(
                    pltpu.make_async_copy(
                        whole.at[pl.ds(row, height), pl.ds(col, span)],
                        ref.at[place, pl.ds(first, height), there],
                        sems.at[len(copies)],
                    )
                )
    return copies


def up_grad_kernel(fast, *refs):
    meta, hidden_ref, low_far, wu_far, *others_far = refs[:8]
    outs = refs[8 : (10 if fast else 9)]
    token_ref, _, wu_ref, *others = refs[10 if fast else 9 : -5]
    low_ref, whole, sems, sem_b, sem_c = refs[-5:]
    reads = [pltpu.make_async_copy(low_far, low_ref, sem_b.at[0])]
    go(reads)
    ahead = load_copies(fast, meta, [wu_far], wu_ref, sem_c, 0)
    for i, (source, target) in enumerate(zip(others_far, others)):
        ahead.append(pltpu.make_async_copy(source, target, sem_b.at[1 + i]))
    go(ahead)
    token_ref[...] = jnp.zeros_like(token_ref)
    done(reads)
    ff, d = whole.shape
    height = ff // 4
    waits = []
    for i in range(4):
        here = slice(i * height, (i + 1) * height)
        whole[here, :] = tn(hidden_ref[:, here], low_ref[...]).astype(BF)
        if fast:
            copies = tile_copies(
                meta, whole, outs, sems.at[i], [2 * i, 2 * i + 1], [0, 1], ff // 8, 0, ff // 16,
                d // 2,
            )
            go(copies)
            waits += tile_waits(whole, outs, sems.at[i], 4, 0, ff // 16, d // 2)
    if not fast:
        waits = [pltpu.make_async_copy(whole, outs[0], sems.at[0, 0])]
        go(waits)
    done(waits + ahead)


def up_grad(fast, meta, hidden, low, wu, others, deps=()):
    n, d = low.shape
    ff = hidden.shape[1]
    shapes = grad_shapes(fast, ff, d)
    return kernel_call(
        functools.partial(up_grad_kernel, fast),
        deps,
        [SMEM, WHOLE] + [ANY] * 6,
        [meta, near(hidden), far(low), far(wu), *map(far, others)],
        out_specs=[WHOLE, ANY][-len(shapes) :] + [WHOLE] * 7,
        out_shape=shapes
        + [TOKEN, VMEM((n, ff), BF), VMEM((ff, d), BF)]
        + [VMEM(v.shape, v.dtype) for v in others],
        scratch_shapes=[
            pltpu.VMEM((n, d), BF),
            pltpu.VMEM((ff, d), BF),
            pltpu.SemaphoreType.DMA((4, 8)),
            pltpu.SemaphoreType.DMA((5,)),
            pltpu.SemaphoreType.DMA((32,)),
        ],
        input_output_aliases={1: len(shapes) + 1},
        cost_estimate=pl.CostEstimate(
            flops=4 * n * d * ff, bytes_accessed=2 * n * ff, transcendentals=0
        ),
        mebibytes=12,
        name="up_grad",
    )


def first_back_kernel(*refs):
    second_ref, hidden_ref, wu_ref, xhat_ref, rstd_ref, wo_ref, gain_ref = refs[:7]
    sum_far, low_far, mix_ref, sums_ref, sum_ref, low_ref, sem = refs[7:]
    n, d = low_ref.shape
    tile = 256
    count = n // tile
    writes = []
    for i in range(count):
        part = pl.ds(i * tile, tile)
        writes.append(
            [
                pltpu.make_async_copy(sum_ref.at[part], sum_far.at[part], sem.at[0, i]),
                pltpu.make_async_copy(low_ref.at[part], low_far.at[part], sem.at[1, i]),
            ]
        )
    product = nn(hidden_ref[:tile, :], wu_ref[...])
    sums = [jnp.zeros((1, d), F32)] * 3
    for i in range(count):
        part = slice(i * tile, (i + 1) * tile)
        if i:
            go(writes[i - 1])
        grad = second_ref[part, :] + product
        if i + 1 < count:
            product = nn(hidden_ref[(i + 1) * tile : (i + 2) * tile, :], wu_ref[...])
        xhat = xhat_ref[part, :]
        attn_sum = norm_back(grad, xhat, rstd_ref[part, :1], gain_ref[...])
        sum_ref[part, :] = attn_sum
        low = attn_sum.astype(BF)
        low_ref[part, :] = low
        mix_ref[part, :] = nn(low, wo_ref[...]).astype(BF)
        for k, value in enumerate((grad * xhat, grad, low.astype(F32))):
            sums[k] = sums[k] + jnp.sum(value, axis=0, keepdims=True)
    go(writes[-1])
    for k in range(3):
        sums_ref[k : k + 1, :] = sums[k]
    for group in writes:
        done(group)


def first_back(second, hidden, wu, xhat, rstd, wo, gain, deps=()):
    n, ff = hidden.shape
    d = xhat.shape[1]
    return kernel_call(
        first_back_kernel,
        deps,
        [WHOLE] * 7,
        [near(v) for v in (second, hidden, wu, xhat, rstd, wo)] + [gain],
        out_specs=[ANY, ANY, WHOLE, WHOLE],
        out_shape=[
            HBM((n, d), F32),
            HBM((n, d), BF),
            VMEM((n, d), BF),
            jax.ShapeDtypeStruct((8, d), F32),
        ],
        scratch_shapes=[
            pltpu.VMEM((n, d), F32),
            pltpu.VMEM((n, d), BF),
            pltpu.SemaphoreType.DMA((2, n // 256)),
        ],
        cost_estimate=pl.CostEstimate(
            flops=4 * n * d * ff, bytes_accessed=2 * n * ff, transcendentals=0
        ),
        mebibytes=12,
        name="first_back",
    )


def attention_back_kernel(seq, *refs):
    mix_ref, joined_ref, probs_ref, *others_far = refs[:6]
    grad_ref, sums_ref, near_ref, *others, sem = refs[6:]
    step = pl.program_id(0)
    ahead = [
        pltpu.make_async_copy(source, target, sem.at[i])
        for i, (source, target) in enumerate(zip(others_far, others))
    ]
    d = mix_ref.shape[1]

    @pl.when(step == 0)
    def _():
        go(ahead)
        sums_ref[...] = jnp.zeros_like(sums_ref)

    for p in range(mix_ref.shape[0] // seq):
        here = pl.ds(p * seq, seq)
        for h in range(d // 128):
            one = pl.ds(h * 128, 128)
            two = pl.ds(d + h * 128, 128)
            three = pl.ds(2 * d + h * 128, 128)
            outer = split_heads(mix_ref[here, one])
            probs = probs_ref[p, h]
            grad_probs = nt(joined_ref[here, three], outer)
            wide = probs.astype(F32)
            product = wide * grad_probs
            scores = product - wide * jnp.sum(product, axis=0, keepdims=True)
            scores = scores.astype(BF)
            grad_ref[here, three] = nn(probs, outer).astype(BF)
            grad_ref[here, two] = nn(scores, split_heads(joined_ref[here, one])).astype(BF)
            keys = split_heads(joined_ref[here, two])
            grad_ref[here, one] = (nn(turn_heads(scores), keys) * 0.125).astype(BF)
    tile = mix_ref.shape[0]
    near_ref[pl.ds(pl.multiple_of(step * tile, tile), tile), :] = grad_ref[...]
    sums_ref[0:1, :] += jnp.sum(grad_ref[:, :d].astype(F32), axis=0, keepdims=True)
    sums_ref[1:2, :] += jnp.sum(grad_ref[:, 2 * d :].astype(F32), axis=0, keepdims=True)

    @pl.when(step == pl.num_programs(0) - 1)
    def _():
        done(ahead)


def attention_back(mix, joined, probs, others, seq, deps=()):
    n, d = mix.shape
    tile = 2 * seq
    return kernel_call(
        functools.partial(attention_back_kernel, seq),
        deps,
        [
            rows((tile, d)),
            rows((tile, 3 * d)),
            rows((2, d // 128, seq, 2 * seq)),
            ANY,
            ANY,
            ANY,
        ],
        [near(mix), far(joined), far(probs), *map(far, others)],
        grid=(n // tile,),
        out_specs=[rows((tile, 3 * d)), fixed((8, d))] + [WHOLE] * 4,
        out_shape=[
            HBM((n, 3 * d), BF),
            jax.ShapeDtypeStruct((8, d), F32),
            VMEM((n, 3 * d), BF),
        ]
        + [VMEM((n, d), BF)] * 3,
        scratch_shapes=[pltpu.SemaphoreType.DMA((3,))],
        cost_estimate=pl.CostEstimate(
            flops=16 * n * d * d, bytes_accessed=30 * n * d, transcendentals=0
        ),
        mebibytes=14,
        name="attention_back",
    )


def qkv_grad_kernel(fast, *refs):
    meta, grad_ref, x_ref, low_ref, mix_ref = refs[:5]
    outs = refs[5:7]
    token_ref, whole, whole_out, sem_a, sem_b = refs[7:]
    token_ref[...] = jnp.zeros_like(token_ref)
    total, d = whole.shape
    waits = []
    for i in range(2):
        here = slice(i * total // 2, (i + 1) * total // 2)
        whole[here, :] = tn(grad_ref[:, here], x_ref[...]).astype(BF)
        if fast:
            go(
                tile_copies(
                    meta, whole, outs, sem_a.at[i], range(4 * i, 4 * i + 4), [0, 1], total // 8,
                    0, total // 16, d // 2,
                )
            )
            waits += tile_waits(whole, outs, sem_a.at[i], 8, 0, total // 16, d // 2)
    whole_out[...] = tn(low_ref[...], mix_ref[...]).astype(BF)
    if fast:
        go(
            tile_copies(
                meta, whole_out, outs, sem_b, range(8), [0, 1], d // 8, total // 16, d // 16,
                d // 2,
            )
        )
        waits += tile_waits(whole_out, outs, sem_b, 16, total // 16, d // 16, d // 2)
    else:
        waits = [
            pltpu.make_async_copy(whole, outs[0], sem_b.at[0]),
            pltpu.make_async_copy(whole_out, outs[1], sem_b.at[1]),
        ]
        go(waits)
    done(waits)


def qkv_grad(fast, meta, grad, x, low, mix, deps=()):
    n, d = x.shape
    if fast:
        shapes = [f((16, 4 * d // 16, d // 2), BF) for f in (VMEM, HBM)]
    else:
        shapes = [jax.ShapeDtypeStruct((3 * d, d), BF), jax.ShapeDtypeStruct((d, d), BF)]
    return kernel_call(
        functools.partial(qkv_grad_kernel, fast),
        deps,
        [SMEM, WHOLE, WHOLE, WHOLE, WHOLE],
        [meta, near(grad), near(x), near(low), near(mix)],
        out_specs=([WHOLE, ANY] if fast else [ANY] * 2) + [WHOLE],
        out_shape=shapes + [TOKEN],
        scratch_shapes=[
            pltpu.VMEM((3 * d, d), BF),
            pltpu.VMEM((d, d), BF),
            pltpu.SemaphoreType.DMA((2, 16)),
            pltpu.SemaphoreType.DMA((32,)),
        ],
        cost_estimate=pl.CostEstimate(
            flops=16 * n * d * d, bytes_accessed=16 * n * d, transcendentals=0
        ),
        mebibytes=20,
        name="qkv_grad",
    )


def tokens_grad_kernel(sum_ref, grad_ref, w_ref, out_ref, token_ref):
    token_ref[...] = jnp.zeros_like(token_ref)
    out_ref[...] = sum_ref[...] + nn(grad_ref[...], w_ref[...])


def tokens_back(attn_sum, grad, w, deps=()):
    n, d = attn_sum.shape
    tile = 256
    return kernel_call(
        tokens_grad_kernel,
        deps,
        [rows((tile, d)), rows((tile, 3 * d)), fixed((3 * d, d))],
        [far(attn_sum), far(grad), far(w)],
        grid=(n // tile,),
        out_specs=[rows((tile, d)), fixed((8, 128))],
        out_shape=[HBM((n, d), F32), TOKEN],
        cost_estimate=pl.CostEstimate(
            flops=12 * n * d * d, bytes_accessed=14 * n * d, transcendentals=0
        ),
        mebibytes=14,
        name="tokens_back",
    )


AXES = ("rep", "shard")


def route(fn):
    pairs = []
    for x in range(2):
        for c in range(2):
            for z in range(4):
                for y in range(2):
                    to = fn(x, c, z, y)
                    pairs.append(
                        ((x * 2 + c) * 8 + z * 2 + y, (to[0] * 2 + to[1]) * 8 + to[2] * 2 + to[3])
                    )
    return pairs


def to_core(v):
    return lax.ppermute(v, AXES, route(lambda x, c, z, y: (x, 1 - c, z, y)))


def to_x(v):
    return lax.ppermute(v, AXES, route(lambda x, c, z, y: (1 - x, c, z, y)))


def to_z(v, k):
    return lax.ppermute(v, AXES, route(lambda x, c, z, y: (x, c, z ^ k, y)))


def to_cross(v, first_core):
    return lax.ppermute(
        v,
        AXES,
        route(lambda x, c, z, y: (1 - x, c, z, y) if c == first_core else (x, c, z, 1 - y)),
    )


def after(value, *others):
    return lax.optimization_barrier((value, others))[0]


def start_gather(own):
    return jnp.stack([own] + [to_z(own, k) for k in (1, 2, 3)])


def first_cross(along):
    return jnp.concatenate([along, to_cross(along, 0)])


def add_core_kernel(kept_ref, got_ref, *refs):
    keep_ref, send_ref = refs[-2:]
    count, height, width = keep_ref.shape
    for k in range(count):
        here = slice(k * height, (k + 1) * height)
        keep_ref[k] = (kept_ref[k].astype(F32) + got_ref[k].astype(F32)).astype(BF)
        other = kept_ref[count + k].astype(F32) + got_ref[count + k].astype(F32)
        send_ref[here, :] = other.astype(BF)
    if len(refs) == 3:
        send_ref[count * height :, :] = refs[0][...].astype(BF)


def add_cross_kernel(keep_ref, got_ref, *refs):
    small = len(refs) == 4
    new_ref, send_ref = refs[1:3] if small else refs
    count, height, width = new_ref.shape
    for k in range(2 * count):
        here = slice(k * height, (k + 1) * height)
        total = (keep_ref[k].astype(F32) + got_ref[here, :].astype(F32)).astype(BF)
        if k < count:
            new_ref[k] = total
        else:
            send_ref[(k - count) * height : (k - count + 1) * height, :] = total
    if small:
        rows_in = refs[0][...] + got_ref[2 * count * height :, :].astype(F32)
        refs[3][...] = rows_in
        tail = jnp.concatenate([rows_in[count : 2 * count], rows_in[2 * count :]], axis=0)
        tail = jnp.concatenate([tail, jnp.zeros((count, width), F32)], axis=0)
        send_ref[count * height :, :] = tail.astype(BF)


def add_last_kernel(keep_ref, got_ref, *refs):
    small = len(refs) == 5
    outs = refs[1:] if small else refs
    count, height, width = keep_ref.shape
    if small:
        rows_in = refs[0][...] + got_ref[count * height :, :].astype(F32)
        place = lax.broadcasted_iota(jnp.int32, rows_in.shape, 0)
    for k in range(count):
        here = slice(k * height, (k + 1) * height)
        total = keep_ref[k].astype(F32) + got_ref[here, :].astype(F32)
        outs[k][:height, :] = total.astype(outs[k].dtype)
        if small:
            row = jnp.sum(jnp.where(place == k, rows_in, 0.0), axis=0, keepdims=True)
            outs[k][height:, :] = jnp.broadcast_to(row, (16, width)).astype(outs[k].dtype)


def total_kernel(own_ref, one_ref, two_ref, three_ref, out_ref):
    total = own_ref[...] + one_ref[...].astype(F32)
    total = total + two_ref[...].astype(F32) + three_ref[...].astype(F32)
    out_ref[...] = total.astype(BF)


class Scatter:
    def __init__(self, kept, sent):
        self.kept, self.small = kept, None
        self.got = to_core(sent)

    def call(self, body, out_shape, extra, deps, name):
        args = [near(self.keep), near(self.got)] + list(extra)

        def marked(*refs):
            refs[-1][...] = jnp.zeros_like(refs[-1])
            body(*refs[:-1])

        *out, self.token = kernel_call(
            marked,
            deps,
            [WHOLE] * len(args),
            args,
            out_specs=[WHOLE] * (len(out_shape) + 1),
            out_shape=out_shape + [TOKEN],
            name=name,
        )
        return out

    def add_core(self, deps=(), small=None):
        self.keep = self.kept
        count, height, width = self.kept.shape[0] // 2, *self.kept.shape[1:]
        tail, extra = 0, []
        if small is not None:
            tail, extra = 16, [jnp.concatenate([small[8:], jnp.zeros_like(small[8:])])]
            self.small = jnp.concatenate([small[:8], jnp.zeros_like(small[8:])])
        self.keep, self.send = self.call(
            add_core_kernel,
            [VMEM((count, height, width), BF), VMEM((count * height + tail, width), BF)],
            extra,
            deps,
            "add_core",
        )
        return self.token

    def cross(self, core):
        self.got = to_cross(self.send, core)

    def add_cross(self, deps=()):
        count, height, width = self.keep.shape[0] // 2, *self.keep.shape[1:]
        small = self.small is not None
        outs = [
            VMEM((count, height, width), BF),
            VMEM((count * height + 16 * small, width), BF),
        ]
        if small:
            outs.append(VMEM((16, width), F32))
        out = self.call(
            add_cross_kernel, outs, [self.small] if small else [], deps, "add_cross"
        )
        self.keep, self.send = out[:2]
        if small:
            self.small = out[2]
        return self.token

    def add_last(self, deps=()):
        height, width = self.keep.shape[1:]
        small = self.small is not None
        shape = (height + 16 * small, width)
        self.parts = self.call(
            add_last_kernel,
            [VMEM(shape, F32)] + [VMEM(shape, BF)] * 3,
            [self.small] if small else [],
            deps,
            "add_last",
        )
        return self.token

    def along(self):
        self.got = [to_z(self.parts[k], k) for k in (1, 2, 3)]

    def total(self, deps=()):
        args = [near(v) for v in [self.parts[0]] + self.got]
        return kernel_call(
            total_kernel,
            deps,
            [WHOLE] * 4,
            args,
            out_specs=WHOLE,
            out_shape=jax.ShapeDtypeStruct(self.parts[0].shape, BF),
            name="total",
        )


def finish_kernel(meta, mine_ref, other_ref, qkv_ref, out_ref, small_ref):
    c = meta[1]
    first = 0
    for target in (qkv_ref, out_ref):
        half = target.shape[0] // 2
        part = slice(first, first + half)
        target[pl.ds(pl.multiple_of(c * half, 8), half), :] = mine_ref[part, :].astype(F32)
        target[pl.ds(pl.multiple_of((1 - c) * half, 8), half), :] = other_ref[part, :].astype(F32)
        first += half
    mine = mine_ref[first : first + 16, :].astype(F32)[:1]
    other = other_ref[first : first + 16, :].astype(F32)[:1]
    width = small_ref.shape[1]
    for k, line in enumerate((jnp.where(c == 0, mine, other), jnp.where(c == 0, other, mine))):
        small_ref[2 * k : 2 * k + 1, :] = line[:, :width]
        small_ref[2 * k + 1 : 2 * k + 2, :] = line[:, width:]


def finish(meta, mine, other, d):
    return kernel_call(
        finish_kernel,
        [],
        [SMEM, WHOLE, WHOLE],
        [meta, near(mine), near(other)],
        out_specs=[WHOLE] * 3,
        out_shape=[HBM((3 * d // 8, d), F32), HBM((d // 8, d), F32), VMEM((4, d // 2), F32)],
        name="finish",
    )


def in_columns(piece):
    return jnp.concatenate(jnp.split(piece, 4, axis=0), axis=1)


def side_by_side(low, across, x):
    return jnp.concatenate(
        [jnp.where(x == 0, low, across), jnp.where(x == 0, across, low)], axis=1
    )


def owner_block(mine, other, c, first, height):
    mine, other = mine[first : first + height], other[first : first + height]
    return jnp.concatenate(
        [jnp.where(c == 0, mine, other), jnp.where(c == 0, other, mine)], axis=0
    ).astype(F32)


def quarter_of(w, x, c):
    half_rows, half_cols = w.shape[0] // 2, w.shape[1] // 2
    side = jnp.where(x == 0, w[:, :half_cols], w[:, half_cols:])
    return jnp.where(c == 0, side[:half_rows], side[half_rows:]).astype(BF)


def order_matrix(x, c, z, y):
    rel = jnp.arange(32, dtype=jnp.int32)
    other, a, b, rz = rel // 16, rel // 8 % 2, rel // 4 % 2, rel % 4
    cc = c ^ other
    y_rel = jnp.where(cc == 0, a, b)
    x_rel = jnp.where(cc == 0, b, a)
    place = (((z ^ rz) * 2 + (y ^ y_rel)) * 2 + cc) * 2 + (x ^ x_rel)
    return (place[:, None] == rel[None, :]).astype(F32)


def line_tables(heights):
    place = []
    for shard in range(8):
        at = 0
        for height in heights:
            place += [at + shard * height + k for k in range(height)]
            at += 8 * height
    place = np.array(place).reshape(32, -1)
    count = place.size // 8
    row = np.zeros((place.shape[1], 32, 16), np.float32)
    lane = np.zeros((place.shape[1], 32, 8), np.float32)
    for piece in range(32):
        for k in range(place.shape[1]):
            row[k, piece, place[piece, k] // 8] = 1.0
            lane[k, piece, place[piece, k] % 8] = 1.0
    assert count <= 16
    return jnp.asarray(row), jnp.asarray(lane)


def pack_kernel(order, rows_of, lanes_of, attn_ref, first_ref, bias_ref, two_ref, keep_ref, send_ref, vecs):
    d = vecs.shape[1]
    width = d // 8
    vecs[...] = jnp.zeros_like(vecs)
    vecs[0:2, :] = attn_ref[0:2, :]
    vecs[2:3, :] = first_ref[2:3, :]
    vecs[3:5, :] = first_ref[0:2, :]
    for k in range(4):
        vecs[5 + k : 6 + k, :] = bias_ref[:, k * d : (k + 1) * d]
    vecs[9:10, :] = two_ref[2:3, :]
    vecs[10:12, :] = two_ref[0:2, :]
    parts = []
    for k in range(rows_of.shape[0]):
        chosen = jnp.dot(
            rows_of[k], vecs[...], preferred_element_type=F32, precision=lax.Precision.HIGHEST
        )
        part = jnp.zeros((32, width), F32)
        for m in range(8):
            part = part + chosen[:, m * width : (m + 1) * width] * lanes_of[k, :, m : m + 1]
        parts.append(part)
    parts.append(jnp.zeros((32, keep_ref.shape[1] - len(parts) * width), F32))
    packed = jnp.concatenate(parts, axis=1)
    packed = jnp.dot(
        order[...], packed, preferred_element_type=F32, precision=lax.Precision.HIGHEST
    )
    keep_ref[...] = packed[:16]
    send_ref[...] = packed[16:].astype(BF)


def pack_small(order, tables, attn, first, bias, two):
    d = attn.shape[1]
    return kernel_call(
        pack_kernel,
        [],
        [WHOLE] * 7,
        [order, *tables, attn, first, bias, two],
        out_specs=[WHOLE] * 2,
        out_shape=[
            jax.ShapeDtypeStruct((16, d // 2), F32),
            jax.ShapeDtypeStruct((16, d // 2), BF),
        ],
        scratch_shapes=[pltpu.VMEM((16, d), F32)],
        name="pack_small",
    )


def per_device(
    tokens,
    word_counts,
    region_counts,
    qkv_weight,
    qkv_bias,
    out_weight,
    out_bias,
    attn_gain,
    attn_shift,
    up_weight,
    up_bias,
    down_weight,
    down_bias,
    ffn_gain,
    ffn_shift,
    cotangent,
):
    pairs, seq, d = tokens.shape
    n = pairs * seq
    shard_count, rep_count = lax.axis_size("shard"), lax.axis_size("rep")
    fast = shard_count == 8 and rep_count == 4
    rep, shard = lax.axis_index("rep"), lax.axis_index("shard")
    x, c, z, y = rep // 2, rep % 2, shard // 2, shard % 2
    meta = jnp.stack([x, c, z, y]).astype(jnp.int32)
    vectors = (qkv_bias, out_bias, attn_gain, attn_shift, up_bias, down_bias, ffn_gain, ffn_shift)
    small_own = jnp.concatenate(vectors)
    sizes = [v.shape[0] for v in vectors]

    flat = tokens.reshape(n, d)
    if fast:
        quarter = small_own.shape[0] // 4
        own_small = jnp.where(
            x == 0,
            jnp.where(c == 0, small_own[:quarter], small_own[2 * quarter : 3 * quarter]),
            jnp.where(c == 0, small_own[quarter : 2 * quarter], small_own[3 * quarter :]),
        )
        own_small = jnp.pad(own_small.astype(BF)[None, :], ((0, 15), (0, d // 2 - quarter)))
        own_one = jnp.concatenate(
            [quarter_of(qkv_weight, x, c), quarter_of(out_weight, x, c), own_small], axis=0
        )
        up_pieces = [lax.all_gather(quarter_of(up_weight, x, c), AXES, axis=0)]
        along_one = start_gather(own_one)
        eight_one = first_cross(along_one)
        more_one = to_cross(eight_one, 1)
        along_two = start_gather(after(quarter_of(down_weight, x, c), eight_one))
        other_one = to_core(eight_one)
        along_two, more_one, other_one = after((along_two, more_one, other_one))
        last_one = to_core(more_one)
        qkv_pieces = [eight_one, more_one, other_one, last_one]
        order = order_matrix(x, c, z, y)
        row = d // 4
        tables = line_tables([v // (d // 8) for v in sizes])
        rel_small = jnp.concatenate([p[:, row, :quarter] for p in qkv_pieces]).astype(F32)
        whole_small = lax.dot_general(
            order, rel_small, (((0,), (0,)), ((), ())), precision=lax.Precision.HIGHEST
        ).reshape(8, -1)
        cross_two = to_cross(along_two, 0)
        first_deps = [along_two]
    else:
        qkv_pieces = [
            lax.all_gather(w.astype(BF), "shard", axis=0, tiled=True)
            for w in (qkv_weight, out_weight)
        ]
        whole_small = lax.all_gather(small_own.astype(BF), "shard", axis=0).astype(F32)
        first_deps = []
    parts, at = [], 0
    for size in sizes:
        parts.append(whole_small[:, at : at + size].reshape(1, -1))
        at += size
    bqv, bo, g1, c1, bu, bd, g2, c2 = parts

    vec_one = jnp.concatenate([bqv, bo, g1, c1], axis=1)
    vec_two = jnp.concatenate([g1, c1, bd, g2, c2], axis=1)
    joined, probs, mix, low, xhat, rstd, wqkv, wo = attention_forward(
        fast, meta, word_counts, region_counts, flat, vec_one, qkv_pieces, seq, first_deps
    )
    if fast:
        cross_two = after(cross_two, rstd)
        eight_two = jnp.concatenate([along_two, cross_two])
        more_two = to_cross(eight_two, 1)
        up_deps = [eight_two, vec_two]
    else:
        up_pieces = [lax.all_gather(up_weight.astype(BF), "shard", axis=0, tiled=True)]
        up_deps = []
    act, slope, token = up_forward(fast, meta, low, bu, up_pieces, up_deps)
    if fast:
        more_two = after(more_two, token)
        down_pieces = [eight_two, more_two, to_core(after(eight_two, token)), to_core(more_two)]
    else:
        down_pieces = [lax.all_gather(down_weight.astype(BF), "shard", axis=0, tiled=True)]
    layer_out, second, feed, sums_two, wd, slope, *down_grads = down_forward(
        fast, meta, word_counts, region_counts, act, slope, xhat, vec_two,
        cotangent.reshape(n, d), down_pieces, seq,
    )
    deps = []
    if fast:
        down_sum = Scatter(*down_grads)
    hidden, grad_bu = hidden_grad(feed, slope, wd)
    if fast:
        deps = [down_sum.add_core([grad_bu])]
        down_sum.cross(1)
    up_out = up_grad(fast, meta, hidden, low, up_pieces[0], [second, xhat, rstd, wo], deps)
    up_grads, (token, hidden, wu, second, xhat, rstd, wo) = up_out[:-7], up_out[-7:]
    deps = [token]
    if fast:
        deps = [down_sum.add_cross([token])]
        up_sum = Scatter(up_grads[0], after(up_grads[1], deps[0]))
        down_sum.cross(0)
    attn_sum, attn_low, grad_mix, sums_first = first_back(
        second, hidden, wu, xhat, rstd, wo, g1, deps
    )
    if fast:
        deps = [down_sum.add_last([sums_first]), up_sum.add_core([sums_first])]
        down_sum.along()
        up_sum.cross(1)
    grad_joined, sums_attn, joined_near, *others = attention_back(
        grad_mix, joined, probs, [flat, attn_low, mix], seq, deps
    )
    grad_vectors = [
        jnp.concatenate([sums_attn[0:1], sums_attn[1:2]], axis=1),
        sums_first[2:3],
        sums_first[0:1],
        sums_first[1:2],
        grad_bu,
        sums_two[2:3],
        sums_two[0:1],
        sums_two[1:2],
    ]
    deps = []
    if fast:
        small, small_low = pack_small(order, tables, sums_attn, sums_first, grad_bu, sums_two)
        deps = [up_sum.add_cross([sums_attn]), small_low] + down_sum.got
        up_sum.cross(0)
        small_got = to_core(small_low)
    qkv_out = qkv_grad(fast, meta, joined_near, *others, deps)
    qkv_grads, token = qkv_out[:2], qkv_out[2]
    if fast:
        small_got, up_sum.got = after((small_got, up_sum.got), token)
        qkv_sum = Scatter(qkv_grads[0], after(qkv_grads[1], small_got, up_sum.got))
        up_sum.add_last()
        up_sum.along()
        small = small + small_got.astype(F32)
        token = qkv_sum.add_core([up_sum.token], small=small)
        qkv_sum.cross(1)
        down_total = down_sum.total([token])
        down_across = to_x(down_total)
        tokens_grad, token = tokens_back(attn_sum, grad_joined, wqkv, [token, down_total])
        token = qkv_sum.add_cross([token, down_across] + up_sum.got)
        qkv_sum.cross(0)
        up_total = up_sum.total([token])
        up_across = to_x(up_total)
        token = qkv_sum.add_last([up_across])
        qkv_sum.along()
        down_mine = side_by_side(in_columns(down_total), in_columns(down_across), x)
        up_mine = side_by_side(up_total, up_across, x)
        down_other, up_other = to_core(down_mine), to_core(up_mine)
        grad_down = owner_block(down_mine, down_other, c, 0, down_mine.shape[0])
        grad_up = owner_block(up_mine, up_other, c, 0, up_mine.shape[0])
        grad_up, grad_down, qkv_sum.got = after((grad_up, grad_down, qkv_sum.got))
        qkv_total = qkv_sum.total()
        qkv_mine = side_by_side(qkv_total, to_x(qkv_total), x)
        qkv_other = to_core(qkv_mine)
        grad_qkv, grad_out, small_all = finish(meta, qkv_mine, qkv_other, d)
        small_total = small_all[:, :quarter].reshape(-1)
    else:
        tokens_grad, _ = tokens_back(attn_sum, grad_joined, wqkv)

        def total(v):
            part = lax.psum_scatter(v.astype(F32), "shard", scatter_dimension=0, tiled=True)
            return lax.psum(part, "rep")

        grad_down, grad_up = total(down_grads[0]), total(up_grads[0])
        grad_qkv, grad_out = total(qkv_grads[0]), total(qkv_grads[1])
        small_total = lax.dynamic_index_in_dim(
            jnp.concatenate(
                [lax.psum(g, AXES).reshape(shard_count, -1) for g in grad_vectors], axis=1
            ),
            shard,
            axis=0,
            keepdims=False,
        )
    vector_grads, at = [], 0
    for size in sizes:
        vector_grads.append(small_total[at : at + size])
        at += size
    g_qv, g_bo, g_g1, g_c1, g_bu, g_bd, g_g2, g_c2 = vector_grads
    return (
        layer_out.reshape(tokens.shape),
        tokens_grad.reshape(tokens.shape),
        grad_qkv,
        g_qv,
        grad_out,
        g_bo,
        g_g1,
        g_c1,
        grad_up,
        g_bu,
        grad_down,
        g_bd,
        g_g2,
        g_c2,
    )


def solution(mesh):
    matrix, vector = P("shard", None), P("shard")
    batch, counts = P(AXES, None, None), P(AXES)
    weights = (
        matrix, vector, matrix, vector, vector, vector,
        matrix, vector, matrix, vector, vector, vector,
    )
    return jax.shard_map(
        per_device,
        mesh=mesh,
        in_specs=(batch, counts, counts) + weights + (batch,),
        out_specs=(batch, batch) + weights,
        check_vma=False,
    )
```

```python
import functools

import jax
import jax.numpy as jnp
import numpy as np
from jax import lax
from jax.experimental import pallas as pl
from jax.experimental.pallas import tpu as pltpu
from jax.sharding import PartitionSpec as P

HEADS = 12
WORDS_MAX = 28
EPS = 1e-05
BF = jnp.bfloat16
F32 = jnp.float32
ANY = pl.BlockSpec(memory_space=pl.ANY)
SMEM = pl.BlockSpec(memory_space=pltpu.SMEM)
HBM, VMEM = pltpu.HBM, pltpu.VMEM
TOKEN = jax.ShapeDtypeStruct((8, 128), F32)
WHOLE = pl.BlockSpec(memory_space=pltpu.VMEM)
SQRT_HALF = 0.7071067811865476
INV_SQRT_2PI = 0.3989422804014327


def nt(a, b):
    return lax.dot_general(a, b, (((1,), (1,)), ((), ())), preferred_element_type=F32)


def nn(a, b):
    return jnp.dot(a, b, preferred_element_type=F32)


def tn(a, b):
    return lax.dot_general(a, b, (((0,), (0,)), ((), ())), preferred_element_type=F32)


def fixed(shape):
    return pl.BlockSpec(shape, lambda i: (0,) * len(shape))


def rows(shape):
    return pl.BlockSpec(shape, lambda i: (i,) + (0,) * (len(shape) - 1))


def far(value):
    return pltpu.with_memory_space_constraint(value, HBM)


def near(value):
    return pltpu.with_memory_space_constraint(value, VMEM)


def kernel_call(body, deps, in_specs, args, mebibytes=8, **options):
    count, extra = len(args), len(deps)

    def inner(*refs):
        body(*refs[:count], *refs[count + extra :])

    call = pl.pallas_call(
        inner, in_specs=list(in_specs) + [ANY] * extra, compiler_params=params(mebibytes), **options
    )
    return call(*args, *deps)


def params(mebibytes):
    return pltpu.CompilerParams(vmem_limit_bytes=mebibytes * 1024 * 1024)


def piece_place(meta, cc, a, b, rz, local_rows, start, height, width):
    x0, z0, y0 = meta[0], meta[2], meta[3]
    y_rel = jnp.where(cc == 0, a, b)
    x_rel = jnp.where(cc == 0, b, a)
    shard = (z0 ^ rz) * 2 + (y0 ^ y_rel)
    row = shard * local_rows + cc * height + start
    col = (x0 ^ x_rel) * width
    return pl.multiple_of(row, 16), pl.multiple_of(col, 128)


def piece_copies(meta, pieces, whole, sems, local_rows, first, height, width):
    copies = []
    for number, ref in enumerate(pieces):
        cc = meta[1] if number < 2 else 1 - meta[1]
        a = number % 2
        for b in range(2):
            for rz in range(4):
                row, col = piece_place(meta, cc, a, b, rz, local_rows, 0, height, width)
                copies.append(
                    pltpu.make_async_copy(
                        ref.at[b * 4 + rz, pl.ds(first, height), :],
                        whole.at[pl.ds(row, height), pl.ds(col, width)],
                        sems.at[len(copies)],
                    )
                )
    return copies


def tile_waits(whole, outs, sems, count, first, height, span):
    return [
        pltpu.make_async_copy(
            whole.at[pl.ds(0, height), pl.ds(0, span)],
            ref.at[0, pl.ds(first, height), pl.ds(0, span)],
            sems.at[number * count + i],
        )
        for number, ref in enumerate(outs[1:])
        for i in range(count)
    ]


def load_copies(fast, meta, refs, whole, sems, first):
    if not fast:
        return [pltpu.make_async_copy(refs[0], whole, sems.at[0])]
    local_rows, cols = whole.shape[0] // 8, whole.shape[1]
    if len(refs) == 1:
        height, width = local_rows // 2, cols // 2
        return [
            pltpu.make_async_copy(
                refs[0].at[(x * 2 + c) * 8 + shard],
                whole.at[
                    pl.ds(shard * local_rows + c * height, height), pl.ds(x * width, width)
                ],
                sems.at[(x * 2 + c) * 8 + shard],
            )
            for x in range(2)
            for c in range(2)
            for shard in range(8)
        ]
    return piece_copies(meta, refs, whole, sems, local_rows, first, local_rows // 2, cols // 2)


def go(copies):
    for copy in copies:
        copy.start()


def done(copies):
    for copy in copies:
        copy.wait()


def key_mask(words, regions, shape, axis):
    place = lax.broadcasted_iota(jnp.int32, shape, axis)
    return (place < words) | ((place >= WORDS_MAX) & (place < WORDS_MAX + regions))


def split_heads(block):
    low = lax.broadcasted_iota(jnp.int32, block.shape, 1) < 64
    zero = jnp.zeros_like(block)
    return jnp.concatenate([jnp.where(low, block, zero), jnp.where(low, zero, block)], axis=0)


def turn_heads(block):
    n = block.shape[0]
    return jnp.concatenate([block[:, :n].T, block[:, n:].T], axis=1)


def norm_parts(value):
    center = value - jnp.mean(value, axis=-1, keepdims=True)
    rstd = lax.rsqrt(jnp.mean(center * center, axis=-1, keepdims=True) + EPS)
    return center * rstd, rstd


def norm_back(grad, xhat, rstd, gain):
    scaled = grad * gain
    mean_one = jnp.mean(scaled, axis=-1, keepdims=True)
    mean_two = jnp.mean(scaled * xhat, axis=-1, keepdims=True)
    return rstd * (scaled - mean_one - xhat * mean_two)


def attention_kernel(fast, n_in, *refs):
    meta, words, regions = refs[:3]
    x_ref, vec_ref = refs[3:5]
    pieces = refs[5 : 5 + n_in]
    (joined_ref, probs_ref, mix_ref, low_ref, xhat_ref, rstd_ref, wqkv_out, wo_out) = refs[
        5 + n_in : 13 + n_in
    ]
    wqkv, wo, sem_a, sem_b, sem_c = refs[13 + n_in :]
    step = pl.program_id(0)
    d = x_ref.shape[1]
    seq = probs_ref.shape[2]

    @pl.when(step == 0)
    def _():
        if fast:
            first = load_copies(fast, meta, pieces, wqkv, sem_a, 0)
            second = load_copies(fast, meta, pieces, wo, sem_b, wqkv.shape[0] // 16)
        else:
            first = load_copies(fast, meta, pieces[:1], wqkv, sem_a, 0)
            second = load_copies(fast, meta, pieces[1:], wo, sem_b, 0)
        go(first)
        go(second)
        done(first)
        done(second)

    saves = [
        pltpu.make_async_copy(wqkv, wqkv_out, sem_c.at[0]),
        pltpu.make_async_copy(wo, wo_out, sem_c.at[1]),
    ]

    @pl.when(step == 0)
    def _():
        go(saves)

    x = x_ref[...]
    bq = vec_ref[:, :d]
    bv = vec_ref[:, d : 2 * d]
    joined_ref[:, :d] = (nt(x, wqkv[:d, :]) + bq).astype(BF) * BF(0.125)
    joined_ref[:, d : 2 * d] = nt(x, wqkv[d : 2 * d, :]).astype(BF)
    joined_ref[:, 2 * d :] = (nt(x, wqkv[2 * d :, :]) + bv).astype(BF)
    per_step = x_ref.shape[0] // seq
    for p in range(per_step):
        pair = step * per_step + p
        valid = key_mask(words[pair], regions[pair], (seq, 2 * seq), 0)
        here = pl.ds(p * seq, seq)
        for h in range(d // 128):
            cols = pl.ds(h * 128, 128)
            queries = split_heads(joined_ref[here, pl.ds(h * 128, 128)])
            keys = joined_ref[here, pl.ds(d + h * 128, 128)]
            values = split_heads(joined_ref[here, pl.ds(2 * d + h * 128, 128)])
            scores = jnp.where(valid, nt(keys, queries), -1000000000.0)
            exponent = jnp.exp(scores - jnp.max(scores, axis=0, keepdims=True))
            probs = exponent * (1.0 / jnp.sum(exponent, axis=0, keepdims=True))
            probs = probs.astype(BF)
            probs_ref[p, h] = probs
            mix_ref[here, cols] = nn(turn_heads(probs), values).astype(BF)
    first_sum = x.astype(F32) + nt(mix_ref[...], wo[...]) + vec_ref[:, 2 * d : 3 * d]
    xhat, rstd = norm_parts(first_sum)
    xhat_ref[...] = xhat
    rstd_ref[...] = jnp.broadcast_to(rstd, rstd_ref.shape)
    low_ref[...] = (xhat * vec_ref[:, 3 * d : 4 * d] + vec_ref[:, 4 * d : 5 * d]).astype(BF)

    @pl.when(step == pl.num_programs(0) - 1)
    def _():
        done(saves)


def attention_forward(fast, meta, words, regions, x, vec, pieces, seq, deps=()):
    n, d = x.shape
    tile = 2 * seq
    shapes = [
        HBM((n, 3 * d), BF),
        HBM((n // seq, d // 128, seq, 2 * seq), BF),
        HBM((n, d), BF),
        HBM((n, d), BF),
        HBM((n, d), F32),
        HBM((n, 128), F32),
        HBM((3 * d, d), BF),
        HBM((d, d), BF),
    ]
    return kernel_call(
        functools.partial(attention_kernel, fast, len(pieces)),
        deps,
        [SMEM] * 3 + [rows((tile, d)), fixed(vec.shape)] + [ANY] * len(pieces),
        [meta, words, regions, far(x), vec, *map(far, pieces)],
        grid=(n // tile,),
        out_specs=[
            rows((tile, 3 * d)),
            rows((2, d // 128, seq, 2 * seq)),
            rows((tile, d)),
            rows((tile, d)),
            rows((tile, d)),
            rows((tile, 128)),
            ANY,
            ANY,
        ],
        out_shape=shapes,
        scratch_shapes=[
            pltpu.VMEM((3 * d, d), BF),
            pltpu.VMEM((d, d), BF),
            pltpu.SemaphoreType.DMA((32,)),
            pltpu.SemaphoreType.DMA((32,)),
            pltpu.SemaphoreType.DMA((2,)),
        ],
        cost_estimate=pl.CostEstimate(
            flops=2 * n * d * 4 * d, bytes_accessed=16 * n * d, transcendentals=0
        ),
        mebibytes=17,
        name="attention_forward",
    )


def up_kernel(fast, n_in, *refs):
    meta, low_far, bias_ref = refs[:3]
    pieces = refs[3 : 3 + n_in]
    act_ref, slope_ref, token_ref, low_ref, w, sem_a, sem_b = refs[3 + n_in :]
    token_ref[...] = jnp.zeros_like(token_ref)
    n = low_ref.shape[0]
    tile, width = 256, w.shape[0] // 4
    reads = [pltpu.make_async_copy(low_far, low_ref, sem_b.at[0])]
    go(reads)
    loads = load_copies(fast, meta, pieces, w, sem_a, 0)
    parts = [loads] + [[]] * 3
    if len(loads) == 32:
        parts = [[v for k, v in enumerate(loads) if k % 8 // 2 == j] for j in range(4)]
    for part in parts:
        go(part)
    done(reads)
    for j in range(4):
        done(parts[j])
        here = slice(j * width, (j + 1) * width)
        for i in range(n // tile):
            part = slice(i * tile, (i + 1) * tile)
            hidden = nt(low_ref[part, :], w[here, :]) + bias_ref[:, here]
            phi = 0.5 + 0.5 * lax.erf(hidden * SQRT_HALF)
            act_ref[part, here] = (hidden * phi).astype(BF)
            bell = jnp.exp(hidden * hidden * -0.5) * INV_SQRT_2PI
            slope_ref[part, here] = (phi + hidden * bell).astype(BF)


def up_forward(fast, meta, low, bias, pieces, deps=()):
    n, d = low.shape
    ff = bias.shape[1]
    return kernel_call(
        functools.partial(up_kernel, fast, len(pieces)),
        deps,
        [SMEM, ANY, WHOLE] + [ANY] * len(pieces),
        [meta, far(low), bias, *map(far, pieces)],
        out_specs=[WHOLE] * 3,
        out_shape=[VMEM((n, ff), BF), VMEM((n, ff), BF), TOKEN],
        scratch_shapes=[
            pltpu.VMEM((n, d), BF),
            pltpu.VMEM((ff, d), BF),
            pltpu.SemaphoreType.DMA((32,)),
            pltpu.SemaphoreType.DMA((1,)),
        ],
        cost_estimate=pl.CostEstimate(
            flops=4 * n * d * ff, bytes_accessed=4 * n * ff, transcendentals=0
        ),
        mebibytes=14,
        name="up_forward",
    )


def down_kernel(fast, n_in, seq, *refs):
    meta, words, regions = refs[:3]
    act_ref, slope_ref, xhat_far, vec_ref, cot_far = refs[3:8]
    pieces = refs[8 : 8 + n_in]
    outs_end = 14 + n_in + (2 if fast else 1)
    out_far, second_far, feed_ref, sums_ref, w, _ = refs[8 + n_in : 14 + n_in]
    grads = refs[14 + n_in : outs_end]
    xhat_ref, cot_ref, out_ref, second_ref, whole = refs[outs_end:-3]
    sem_a, sem_b, sem_c = refs[-3:]
    n, d = feed_ref.shape
    ff = act_ref.shape[1]
    tile = 256
    count = n // tile
    loads = load_copies(fast, meta, pieces, w, sem_a, 0)
    go(loads)
    reads, writes = [], []
    for i in range(count):
        part = pl.ds(i * tile, tile)
        reads.append(
            [
                pltpu.make_async_copy(xhat_far.at[part], xhat_ref.at[part], sem_b.at[0, i]),
                pltpu.make_async_copy(cot_far.at[part], cot_ref.at[part], sem_b.at[1, i]),
            ]
        )
        writes += [
            pltpu.make_async_copy(out_ref.at[part], out_far.at[part], sem_b.at[2, i]),
            pltpu.make_async_copy(second_ref.at[part], second_far.at[part], sem_b.at[3, i]),
        ]
    for pair in reads:
        go(pair)
    gain_one, shift_one = vec_ref[:, :d], vec_ref[:, d : 2 * d]
    bias, gain, shift = vec_ref[:, 2 * d : 3 * d], vec_ref[:, 3 * d : 4 * d], vec_ref[:, 4 * d :]
    done(loads)
    sums = [jnp.zeros((1, d), F32)] * 3
    product = nt(act_ref[:tile, :], w[...])
    for i in range(count):
        part = slice(i * tile, (i + 1) * tile)
        done(reads[i])
        if i:
            go(writes[2 * i - 2 : 2 * i])
        this = product
        if i + 1 < count:
            product = nt(act_ref[(i + 1) * tile : (i + 2) * tile, :], w[...])
        second_sum = xhat_ref[part, :] * gain_one + shift_one + this + bias
        xhat, rstd = norm_parts(second_sum)
        first = i * (tile // seq)
        keep = jnp.concatenate(
            [
                key_mask(words[first + p], regions[first + p], (seq, 128), 0)
                for p in range(tile // seq)
            ],
            axis=0,
        )[:, :1]
        out_ref[part, :] = jnp.where(keep, xhat * gain + shift, 0.0).astype(BF)
        grad = jnp.where(keep, cot_ref[part, :].astype(F32), 0.0)
        second = norm_back(grad, xhat, rstd, gain)
        second_ref[part, :] = second
        feed = second.astype(BF)
        feed_ref[part, :] = feed
        for k, value in enumerate((grad * xhat, grad, feed.astype(F32))):
            sums[k] = sums[k] + jnp.sum(value, axis=0, keepdims=True)
    go(writes[-2:])
    for k in range(3):
        sums_ref[k : k + 1, :] = sums[k]
    waits = []
    width, span = ff // 4, ff // 8
    for i in range(4):
        here = slice(i * width, (i + 1) * width)
        whole[:, here] = tn(feed_ref[...], act_ref[:, here]).astype(BF)
        if fast:
            for k in range(2):
                chunk = (i % 2) * 2 + k
                copies = tile_copies(
                    meta, whole, grads, sem_c.at[2 * i + k], range(8), [i // 2], d // 8,
                    chunk * (d // 16), d // 16, ff // 2, (chunk * span, span),
                )
                go(copies)
                waits += tile_waits(
                    whole, grads, sem_c.at[2 * i + k], 8, chunk * (d // 16), d // 16, span
                )
    if not fast:
        waits = [pltpu.make_async_copy(whole, grads[0], sem_c.at[0, 0])]
        go(waits)
    done(waits)
    done(writes)


def down_forward(
    fast, meta, words, regions, act, slope, xhat, vec, cot, pieces, seq, deps=()
):
    n, ff = act.shape
    d = xhat.shape[1]
    shapes = grad_shapes(fast, d, ff)
    return kernel_call(
        functools.partial(down_kernel, fast, len(pieces), seq),
        deps,
        [SMEM] * 3 + [WHOLE, WHOLE, ANY, WHOLE, ANY] + [ANY] * len(pieces),
        [meta, words, regions, near(act), near(slope), far(xhat), vec, far(cot), *map(far, pieces[:-1]), *pieces[-1:]],
        out_specs=[ANY, ANY, WHOLE, WHOLE, WHOLE, WHOLE] + [WHOLE, ANY][-len(shapes) :],
        out_shape=[
            HBM((n, d), BF),
            HBM((n, d), F32),
            VMEM((n, d), BF),
            jax.ShapeDtypeStruct((8, d), F32),
            VMEM((d, ff), BF),
            VMEM((n, ff), BF),
        ]
        + shapes,
        scratch_shapes=[
            pltpu.VMEM((n, d), F32),
            pltpu.VMEM((n, d), BF),
            pltpu.VMEM((n, d), BF),
            pltpu.VMEM((n, d), F32),
            pltpu.VMEM((d, ff), BF),
            pltpu.SemaphoreType.DMA((32,)),
            pltpu.SemaphoreType.DMA((4, n // 256)),
            pltpu.SemaphoreType.DMA((8, 16)),
        ],
        cost_estimate=pl.CostEstimate(
            flops=12 * n * d * ff, bytes_accessed=2 * n * ff, transcendentals=0
        ),
        input_output_aliases={4: 5},
        mebibytes=24,
        name="down_forward",
    )


def hidden_grad_kernel(feed_ref, slope_ref, w, hidden_ref, bias_ref):
    width = 512
    for i in range(slope_ref.shape[1] // width):
        here = slice(i * width, (i + 1) * width)
        hidden = nn(feed_ref[...], w[:, here]) * slope_ref[:, here].astype(F32)
        hidden = hidden.astype(BF)
        hidden_ref[:, here] = hidden
        bias_ref[:, here] = jnp.sum(hidden.astype(F32), axis=0, keepdims=True)


def hidden_grad(feed, slope, w, deps=()):
    n, ff = slope.shape
    d = feed.shape[1]
    return kernel_call(
        hidden_grad_kernel,
        deps,
        [WHOLE] * 3,
        [near(feed), near(slope), near(w)],
        out_specs=[WHOLE] * 2,
        out_shape=[VMEM((n, ff), BF), jax.ShapeDtypeStruct((1, ff), F32)],
        cost_estimate=pl.CostEstimate(
            flops=4 * n * d * ff, bytes_accessed=4 * n * ff, transcendentals=0
        ),
        mebibytes=10,
        name="hidden_grad",
    )


def grad_shapes(fast, total_rows, cols):
    if fast:
        width = min(total_rows, cols) // 2
        shape = (16, total_rows * cols // (32 * width), width)
        return [VMEM(shape, BF), HBM(shape, BF)]
    return [HBM((total_rows, cols), BF)]


def tile_copies(meta, whole, outs, sems, shards, sides, local_rows, first, height, width, cols=None):
    x0, c0, z0, y0 = meta[0], meta[1], meta[2], meta[3]
    offset, span = (0, width) if cols is None else cols
    there = pl.ds(0, span)
    copies = []
    for number, ref in enumerate(outs):
        cc = c0 ^ number
        for shard in shards:
            for side in sides:
                y_rel, x_rel = y0 ^ (shard % 2), x0 ^ side
                a = jnp.where(cc == 0, y_rel, x_rel)
                b = jnp.where(cc == 0, x_rel, y_rel)
                row = pl.multiple_of(shard * local_rows + cc * height, 16)
                col = pl.multiple_of(side * width + offset, 128)
                place = a * 8 + b * 4 + (z0 ^ (shard // 2))
                if number == 0:
                    static = pl.ds(side * width + offset, span)
                    ref[place, pl.ds(first, height), there] = whole[pl.ds(row, height), static]
                    continue
                copies.append(
                    pltpu.make_async_copy(
                        whole.at[pl.ds(row, height), pl.ds(col, span)],
                        ref.at[place, pl.ds(first, height), there],
                        sems.at[len(copies)],
                    )
                )
    return copies


def up_grad_kernel(fast, *refs):
    meta, hidden_ref, low_far, wu_far, *others_far = refs[:8]
    outs = refs[8 : (10 if fast else 9)]
    token_ref, _, wu_ref, *others = refs[10 if fast else 9 : -5]
    low_ref, whole, sems, sem_b, sem_c = refs[-5:]
    reads = [pltpu.make_async_copy(low_far, low_ref, sem_b.at[0])]
    go(reads)
    ahead = load_copies(fast, meta, [wu_far], wu_ref, sem_c, 0)
    for i, (source, target) in enumerate(zip(others_far, others)):
        ahead.append(pltpu.make_async_copy(source, target, sem_b.at[1 + i]))
    go(ahead)
    token_ref[...] = jnp.zeros_like(token_ref)
    done(reads)
    ff, d = whole.shape
    height = ff // 4
    waits = []
    for i in range(4):
        here = slice(i * height, (i + 1) * height)
        whole[here, :] = tn(hidden_ref[:, here], low_ref[...]).astype(BF)
        if fast:
            copies = tile_copies(
                meta, whole, outs, sems.at[i], [2 * i, 2 * i + 1], [0, 1], ff // 8, 0, ff // 16,
                d // 2,
            )
            go(copies)
            waits += tile_waits(whole, outs, sems.at[i], 4, 0, ff // 16, d // 2)
    if not fast:
        waits = [pltpu.make_async_copy(whole, outs[0], sems.at[0, 0])]
        go(waits)
    done(waits + ahead)


def up_grad(fast, meta, hidden, low, wu, others, deps=()):
    n, d = low.shape
    ff = hidden.shape[1]
    shapes = grad_shapes(fast, ff, d)
    return kernel_call(
        functools.partial(up_grad_kernel, fast),
        deps,
        [SMEM, WHOLE] + [ANY] * 6,
        [meta, near(hidden), far(low), far(wu), *map(far, others)],
        out_specs=[WHOLE, ANY][-len(shapes) :] + [WHOLE] * 7,
        out_shape=shapes
        + [TOKEN, VMEM((n, ff), BF), VMEM((ff, d), BF)]
        + [VMEM(v.shape, v.dtype) for v in others],
        scratch_shapes=[
            pltpu.VMEM((n, d), BF),
            pltpu.VMEM((ff, d), BF),
            pltpu.SemaphoreType.DMA((4, 8)),
            pltpu.SemaphoreType.DMA((5,)),
            pltpu.SemaphoreType.DMA((32,)),
        ],
        input_output_aliases={1: len(shapes) + 1},
        cost_estimate=pl.CostEstimate(
            flops=4 * n * d * ff, bytes_accessed=2 * n * ff, transcendentals=0
        ),
        mebibytes=12,
        name="up_grad",
    )


def first_back_kernel(*refs):
    second_ref, hidden_ref, wu_ref, xhat_ref, rstd_ref, wo_ref, gain_ref = refs[:7]
    sum_far, low_far, mix_ref, sums_ref, sum_ref, low_ref, sem = refs[7:]
    n, d = low_ref.shape
    tile = 256
    count = n // tile
    writes = []
    for i in range(count):
        part = pl.ds(i * tile, tile)
        writes.append(
            [
                pltpu.make_async_copy(sum_ref.at[part], sum_far.at[part], sem.at[0, i]),
                pltpu.make_async_copy(low_ref.at[part], low_far.at[part], sem.at[1, i]),
            ]
        )
    product = nn(hidden_ref[:tile, :], wu_ref[...])
    sums = [jnp.zeros((1, d), F32)] * 3
    for i in range(count):
        part = slice(i * tile, (i + 1) * tile)
        if i:
            go(writes[i - 1])
        grad = second_ref[part, :] + product
        if i + 1 < count:
            product = nn(hidden_ref[(i + 1) * tile : (i + 2) * tile, :], wu_ref[...])
        xhat = xhat_ref[part, :]
        attn_sum = norm_back(grad, xhat, rstd_ref[part, :1], gain_ref[...])
        sum_ref[part, :] = attn_sum
        low = attn_sum.astype(BF)
        low_ref[part, :] = low
        mix_ref[part, :] = nn(low, wo_ref[...]).astype(BF)
        for k, value in enumerate((grad * xhat, grad, low.astype(F32))):
            sums[k] = sums[k] + jnp.sum(value, axis=0, keepdims=True)
    go(writes[-1])
    for k in range(3):
        sums_ref[k : k + 1, :] = sums[k]
    for group in writes:
        done(group)


def first_back(second, hidden, wu, xhat, rstd, wo, gain, deps=()):
    n, ff = hidden.shape
    d = xhat.shape[1]
    return kernel_call(
        first_back_kernel,
        deps,
        [WHOLE] * 7,
        [near(v) for v in (second, hidden, wu, xhat, rstd, wo)] + [gain],
        out_specs=[ANY, ANY, WHOLE, WHOLE],
        out_shape=[
            HBM((n, d), F32),
            HBM((n, d), BF),
            VMEM((n, d), BF),
            jax.ShapeDtypeStruct((8, d), F32),
        ],
        scratch_shapes=[
            pltpu.VMEM((n, d), F32),
            pltpu.VMEM((n, d), BF),
            pltpu.SemaphoreType.DMA((2, n // 256)),
        ],
        cost_estimate=pl.CostEstimate(
            flops=4 * n * d * ff, bytes_accessed=2 * n * ff, transcendentals=0
        ),
        mebibytes=12,
        name="first_back",
    )


def attention_back_kernel(seq, *refs):
    mix_ref, joined_ref, probs_ref, *others_far = refs[:6]
    grad_ref, sums_ref, near_ref, *others, sem = refs[6:]
    step = pl.program_id(0)
    ahead = [
        pltpu.make_async_copy(source, target, sem.at[i])
        for i, (source, target) in enumerate(zip(others_far, others))
    ]
    d = mix_ref.shape[1]

    @pl.when(step == 0)
    def _():
        go(ahead)
        sums_ref[...] = jnp.zeros_like(sums_ref)

    for p in range(mix_ref.shape[0] // seq):
        here = pl.ds(p * seq, seq)
        for h in range(d // 128):
            one = pl.ds(h * 128, 128)
            two = pl.ds(d + h * 128, 128)
            three = pl.ds(2 * d + h * 128, 128)
            outer = split_heads(mix_ref[here, one])
            probs = probs_ref[p, h]
            grad_probs = nt(joined_ref[here, three], outer)
            wide = probs.astype(F32)
            product = wide * grad_probs
            scores = product - wide * jnp.sum(product, axis=0, keepdims=True)
            scores = scores.astype(BF)
            grad_ref[here, three] = nn(probs, outer).astype(BF)
            grad_ref[here, two] = nn(scores, split_heads(joined_ref[here, one])).astype(BF)
            keys = split_heads(joined_ref[here, two])
            grad_ref[here, one] = (nn(turn_heads(scores), keys) * 0.125).astype(BF)
    tile = mix_ref.shape[0]
    near_ref[pl.ds(pl.multiple_of(step * tile, tile), tile), :] = grad_ref[...]
    sums_ref[0:1, :] += jnp.sum(grad_ref[:, :d].astype(F32), axis=0, keepdims=True)
    sums_ref[1:2, :] += jnp.sum(grad_ref[:, 2 * d :].astype(F32), axis=0, keepdims=True)

    @pl.when(step == pl.num_programs(0) - 1)
    def _():
        done(ahead)


def attention_back(mix, joined, probs, others, seq, deps=()):
    n, d = mix.shape
    tile = 2 * seq
    return kernel_call(
        functools.partial(attention_back_kernel, seq),
        deps,
        [
            rows((tile, d)),
            rows((tile, 3 * d)),
            rows((2, d // 128, seq, 2 * seq)),
            ANY,
            ANY,
            ANY,
        ],
        [near(mix), far(joined), far(probs), *map(far, others)],
        grid=(n // tile,),
        out_specs=[rows((tile, 3 * d)), fixed((8, d))] + [WHOLE] * 4,
        out_shape=[
            HBM((n, 3 * d), BF),
            jax.ShapeDtypeStruct((8, d), F32),
            VMEM((n, 3 * d), BF),
        ]
        + [VMEM((n, d), BF)] * 3,
        scratch_shapes=[pltpu.SemaphoreType.DMA((3,))],
        cost_estimate=pl.CostEstimate(
            flops=16 * n * d * d, bytes_accessed=30 * n * d, transcendentals=0
        ),
        mebibytes=14,
        name="attention_back",
    )


def qkv_grad_kernel(fast, *refs):
    meta, grad_ref, x_ref, low_ref, mix_ref = refs[:5]
    outs = refs[5:7]
    token_ref, whole, whole_out, sem_a, sem_b = refs[7:]
    token_ref[...] = jnp.zeros_like(token_ref)
    total, d = whole.shape
    waits = []
    for i in range(2):
        here = slice(i * total // 2, (i + 1) * total // 2)
        whole[here, :] = tn(grad_ref[:, here], x_ref[...]).astype(BF)
        if fast:
            go(
                tile_copies(
                    meta, whole, outs, sem_a.at[i], range(4 * i, 4 * i + 4), [0, 1], total // 8,
                    0, total // 16, d // 2,
                )
            )
            waits += tile_waits(whole, outs, sem_a.at[i], 8, 0, total // 16, d // 2)
    whole_out[...] = tn(low_ref[...], mix_ref[...]).astype(BF)
    if fast:
        go(
            tile_copies(
                meta, whole_out, outs, sem_b, range(8), [0, 1], d // 8, total // 16, d // 16,
                d // 2,
            )
        )
        waits += tile_waits(whole_out, outs, sem_b, 16, total // 16, d // 16, d // 2)
    else:
        waits = [
            pltpu.make_async_copy(whole, outs[0], sem_b.at[0]),
            pltpu.make_async_copy(whole_out, outs[1], sem_b.at[1]),
        ]
        go(waits)
    done(waits)


def qkv_grad(fast, meta, grad, x, low, mix, deps=()):
    n, d = x.shape
    if fast:
        shapes = [f((16, 4 * d // 16, d // 2), BF) for f in (VMEM, HBM)]
    else:
        shapes = [jax.ShapeDtypeStruct((3 * d, d), BF), jax.ShapeDtypeStruct((d, d), BF)]
    return kernel_call(
        functools.partial(qkv_grad_kernel, fast),
        deps,
        [SMEM, WHOLE, WHOLE, WHOLE, WHOLE],
        [meta, near(grad), near(x), near(low), near(mix)],
        out_specs=([WHOLE, ANY] if fast else [ANY] * 2) + [WHOLE],
        out_shape=shapes + [TOKEN],
        scratch_shapes=[
            pltpu.VMEM((3 * d, d), BF),
            pltpu.VMEM((d, d), BF),
            pltpu.SemaphoreType.DMA((2, 16)),
            pltpu.SemaphoreType.DMA((32,)),
        ],
        cost_estimate=pl.CostEstimate(
            flops=16 * n * d * d, bytes_accessed=16 * n * d, transcendentals=0
        ),
        mebibytes=20,
        name="qkv_grad",
    )


def tokens_grad_kernel(sum_ref, grad_ref, w_ref, out_ref, token_ref):
    token_ref[...] = jnp.zeros_like(token_ref)
    out_ref[...] = sum_ref[...] + nn(grad_ref[...], w_ref[...])


def tokens_back(attn_sum, grad, w, deps=()):
    n, d = attn_sum.shape
    tile = 256
    return kernel_call(
        tokens_grad_kernel,
        deps,
        [rows((tile, d)), rows((tile, 3 * d)), fixed((3 * d, d))],
        [far(attn_sum), far(grad), far(w)],
        grid=(n // tile,),
        out_specs=[rows((tile, d)), fixed((8, 128))],
        out_shape=[HBM((n, d), F32), TOKEN],
        cost_estimate=pl.CostEstimate(
            flops=12 * n * d * d, bytes_accessed=14 * n * d, transcendentals=0
        ),
        mebibytes=14,
        name="tokens_back",
    )


AXES = ("rep", "shard")


def route(fn):
    pairs = []
    for x in range(2):
        for c in range(2):
            for z in range(4):
                for y in range(2):
                    to = fn(x, c, z, y)
                    pairs.append(
                        ((x * 2 + c) * 8 + z * 2 + y, (to[0] * 2 + to[1]) * 8 + to[2] * 2 + to[3])
                    )
    return pairs


def to_core(v):
    return lax.ppermute(v, AXES, route(lambda x, c, z, y: (x, 1 - c, z, y)))


def to_x(v):
    return lax.ppermute(v, AXES, route(lambda x, c, z, y: (1 - x, c, z, y)))


def to_z(v, k):
    return lax.ppermute(v, AXES, route(lambda x, c, z, y: (x, c, z ^ k, y)))


def to_cross(v, first_core):
    return lax.ppermute(
        v,
        AXES,
        route(lambda x, c, z, y: (1 - x, c, z, y) if c == first_core else (x, c, z, 1 - y)),
    )


def after(value, *others):
    return lax.optimization_barrier((value, others))[0]


def start_gather(own):
    return jnp.stack([own] + [to_z(own, k) for k in (1, 2, 3)])


def first_cross(along):
    return jnp.concatenate([along, to_cross(along, 0)])


def add_core_kernel(kept_ref, got_ref, *refs):
    keep_ref, send_ref = refs[-2:]
    count, height, width = keep_ref.shape
    for k in range(count):
        here = slice(k * height, (k + 1) * height)
        keep_ref[k] = (kept_ref[k].astype(F32) + got_ref[k].astype(F32)).astype(BF)
        other = kept_ref[count + k].astype(F32) + got_ref[count + k].astype(F32)
        send_ref[here, :] = other.astype(BF)
    if len(refs) == 3:
        send_ref[count * height :, :] = refs[0][...].astype(BF)


def add_cross_kernel(keep_ref, got_ref, *refs):
    small = len(refs) == 4
    new_ref, send_ref = refs[1:3] if small else refs
    count, height, width = new_ref.shape
    for k in range(2 * count):
        here = slice(k * height, (k + 1) * height)
        total = (keep_ref[k].astype(F32) + got_ref[here, :].astype(F32)).astype(BF)
        if k < count:
            new_ref[k] = total
        else:
            send_ref[(k - count) * height : (k - count + 1) * height, :] = total
    if small:
        rows_in = refs[0][...] + got_ref[2 * count * height :, :].astype(F32)
        refs[3][...] = rows_in
        tail = jnp.concatenate([rows_in[count : 2 * count], rows_in[2 * count :]], axis=0)
        tail = jnp.concatenate([tail, jnp.zeros((count, width), F32)], axis=0)
        send_ref[count * height :, :] = tail.astype(BF)


def add_last_kernel(keep_ref, got_ref, *refs):
    small = len(refs) == 5
    outs = refs[1:] if small else refs
    count, height, width = keep_ref.shape
    if small:
        rows_in = refs[0][...] + got_ref[count * height :, :].astype(F32)
        place = lax.broadcasted_iota(jnp.int32, rows_in.shape, 0)
    for k in range(count):
        here = slice(k * height, (k + 1) * height)
        total = keep_ref[k].astype(F32) + got_ref[here, :].astype(F32)
        outs[k][:height, :] = total.astype(outs[k].dtype)
        if small:
            row = jnp.sum(jnp.where(place == k, rows_in, 0.0), axis=0, keepdims=True)
            outs[k][height:, :] = jnp.broadcast_to(row, (16, width)).astype(outs[k].dtype)


def total_kernel(own_ref, one_ref, two_ref, three_ref, out_ref):
    total = own_ref[...] + one_ref[...].astype(F32)
    total = total + two_ref[...].astype(F32) + three_ref[...].astype(F32)
    out_ref[...] = total.astype(BF)


class Scatter:
    def __init__(self, kept, sent):
        self.kept, self.small = kept, None
        self.got = to_core(sent)

    def call(self, body, out_shape, extra, deps, name):
        args = [near(self.keep), near(self.got)] + list(extra)

        def marked(*refs):
            refs[-1][...] = jnp.zeros_like(refs[-1])
            body(*refs[:-1])

        *out, self.token = kernel_call(
            marked,
            deps,
            [WHOLE] * len(args),
            args,
            out_specs=[WHOLE] * (len(out_shape) + 1),
            out_shape=out_shape + [TOKEN],
            name=name,
        )
        return out

    def add_core(self, deps=(), small=None):
        self.keep = self.kept
        count, height, width = self.kept.shape[0] // 2, *self.kept.shape[1:]
        tail, extra = 0, []
        if small is not None:
            tail, extra = 16, [jnp.concatenate([small[8:], jnp.zeros_like(small[8:])])]
            self.small = jnp.concatenate([small[:8], jnp.zeros_like(small[8:])])
        self.keep, self.send = self.call(
            add_core_kernel,
            [VMEM((count, height, width), BF), VMEM((count * height + tail, width), BF)],
            extra,
            deps,
            "add_core",
        )
        return self.token

    def cross(self, core):
        self.got = to_cross(self.send, core)

    def add_cross(self, deps=()):
        count, height, width = self.keep.shape[0] // 2, *self.keep.shape[1:]
        small = self.small is not None
        outs = [
            VMEM((count, height, width), BF),
            VMEM((count * height + 16 * small, width), BF),
        ]
        if small:
            outs.append(VMEM((16, width), F32))
        out = self.call(
            add_cross_kernel, outs, [self.small] if small else [], deps, "add_cross"
        )
        self.keep, self.send = out[:2]
        if small:
            self.small = out[2]
        return self.token

    def add_last(self, deps=()):
        height, width = self.keep.shape[1:]
        small = self.small is not None
        shape = (height + 16 * small, width)
        self.parts = self.call(
            add_last_kernel,
            [VMEM(shape, F32)] + [VMEM(shape, BF)] * 3,
            [self.small] if small else [],
            deps,
            "add_last",
        )
        return self.token

    def along(self):
        self.got = [to_z(self.parts[k], k) for k in (1, 2, 3)]

    def total(self, deps=()):
        args = [near(v) for v in [self.parts[0]] + self.got]
        return kernel_call(
            total_kernel,
            deps,
            [WHOLE] * 4,
            args,
            out_specs=WHOLE,
            out_shape=jax.ShapeDtypeStruct(self.parts[0].shape, BF),
            name="total",
        )


def finish_kernel(meta, mine_ref, other_ref, qkv_ref, out_ref, small_ref):
    c = meta[1]
    first = 0
    for target in (qkv_ref, out_ref):
        half = target.shape[0] // 2
        part = slice(first, first + half)
        target[pl.ds(pl.multiple_of(c * half, 8), half), :] = mine_ref[part, :].astype(F32)
        target[pl.ds(pl.multiple_of((1 - c) * half, 8), half), :] = other_ref[part, :].astype(F32)
        first += half
    mine = mine_ref[first : first + 16, :].astype(F32)[:1]
    other = other_ref[first : first + 16, :].astype(F32)[:1]
    side, quarter = mine.shape[1] // 2, small_ref.shape[1] // 4
    parts = []
    for line in (jnp.where(c == 0, mine, other), jnp.where(c == 0, other, mine)):
        parts += [line[:, :quarter], line[:, side : side + quarter]]
    small_ref[...] = jnp.concatenate(parts, axis=1)


def finish(meta, mine, other, d, quarter):
    return kernel_call(
        finish_kernel,
        [],
        [SMEM, WHOLE, WHOLE],
        [meta, near(mine), near(other)],
        out_specs=[WHOLE] * 3,
        out_shape=[HBM((3 * d // 8, d), F32), HBM((d // 8, d), F32), VMEM((1, 4 * quarter), F32)],
        name="finish",
    )


def in_columns(piece):
    return jnp.concatenate(jnp.split(piece, 4, axis=0), axis=1)


def side_by_side(low, across, x):
    return jnp.concatenate(
        [jnp.where(x == 0, low, across), jnp.where(x == 0, across, low)], axis=1
    )


def owner_block(mine, other, c, first, height):
    mine, other = mine[first : first + height], other[first : first + height]
    return jnp.concatenate(
        [jnp.where(c == 0, mine, other), jnp.where(c == 0, other, mine)], axis=0
    ).astype(F32)


def quarter_of(w, x, c):
    half_rows, half_cols = w.shape[0] // 2, w.shape[1] // 2
    side = jnp.where(x == 0, w[:, :half_cols], w[:, half_cols:])
    return jnp.where(c == 0, side[:half_rows], side[half_rows:]).astype(BF)


def order_matrix(x, c, z, y):
    rel = jnp.arange(32, dtype=jnp.int32)
    other, a, b, rz = rel // 16, rel // 8 % 2, rel // 4 % 2, rel % 4
    cc = c ^ other
    y_rel = jnp.where(cc == 0, a, b)
    x_rel = jnp.where(cc == 0, b, a)
    place = (((z ^ rz) * 2 + (y ^ y_rel)) * 2 + cc) * 2 + (x ^ x_rel)
    return (place[:, None] == rel[None, :]).astype(F32)


def line_tables(heights):
    place = []
    for shard in range(8):
        at = 0
        for height in heights:
            place += [at + shard * height + k for k in range(height)]
            at += 8 * height
    place = np.array(place).reshape(32, -1)
    count = place.size // 8
    row = np.zeros((place.shape[1], 32, 16), np.float32)
    lane = np.zeros((place.shape[1], 32, 8), np.float32)
    for piece in range(32):
        for k in range(place.shape[1]):
            row[k, piece, place[piece, k] // 8] = 1.0
            lane[k, piece, place[piece, k] % 8] = 1.0
    assert count <= 16
    return jnp.asarray(row), jnp.asarray(lane)


def pack_kernel(order, rows_of, lanes_of, attn_ref, first_ref, bias_ref, two_ref, keep_ref, send_ref, vecs):
    d = vecs.shape[1]
    width = d // 8
    vecs[...] = jnp.zeros_like(vecs)
    vecs[0:2, :] = attn_ref[0:2, :]
    vecs[2:3, :] = first_ref[2:3, :]
    vecs[3:5, :] = first_ref[0:2, :]
    for k in range(4):
        vecs[5 + k : 6 + k, :] = bias_ref[:, k * d : (k + 1) * d]
    vecs[9:10, :] = two_ref[2:3, :]
    vecs[10:12, :] = two_ref[0:2, :]
    parts = []
    for k in range(rows_of.shape[0]):
        chosen = jnp.dot(
            rows_of[k], vecs[...], preferred_element_type=F32, precision=lax.Precision.HIGHEST
        )
        part = jnp.zeros((32, width), F32)
        for m in range(8):
            part = part + chosen[:, m * width : (m + 1) * width] * lanes_of[k, :, m : m + 1]
        parts.append(part)
    parts.append(jnp.zeros((32, keep_ref.shape[1] - len(parts) * width), F32))
    packed = jnp.concatenate(parts, axis=1)
    packed = jnp.dot(
        order[...], packed, preferred_element_type=F32, precision=lax.Precision.HIGHEST
    )
    keep_ref[...] = packed[:16]
    send_ref[...] = packed[16:].astype(BF)


def pack_small(order, tables, attn, first, bias, two):
    d = attn.shape[1]
    return kernel_call(
        pack_kernel,
        [],
        [WHOLE] * 7,
        [order, *tables, attn, first, bias, two],
        out_specs=[WHOLE] * 2,
        out_shape=[
            jax.ShapeDtypeStruct((16, d // 2), F32),
            jax.ShapeDtypeStruct((16, d // 2), BF),
        ],
        scratch_shapes=[pltpu.VMEM((16, d), F32)],
        name="pack_small",
    )


def per_device(
    tokens,
    word_counts,
    region_counts,
    qkv_weight,
    qkv_bias,
    out_weight,
    out_bias,
    attn_gain,
    attn_shift,
    up_weight,
    up_bias,
    down_weight,
    down_bias,
    ffn_gain,
    ffn_shift,
    cotangent,
):
    pairs, seq, d = tokens.shape
    n = pairs * seq
    shard_count, rep_count = lax.axis_size("shard"), lax.axis_size("rep")
    fast = shard_count == 8 and rep_count == 4
    rep, shard = lax.axis_index("rep"), lax.axis_index("shard")
    x, c, z, y = rep // 2, rep % 2, shard // 2, shard % 2
    meta = jnp.stack([x, c, z, y]).astype(jnp.int32)
    vectors = (qkv_bias, out_bias, attn_gain, attn_shift, up_bias, down_bias, ffn_gain, ffn_shift)
    small_own = jnp.concatenate(vectors)
    sizes = [v.shape[0] for v in vectors]

    flat = tokens.reshape(n, d)
    if fast:
        quarter = small_own.shape[0] // 4
        own_small = jnp.where(
            x == 0,
            jnp.where(c == 0, small_own[:quarter], small_own[2 * quarter : 3 * quarter]),
            jnp.where(c == 0, small_own[quarter : 2 * quarter], small_own[3 * quarter :]),
        )
        own_small = jnp.pad(own_small.astype(BF)[None, :], ((0, 15), (0, d // 2 - quarter)))
        own_one = jnp.concatenate(
            [quarter_of(qkv_weight, x, c), quarter_of(out_weight, x, c), own_small], axis=0
        )
        up_pieces = [lax.all_gather(quarter_of(up_weight, x, c), AXES, axis=0)]
        along_one = start_gather(own_one)
        eight_one = first_cross(along_one)
        more_one = to_cross(eight_one, 1)
        along_two = start_gather(after(quarter_of(down_weight, x, c), eight_one))
        other_one = to_core(eight_one)
        along_two, more_one, other_one = after((along_two, more_one, other_one))
        last_one = to_core(more_one)
        qkv_pieces = [eight_one, more_one, other_one, last_one]
        order = order_matrix(x, c, z, y)
        row = d // 4
        tables = line_tables([v // (d // 8) for v in sizes])
        rel_small = jnp.concatenate([p[:, row, :quarter] for p in qkv_pieces]).astype(F32)
        whole_small = lax.dot_general(
            order, rel_small, (((0,), (0,)), ((), ())), precision=lax.Precision.HIGHEST
        ).reshape(8, -1)
        cross_two = to_cross(along_two, 0)
        first_deps = [along_two]
    else:
        qkv_pieces = [
            lax.all_gather(w.astype(BF), "shard", axis=0, tiled=True)
            for w in (qkv_weight, out_weight)
        ]
        whole_small = lax.all_gather(small_own.astype(BF), "shard", axis=0).astype(F32)
        first_deps = []
    parts, at = [], 0
    for size in sizes:
        parts.append(whole_small[:, at : at + size].reshape(1, -1))
        at += size
    bqv, bo, g1, c1, bu, bd, g2, c2 = parts

    vec_one = jnp.concatenate([bqv, bo, g1, c1], axis=1)
    vec_two = jnp.concatenate([g1, c1, bd, g2, c2], axis=1)
    joined, probs, mix, low, xhat, rstd, wqkv, wo = attention_forward(
        fast, meta, word_counts, region_counts, flat, vec_one, qkv_pieces, seq, first_deps
    )
    if fast:
        cross_two = after(cross_two, rstd)
        eight_two = jnp.concatenate([along_two, cross_two])
        more_two = to_cross(eight_two, 1)
        up_deps = [eight_two, vec_two]
    else:
        up_pieces = [lax.all_gather(up_weight.astype(BF), "shard", axis=0, tiled=True)]
        up_deps = []
    act, slope, token = up_forward(fast, meta, low, bu, up_pieces, up_deps)
    if fast:
        more_two = after(more_two, token)
        down_pieces = [eight_two, more_two, to_core(after(eight_two, token)), to_core(more_two)]
    else:
        down_pieces = [lax.all_gather(down_weight.astype(BF), "shard", axis=0, tiled=True)]
    layer_out, second, feed, sums_two, wd, slope, *down_grads = down_forward(
        fast, meta, word_counts, region_counts, act, slope, xhat, vec_two,
        cotangent.reshape(n, d), down_pieces, seq,
    )
    deps = []
    if fast:
        down_sum = Scatter(*down_grads)
    hidden, grad_bu = hidden_grad(feed, slope, wd)
    if fast:
        deps = [down_sum.add_core([grad_bu])]
        down_sum.cross(1)
    up_out = up_grad(fast, meta, hidden, low, up_pieces[0], [second, xhat, rstd, wo], deps)
    up_grads, (token, hidden, wu, second, xhat, rstd, wo) = up_out[:-7], up_out[-7:]
    deps = [token]
    if fast:
        deps = [down_sum.add_cross([token])]
        up_sum = Scatter(up_grads[0], after(up_grads[1], deps[0]))
        down_sum.cross(0)
    attn_sum, attn_low, grad_mix, sums_first = first_back(
        second, hidden, wu, xhat, rstd, wo, g1, deps
    )
    if fast:
        deps = [down_sum.add_last([sums_first]), up_sum.add_core([sums_first])]
        down_sum.along()
        up_sum.cross(1)
    grad_joined, sums_attn, joined_near, *others = attention_back(
        grad_mix, joined, probs, [flat, attn_low, mix], seq, deps
    )
    grad_vectors = [
        jnp.concatenate([sums_attn[0:1], sums_attn[1:2]], axis=1),
        sums_first[2:3],
        sums_first[0:1],
        sums_first[1:2],
        grad_bu,
        sums_two[2:3],
        sums_two[0:1],
        sums_two[1:2],
    ]
    deps = []
    if fast:
        small, small_low = pack_small(order, tables, sums_attn, sums_first, grad_bu, sums_two)
        deps = [up_sum.add_cross([sums_attn]), small_low] + down_sum.got
        up_sum.cross(0)
        small_got = to_core(small_low)
    qkv_out = qkv_grad(fast, meta, joined_near, *others, deps)
    qkv_grads, token = qkv_out[:2], qkv_out[2]
    if fast:
        small_got, up_sum.got = after((small_got, up_sum.got), token)
        qkv_sum = Scatter(qkv_grads[0], after(qkv_grads[1], small_got, up_sum.got))
        up_sum.add_last()
        up_sum.along()
        small = small + small_got.astype(F32)
        token = qkv_sum.add_core([up_sum.token], small=small)
        qkv_sum.cross(1)
        down_total = down_sum.total([token])
        down_across = to_x(down_total)
        tokens_grad, token = tokens_back(attn_sum, grad_joined, wqkv, [token, down_total])
        token = qkv_sum.add_cross([token, down_across] + up_sum.got)
        qkv_sum.cross(0)
        up_total = up_sum.total([token])
        up_across = to_x(up_total)
        token = qkv_sum.add_last([up_across])
        qkv_sum.along()
        down_mine = side_by_side(in_columns(down_total), in_columns(down_across), x)
        up_mine = side_by_side(up_total, up_across, x)
        down_other, up_other = to_core(down_mine), to_core(up_mine)
        grad_down = owner_block(down_mine, down_other, c, 0, down_mine.shape[0])
        grad_up = owner_block(up_mine, up_other, c, 0, up_mine.shape[0])
        grad_up, grad_down, qkv_sum.got = after((grad_up, grad_down, qkv_sum.got))
        qkv_total = qkv_sum.total()
        qkv_mine = side_by_side(qkv_total, to_x(qkv_total), x)
        qkv_other = to_core(qkv_mine)
        grad_qkv, grad_out, small_all = finish(meta, qkv_mine, qkv_other, d, quarter)
        small_total = small_all.reshape(-1)
    else:
        tokens_grad, _ = tokens_back(attn_sum, grad_joined, wqkv)

        def total(v):
            part = lax.psum_scatter(v.astype(F32), "shard", scatter_dimension=0, tiled=True)
            return lax.psum(part, "rep")

        grad_down, grad_up = total(down_grads[0]), total(up_grads[0])
        grad_qkv, grad_out = total(qkv_grads[0]), total(qkv_grads[1])
        small_total = lax.dynamic_index_in_dim(
            jnp.concatenate(
                [lax.psum(g, AXES).reshape(shard_count, -1) for g in grad_vectors], axis=1
            ),
            shard,
            axis=0,
            keepdims=False,
        )
    vector_grads, at = [], 0
    for size in sizes:
        vector_grads.append(small_total[at : at + size])
        at += size
    g_qv, g_bo, g_g1, g_c1, g_bu, g_bd, g_g2, g_c2 = vector_grads
    return (
        layer_out.reshape(tokens.shape),
        tokens_grad.reshape(tokens.shape),
        grad_qkv,
        g_qv,
        grad_out,
        g_bo,
        g_g1,
        g_c1,
        grad_up,
        g_bu,
        grad_down,
        g_bd,
        g_g2,
        g_c2,
    )


def solution(mesh):
    matrix, vector = P("shard", None), P("shard")
    batch, counts = P(AXES, None, None), P(AXES)
    weights = (
        matrix, vector, matrix, vector, vector, vector,
        matrix, vector, matrix, vector, vector, vector,
    )
    return jax.shard_map(
        per_device,
        mesh=mesh,
        in_specs=(batch, counts, counts) + weights + (batch,),
        out_specs=(batch, batch) + weights,
        check_vma=False,
    )
```
